128 devices in a mesh: section: 2 (over x_hi), dp: 16 (over y, x_lo, core), tensor: 4 (over z).
Axes of the slice: x: 4 (x_hi: 2, x_lo: 2; x = x_hi * 2 + x_lo), y: 4, z: 4, core: 2. Of those that a mesh axis runs over, the one named last changes fastest.
Arguments:
- inputs: bfloat16 [2, 16, 256, 2048], P(None, 'dp', 'tensor'), may hold values from -6 to 6
- cotangent: bfloat16 [2, 16, 256, 2048], P(None, 'dp', 'tensor'), may hold values from -6 to 6
- doc_split: int32 [2, 16], P(None, 'dp'), may hold values from 16 to 240, as said below
- qkv_weight: bfloat16 [2, 2048, 3, 2048], P('section', 'dp', None, 'tensor'), may hold values from -0.125 to 0.125
- qkv_bias: float32 [2, 3, 2048], P('section', None, 'tensor'), may hold values from -3 to 3
- out_weight: bfloat16 [2, 2048, 2048], P('section', 'tensor', 'dp'), may hold values from -0.5 to 0.5
- out_bias: float32 [2, 2048], P('section'), may hold values from -2 to 2
- fc1_weight: bfloat16 [2, 2048, 8192], P('section', 'dp', 'tensor'), may hold values from -0.125 to 0.125
- fc1_bias: float32 [2, 8192], P('section', 'tensor'), may hold values from -3 to 3
- fc2_weight: bfloat16 [2, 8192, 2048], P('section', 'tensor', 'dp'), may hold values from -0.0625 to 0.0625
- fc2_bias: float32 [2, 2048], P('section'), may hold values from -2 to 2
- ln_gain: float32 [2, 2048], P('section'), may hold values from 0.5 to 1.5
- ln_bias: float32 [2, 2048], P('section'), may hold values from -2 to 2
Outputs:
- layer_out: bfloat16 [2, 2, 16, 256, 2048], P('section', None, 'dp', 'tensor')
- input_grad: bfloat16 [2, 2, 16, 256, 2048], P('section', None, 'dp', 'tensor')
- grad_qkv_weight: float32 [2, 2048, 3, 2048], P('section', 'dp', None, 'tensor')
- grad_qkv_bias: float32 [2, 3, 2048], P('section', None, 'tensor')
- grad_out_weight: float32 [2, 2048, 2048], P('section', 'tensor', 'dp')
- grad_out_bias: float32 [2, 2048], P('section')
- grad_fc1_weight: float32 [2, 2048, 8192], P('section', 'dp', 'tensor')
- grad_fc1_bias: float32 [2, 8192], P('section', 'tensor')
- grad_fc2_weight: float32 [2, 8192, 2048], P('section', 'tensor', 'dp')
- grad_fc2_bias: float32 [2, 2048], P('section')
- grad_ln_gain: float32 [2, 2048], P('section')
- grad_ln_bias: float32 [2, 2048], P('section')
The draws below stay inside these ranges and needn't reach their ends.
Inputs may be any that keep to these rules, and one draw needn't show every extreme that they name: `doc_split`: each entry is at most 63 or at least 193; the first document of its slot has that many rows and the second the rest.
All inputs are finite; a program needn't handle non-finite values.
Results may differ from the reference program's by a relative error of at most 0.035.
Values may be sent and summed in bfloat16 or wider, within the bound.
A program may use at most 192 MiB of HBM per device.

```python
import jax
import jax.numpy as jnp
from jax import lax

D = 2048
H = 32
HD = 64
FF = 8192
ROT = 32
MB = 2
SHORT = 16
ROWS = 64
SLOT = 256
N_DP = 16


def draw_doc_split(key, part):
    key = jax.random.fold_in(key, 7)
    key_near, key_side, key_pick = jax.random.split(key, 3)
    count = MB * N_DP
    nearby = jax.random.randint(key_near, (count,), SHORT, ROWS)
    sides = jax.random.randint(key_side, (count,), 0, 2)
    chosen = jnp.where(sides == 1, nearby, SLOT - nearby)
    picked = jax.random.randint(key_pick, (), 0, count)
    places = jnp.arange(count, dtype=jnp.int32)
    chosen = jnp.where(places == picked, SHORT, chosen)
    chosen = jnp.where(places == (picked + 1) % count, SLOT - SHORT, chosen)
    return chosen.reshape(MB, N_DP).astype(jnp.int32)


def level_of(rng, shape, cuts, low, largest):
    level, own = 1.0, jax.random.fold_in(rng, 6)
    for axis_at, blocks in cuts:
        heights = jnp.exp(jax.random.uniform(jax.random.fold_in(own, axis_at), (blocks,), jnp.float32, low / len(cuts), largest / len(cuts)))
        level = level * jnp.repeat(heights, shape[axis_at] // blocks).reshape([-1 if axis == axis_at else 1 for axis in range(len(shape))])
    return level


def noise(own_key, shape, deviation, bound, cuts=(), kind=jnp.bfloat16):
    gain = level_of(own_key, shape, cuts, -0.22, 0.18) if cuts else 1.0
    values = jax.random.normal(own_key, shape, jnp.float32) * deviation * gain
    return jnp.minimum(jnp.maximum(values, -bound), bound).astype(kind)


def setup_inputs(seed: int = 0) -> dict:
    seeds = jax.random.split(jax.random.key(seed), 14)
    inputs = noise(seeds[0], (MB, N_DP, SLOT, D), 1.0, 6.0, ((1, 16), (2, 4)))
    cotangent = noise(seeds[1], (MB, N_DP, SLOT, D), 1.0, 6.0, ((1, 16), (2, 4)))
    doc_split = draw_doc_split(jax.random.fold_in(seeds[13], 71), 0)
    qkv_weight = noise(seeds[3], (2, D, 3, D), D ** -0.5, 0.125, ((0, 2), (1, 16), (3, 4)))
    qkv_bias = noise(seeds[4], (2, 3, D), 0.5, 3.0, ((0, 2), (2, 4)), jnp.float32)
    out_weight = noise(seeds[5], (2, D, D), (D // 16) ** -0.5, 0.5, ((0, 2), (1, 4), (2, 16)))
    out_bias = noise(seeds[6], (2, D), 0.3, 2.0, ((0, 2),), jnp.float32)
    fc1_weight = noise(seeds[7], (2, D, FF), D ** -0.5, 0.125, ((0, 2), (1, 16), (2, 4)))
    fc1_bias = noise(seeds[8], (2, FF), 0.5, 3.0, ((0, 2), (1, 4)), jnp.float32)
    fc2_weight = noise(seeds[9], (2, FF, D), FF ** -0.5, 0.0625, ((0, 2), (1, 4), (2, 16)))
    fc2_bias = noise(seeds[10], (2, D), 0.3, 2.0, ((0, 2),), jnp.float32)
    ln_gain = jnp.clip(1.0 + 0.1 * jax.random.normal(seeds[11], (2, D), jnp.float32), 0.5, 1.5)
    ln_bias = noise(seeds[12], (2, D), 0.3, 2.0, ((0, 2),), jnp.float32)
    return {"inputs": inputs, "cotangent": cotangent, "doc_split": doc_split, "qkv_weight": qkv_weight, "qkv_bias": qkv_bias, "out_weight": out_weight, "out_bias": out_bias, "fc1_weight": fc1_weight, "fc1_bias": fc1_bias, "fc2_weight": fc2_weight, "fc2_bias": fc2_bias, "ln_gain": ln_gain, "ln_bias": ln_bias}


EPSILON = 1e-05

@jax.custom_vjp
def low(v):
    return lax.optimization_barrier(v.astype(jnp.bfloat16)).astype(jnp.float32)

@jax.custom_vjp
def low_back(v):
    return v

def low_keep(v):
    return (low(v), None)

def low_pass(kept, grad):
    return (grad,)

def back_keep(v):
    return (v, None)

def back_low(kept, grad):
    return (low(grad),)
low.defvjp(low_keep, low_pass)
low_back.defvjp(back_keep, back_low)

def layer_norm(values_in, norm_gain, shift_term):
    average = lax.optimization_barrier(jnp.mean(values_in, axis=-1, keepdims=True))
    centred = values_in - average
    variance = lax.optimization_barrier(jnp.mean(centred * centred, axis=-1, keepdims=True))
    return centred * lax.rsqrt(variance + EPSILON) * norm_gain + shift_term

def doc_layout(split_at, count):
    places = jnp.arange(count, dtype=jnp.int32)
    leading = places < split_at
    positions = jnp.where(leading, places, places - split_at).astype(jnp.float32)
    allowed = (places[None, :] <= places[:, None]) & (leading[:, None] == leading[None, :])
    return (positions, allowed)

def rotary_tables(positions):
    halves = ROT // 2
    frequency = 10000.0 ** (-(jnp.arange(halves, dtype=jnp.float32) * (2.0 / ROT)))
    angles = positions[:, None] * frequency[None, :]
    return (jnp.cos(angles), jnp.sin(angles))

def rotate(values_in, cosine_table, sine_table):
    halves = ROT // 2
    leading_half = values_in[..., :halves]
    trailing_half = values_in[..., halves:ROT]
    remainder = values_in[..., ROT:]
    cosine_rows = cosine_table[:, None, :]
    sine_rows = sine_table[:, None, :]
    return jnp.concatenate([leading_half * cosine_rows - trailing_half * sine_rows, trailing_half * cosine_rows + leading_half * sine_rows, remainder], axis=-1)

def attend(queries_in, keys_in, values_in, split_at):
    count = queries_in.shape[0]
    positions, allowed = doc_layout(split_at, count)
    cosine_table, sine_table = rotary_tables(positions)
    queries = low(rotate(queries_in, cosine_table, sine_table))
    key_rows = low(rotate(keys_in, cosine_table, sine_table))
    value_rows = low(values_in)
    scores = low_back(jnp.einsum('qhd,khd->hqk', queries, key_rows, precision=lax.Precision.HIGHEST) * HD ** (-0.5))
    scores = jnp.where(allowed[None], scores, -1e+30)
    row_top = lax.optimization_barrier(jnp.max(scores, axis=-1, keepdims=True))
    weights = jnp.exp(scores - row_top)
    attn_probs = low(weights / lax.optimization_barrier(jnp.sum(weights, axis=-1, keepdims=True)))
    mixed_heads = jnp.einsum('hqk,khd->qhd', attn_probs, value_rows, precision=lax.Precision.HIGHEST)
    return mixed_heads.reshape(count, -1)

def attend_item(item):
    return attend(item[0], item[1], item[2], item[3])

def layer_block(rows_in, qkv_w, qkv_b, out_w, out_b, up_w, up_b, down_w, down_b, norm_gain, shift_term, splits):
    normed = low(layer_norm(rows_in, norm_gain, shift_term))
    projected = jnp.dot(normed, qkv_w.reshape(D, 3 * D), precision=lax.Precision.HIGHEST) + qkv_b.reshape(3 * D)
    projected = low_back(projected)
    grouped = projected.reshape(-1, SLOT, 3, H, HD)
    mixed_heads = lax.map(jax.checkpoint(attend_item), (grouped[:, :, 0], grouped[:, :, 1], grouped[:, :, 2], splits))
    mixed_heads = low(low_back(mixed_heads.reshape(-1, D)))
    hidden_pre = low_back(jnp.dot(normed, up_w, precision=lax.Precision.HIGHEST) + up_b)
    activated = low(jax.nn.gelu(hidden_pre, approximate=True))
    branch = jnp.dot(mixed_heads, out_w, precision=lax.Precision.HIGHEST) + out_b
    branch = branch + jnp.dot(activated, down_w, precision=lax.Precision.HIGHEST) + down_b
    return rows_in + low_back(branch)

def reference(inputs, cotangent, doc_split, qkv_weight, qkv_bias, out_weight, out_bias, fc1_weight, fc1_bias, fc2_weight, fc2_bias, ln_gain, ln_bias):
    splits = doc_split.reshape(-1)
    every_param = (qkv_weight, qkv_bias, out_weight, out_bias, fc1_weight, fc1_bias, fc2_weight, fc2_bias, ln_gain, ln_bias)

    def layer_params(layer_at):
        return tuple((stacked[layer_at].astype(jnp.float32) for stacked in every_param))

    def run_layer(rows_in, *params):
        return layer_block(rows_in, *params, splits)
    first_in = inputs.astype(jnp.float32).reshape(-1, D)
    first_out, first_back = jax.vjp(run_layer, first_in, *layer_params(0))
    second_in = lax.optimization_barrier(first_out.astype(jnp.bfloat16)).astype(jnp.float32)
    second_out, second_back = jax.vjp(run_layer, second_in, *layer_params(1))
    second_grads = second_back(cotangent.astype(jnp.float32).reshape(-1, D))
    passed = lax.optimization_barrier(second_grads[0].astype(jnp.bfloat16)).astype(jnp.float32)
    first_grads = first_back(passed)
    row_shape = (2, MB, N_DP, SLOT, D)
    layer_out = jnp.stack([first_out, second_out]).astype(jnp.bfloat16).reshape(row_shape)
    input_grad = jnp.stack([first_grads[0], second_grads[0]]).astype(jnp.bfloat16).reshape(row_shape)
    grads = [jnp.stack([first_grads[which], second_grads[which]]).astype(jnp.float32) for which in range(1, 11)]
    return (layer_out, input_grad, grads[0], grads[1], grads[2], grads[3], grads[4], grads[5], grads[6], grads[7], grads[8], grads[9])
```

```python
from functools import partial

import jax
import jax.numpy as jnp
import numpy as np
from jax import lax
from jax.experimental import pallas as pl
from jax.experimental.pallas import tpu as pltpu
from jax.sharding import PartitionSpec as P

HD = 64
ROT = 32
EPSILON = 1e-05
MESH = pl.DeviceIdType.MESH
BF = jnp.bfloat16
F32 = jnp.float32

D = 2048
SLOT = 256
ROWS = 64
QKV = 768
UP = 1024
A_COLS = QKV + UP
MIX = 256
B_COLS = MIX + UP
COLS = A_COLS + B_COLS
A_HALF = A_COLS // 2
B_HALF = B_COLS // 2
MIB = 2**20


def dot(a, b):
    return lax.dot_general(a, b, (((1,), (0,)), ((), ())), preferred_element_type=F32)


def dot_nt(a, b):
    return lax.dot_general(a, b, (((1,), (1,)), ((), ())), preferred_element_type=F32)


def dot_tn(a, b):
    return lax.dot_general(a, b, (((0,), (0,)), ((), ())), preferred_element_type=F32)


def remote(src, dst, send, recv, device):
    return pltpu.make_async_remote_copy(
        src_ref=src, dst_ref=dst, send_sem=send, recv_sem=recv, device_id=device, device_id_type=MESH
    )


def greet(peers):
    barrier = pltpu.get_barrier_semaphore()
    for peer in peers:
        pl.semaphore_signal(barrier, inc=1, device_id=peer, device_id_type=MESH)
    pl.semaphore_wait(barrier, len(peers))


class Place:
    def __init__(self):
        self.dp = lax.axis_index("dp")
        self.core = lax.rem(self.dp, 2)
        self.x = lax.rem(self.dp // 2, 2)
        self.y = self.dp // 4
        self.z = lax.axis_index("tensor")
        self.sibling = {"dp": self.dp + 1 - 2 * self.core}
        self.across = {"dp": self.at(self.y, 1 - self.x, self.core)}

    def at(self, y, x, core):
        return (y * 2 + x) * 2 + core

    def turn(self, by):
        return lax.rem(self.y + 4 + by, 4)

    def beside(self, by):
        return {"dp": self.at(self.turn(by), self.x, self.core)}

    def z_peer(self, by):
        return {"tensor": lax.rem(self.z + by, 4)}


def gather_kernel(block, split, w, their_split, own_sem, x_send, x_recv, y_send, y_recv, sib_send, sib_recv):
    me = Place()
    greet([me.sibling, me.across, me.beside(1), me.beside(-1)])

    def rows(dp):
        return pl.ds(pl.multiple_of(dp * 128, 128), 128)

    def chip(y, x):
        return pl.ds(pl.multiple_of((y * 2 + x) * 256, 256), 256)

    other = me.dp + 1 - 2 * me.core
    keep = pltpu.make_async_copy(block.at[me.core], w.at[rows(me.dp)], own_sem)
    keep.start()
    give = remote(block.at[1 - me.core], w.at[rows(me.dp)], sib_send.at[0], sib_recv.at[0], me.sibling)
    give.start()
    tell = remote(split, their_split, sib_send.at[1], sib_recv.at[1], me.sibling)
    tell.start()
    keep.wait()
    remote(block.at[1 - me.core], w.at[rows(other)], sib_send.at[0], sib_recv.at[0], me.sibling).wait_recv()

    cols = [
        pl.ds(0, A_HALF),
        pl.ds(A_HALF, A_HALF),
        pl.ds(A_COLS, B_HALF),
        pl.ds(A_COLS + B_HALF, B_HALF),
    ]

    def part(y, x, which):
        return w.at[chip(y, x), cols[which]]

    def over_x(y, x, which, slot):
        piece = part(y, x, which)
        return remote(piece, piece, x_send.at[slot], x_recv.at[slot], me.across)

    def over_y(by, y, x, which, slot):
        piece = part(y, x, which)
        way = 0 if by > 0 else 1
        return remote(piece, piece, y_send.at[way, slot], y_recv.at[way, slot], me.beside(by))

    sent = []

    def start(copy):
        copy.start()
        sent.append(copy)

    y, x = me.y, me.x
    for which in (0, 1):
        start(over_x(y, x, which, which))
    for which in (2, 3):
        for by in (1, -1):
            start(over_y(by, y, x, which, which))
    for which in (2, 3):
        start(over_x(y, x, which, which))
    for which in (0, 1):
        for by in (1, -1):
            start(over_y(by, y, x, which, which))
    for which in (2, 3):
        for by in (1, -1):
            source = me.turn(-by)
            over_y(by, source, x, which, which).wait_recv()
            if (which == 2) == (by > 0):
                start(over_y(by, source, x, which, 6))
            start(over_x(source, x, which, 2 * which + (0 if by > 0 else 1)))
    for which in (0, 1):
        over_x(y, 1 - x, which, which).wait_recv()
        for by in (1, -1):
            start(over_y(by, y, 1 - x, which, 4 + which))
    far = me.turn(2)
    for which, by in ((2, 1), (3, -1)):
        over_y(by, far, x, which, 6).wait_recv()
        start(over_x(far, x, which, 6 + which))
    for which, by in ((0, 1), (1, -1)):
        source = me.turn(-by)
        over_y(by, source, x, which, which).wait_recv()
        start(over_y(by, source, x, which, 7))
    for which, by in ((0, 1), (1, -1)):
        source = me.turn(-by)
        over_y(by, source, 1 - x, which, 4 + which).wait_recv()
        start(over_y(by, source, 1 - x, which, 8))
    for which, by in ((0, -1), (1, 1)):
        source = me.turn(-by)
        over_y(by, source, x, which, which).wait_recv()
        over_y(by, source, 1 - x, which, 4 + which).wait_recv()
    for which in (2, 3):
        over_x(y, 1 - x, which, which).wait_recv()
        for by in (1, -1):
            over_x(me.turn(-by), 1 - x, which, 2 * which + (0 if by > 0 else 1)).wait_recv()
        over_x(far, 1 - x, which, 6 + which).wait_recv()
    for which, by in ((0, 1), (1, -1)):
        over_y(by, far, x, which, 7).wait_recv()
        over_y(by, far, 1 - x, which, 8).wait_recv()
    for copy in sent:
        copy.wait_send()
    give.wait_send()
    tell.wait()


def gather_weights(block, split):
    return pl.pallas_call(
        gather_kernel,
        out_shape=(jax.ShapeDtypeStruct((D, COLS), BF), jax.ShapeDtypeStruct(split.shape, split.dtype)),
        in_specs=[pl.BlockSpec(memory_space=pl.ANY)] * 2,
        out_specs=[pl.BlockSpec(memory_space=pl.ANY)] * 2,
        scratch_shapes=[
            pltpu.SemaphoreType.DMA,
            pltpu.SemaphoreType.DMA((10,)),
            pltpu.SemaphoreType.DMA((10,)),
            pltpu.SemaphoreType.DMA((2, 9)),
            pltpu.SemaphoreType.DMA((2, 9)),
            pltpu.SemaphoreType.DMA((2,)),
            pltpu.SemaphoreType.DMA((2,)),
        ],
        compiler_params=pltpu.CompilerParams(collective_id=1, has_side_effects=True),
        name="gather_weights",
    )(block, split)


def middle_kernel(
    x_ref, cot_ref, w_hbm, ba_ref, bb_ref, gain_ref, shift_ref, mine_ref, theirs_ref, cos_ref, sin_ref,
    lo_ref, ig_ref, n_out, h_out, g_out, p_out, sa_ref, sb_ref,
    w, normed, grads, qkv, hcat, slope, probs, gproj, part, got, zgot, xrow, grow, ctab, stab, split,
    wsem, agz_s, agz_r, ags_s, ags_r, par_s, par_r, rsz_s, rsz_r, sec_s, sec_r, osem,
):
    me = Place()
    section = lax.axis_index("section")
    core, z = me.core, me.z
    greet([me.z_peer(1), me.z_peer(2), me.z_peer(3), me.sibling, {"section": 1 - section}])

    load_a = pltpu.make_async_copy(w_hbm.at[:, pl.ds(0, A_COLS)], w.at[:, pl.ds(0, A_COLS)], wsem.at[0])
    load_b = pltpu.make_async_copy(w_hbm.at[:, pl.ds(A_COLS, B_COLS)], w.at[:, pl.ds(A_COLS, B_COLS)], wsem.at[1])

    def band(at):
        return pl.ds(pl.multiple_of(at * ROWS, ROWS), ROWS)

    def standard(rows):
        average = jnp.mean(rows, axis=-1, keepdims=True)
        centred = rows - average
        variance = jnp.mean(centred * centred, axis=-1, keepdims=True)
        scale = lax.rsqrt(variance + EPSILON)
        return centred * scale, scale

    def spread_buffer(back):
        return grads if back else normed

    def to_z(back, m, i, k):
        piece = spread_buffer(back).at[i, band(z)]
        return remote(piece, piece, agz_s.at[back, m, k], agz_r.at[back, m, k], me.z_peer(1 + k))

    def from_z(back, m, i, k):
        piece = spread_buffer(back).at[i, band(lax.rem(z + 3 - k, 4))]
        return remote(piece, piece, agz_s.at[back, m, k], agz_r.at[back, m, k], me.z_peer(3 - k))

    def to_sibling(back, m, i, k):
        piece = spread_buffer(back).at[i, band(lax.rem(z + 3 - k, 4))]
        return remote(piece, piece, ags_s.at[back, m, k], ags_r.at[back, m, k], me.sibling)

    def spread_own(back, m):
        i = 2 * m + core
        if back:
            grads[i, band(z)] = grow[m]
        else:
            xhat, _ = standard(xrow[m].astype(F32))
            normed[i, band(z)] = (xhat * gain_ref[...] + shift_ref[...]).astype(BF)
        for k in range(3):
            to_z(back, m, i, k).start()
        to_sibling(back, m, i, 3).start()

    def relay(back, i):
        m = i // 2
        for k in range(3):
            from_z(back, m, i, k).wait_recv()
            to_sibling(back, m, i, k).start()

    def await_rows(back, i):
        m = i // 2

        @pl.when(lax.rem(i, 2) != core)
        def _():
            for k in range(4):
                to_sibling(back, m, i, k).wait_recv()

    def to_pair(back, i):
        m = i // 2
        return remote(part.at[back * 4 + i], got.at[back * 2 + m], par_s.at[back, m], par_r.at[back, m], me.sibling)

    def sum_to_z(back, m, i, k):
        peer = me.z_peer(1 + k)
        return remote(
            part.at[back * 4 + i, band(peer["tensor"])],
            zgot.at[back * 2 + m, k],
            rsz_s.at[back, m, k],
            rsz_r.at[back, m, k],
            peer,
        )

    def pair_sum(back, i):
        m = i // 2
        to_pair(back, i).wait_recv()
        at = back * 4 + i
        part[at] = (part[at].astype(F32) + got[back * 2 + m].astype(F32)).astype(BF)
        for k in range(3):
            sum_to_z(back, m, i, k).start()

    def row_sum(back, i):
        m = i // 2
        total = part[back * 4 + i, band(z)].astype(F32)
        for k in range(3):
            sum_to_z(back, m, i, k).wait_recv()
            total = total + zgot[back * 2 + m, k].astype(F32)
        return total

    def onward(back, m):
        source, target = (ig_ref, grow) if back else (lo_ref, xrow)
        return remote(source.at[m], target.at[m], sec_s.at[back, m], sec_r.at[back, m], {"section": 1 - back})

    def finish_forward(i):
        m = i // 2
        lo_ref[m] = (xrow[m].astype(F32) + row_sum(0, i) + bb_ref[...]).astype(BF)

        @pl.when(section == 0)
        def _():
            onward(0, m).start()

    def finish_backward(i):
        m = i // 2
        grad = row_sum(1, i)
        xhat, scale = standard(xrow[m].astype(F32))
        above = grow[m].astype(F32)
        sb_ref[0:1, :] += jnp.sum(grad * xhat, axis=0, keepdims=True)
        sb_ref[1:2, :] += jnp.sum(grad, axis=0, keepdims=True)
        sb_ref[2:3, :] += jnp.sum(above, axis=0, keepdims=True)
        a = grad * gain_ref[...]
        inner = a - jnp.mean(a, axis=-1, keepdims=True) - xhat * jnp.mean(a * xhat, axis=-1, keepdims=True)
        ig_ref[m] = (above + inner * scale).astype(BF)

        @pl.when(section == 1)
        def _():
            onward(1, m).start()

    lanes = lax.broadcasted_iota(jnp.int32, (SLOT, 128), 1) % HD
    early = lanes < ROT // 2

    def turned(values, i, sign):
        halves = []
        for at in (0, 128):
            piece = values[:, at : at + 128]
            swapped = jnp.where(early, pltpu.roll(piece, 128 - ROT // 2, 1), pltpu.roll(piece, ROT // 2, 1))
            halves.append(piece * ctab[i] + swapped * (stab[i] * sign))
        return jnp.concatenate(halves, axis=1)

    def head_mask(head):
        lane = lax.broadcasted_iota(jnp.int32, (1, MIX), 1)
        return jnp.where(lane // HD == head, 1.0, 0.0).astype(BF)

    def forward_first(i):
        rows = normed[i]
        projected = dot(rows, w[:, 0:QKV]) + ba_ref[0:1, 0:QKV]
        queries = turned(projected[:, 0:MIX], i, 1.0).astype(BF)
        keys = turned(projected[:, MIX : 2 * MIX], i, 1.0).astype(BF)
        values = projected[:, 2 * MIX : 3 * MIX].astype(BF)
        qkv[i, :, 0:MIX] = queries
        qkv[i, :, MIX : 2 * MIX] = keys
        qkv[i, :, 2 * MIX : 3 * MIX] = values
        at = split[pl.ds(i, 1), :]
        at = jnp.concatenate([at, at], axis=1)
        row_at = lax.broadcasted_iota(jnp.int32, (SLOT, SLOT), 0)
        key_at = lax.broadcasted_iota(jnp.int32, (SLOT, SLOT), 1)
        same = jnp.where(row_at < at, 1, 0) == jnp.where(key_at < at, 1, 0)
        allowed = (key_at <= row_at) & same
        mixed = jnp.zeros((SLOT, MIX), F32)
        for head in range(4):
            mask = head_mask(head)
            scores = jnp.where(allowed, dot_nt(queries * mask, keys) * HD**-0.5, -1e30)
            weights = jnp.exp(scores - jnp.max(scores, axis=-1, keepdims=True))
            chances = (weights / jnp.sum(weights, axis=-1, keepdims=True)).astype(BF)
            probs[i, head] = chances
            mixed = mixed + dot(chances, values * mask)
        hcat[i, :, 0:MIX] = mixed.astype(BF)
        v = dot(rows, w[:, QKV:A_COLS]) + ba_ref[0:1, QKV:A_COLS]
        root = np.sqrt(2 / np.pi).astype(np.float32)
        square = v * v
        bent = jnp.tanh(root * (v + 0.044715 * (square * v)))
        half = 0.5 * (1.0 + bent)
        hcat[i, :, MIX:B_COLS] = (v * half).astype(BF)
        slope[i] = (half + 0.5 * v * (1.0 - bent * bent) * (root * (1.0 + 3 * 0.044715 * square))).astype(BF)

    def forward_second(i):
        part[i] = dot_nt(hcat[i], w[:, A_COLS:COLS]).astype(BF)

    def backward_first(i):
        grad_hidden = dot(grads[i], w[:, A_COLS:COLS])
        grad_pre = (grad_hidden[:, MIX:B_COLS] * slope[i].astype(F32)).astype(BF)
        gproj[i, :, QKV:A_COLS] = grad_pre
        sa_ref[0:1, QKV:A_COLS] += jnp.sum(grad_pre.astype(F32), axis=0, keepdims=True)
        grad_mixed = grad_hidden[:, 0:MIX].astype(BF)
        queries = qkv[i, :, 0:MIX]
        keys = qkv[i, :, MIX : 2 * MIX]
        values = qkv[i, :, 2 * MIX : 3 * MIX]
        zero = jnp.zeros((SLOT, MIX), F32)
        grad_queries, grad_keys, grad_values = zero, zero, zero
        for head in range(4):
            mask = head_mask(head)
            chances = probs[i, head]
            masked = grad_mixed * mask
            grad_values = grad_values + dot_tn(chances, masked)
            grad_probs = dot_nt(masked, values)
            wide = chances.astype(F32)
            centre = jnp.sum(wide * grad_probs, axis=-1, keepdims=True)
            grad_scores = (wide * (grad_probs - centre)).astype(BF)
            grad_queries = grad_queries + dot(grad_scores, keys * mask)
            grad_keys = grad_keys + dot_tn(grad_scores, queries * mask)
        pieces = (
            turned(grad_queries * HD**-0.5, i, -1.0).astype(BF),
            turned(grad_keys * HD**-0.5, i, -1.0).astype(BF),
            grad_values.astype(BF),
        )
        for at, piece in enumerate(pieces):
            span = slice(at * MIX, (at + 1) * MIX)
            gproj[i, :, span] = piece
            sa_ref[0:1, span] += jnp.sum(piece.astype(F32), axis=0, keepdims=True)

    def backward_second(i):
        part[4 + i] = dot_nt(gproj[i], w[:, 0:A_COLS]).astype(BF)

    def keep(which, i):
        source, target = ((normed, n_out), (hcat, h_out), (grads, g_out), (gproj, p_out))[which]
        return pltpu.make_async_copy(source.at[i], target.at[i], osem.at[which, i])

    load_a.start()
    load_b.start()
    sa_ref[...] = jnp.zeros_like(sa_ref)
    sb_ref[...] = jnp.zeros_like(sb_ref)

    @pl.when(section == 0)
    def _():
        xrow[...] = x_ref[...]
        for m in range(2):
            spread_own(0, m)

    @pl.when(section == 1)
    def _():
        grow[...] = cot_ref[...]
        for m in range(2):
            spread_own(1, m)

    places = lax.broadcasted_iota(jnp.int32, (SLOT, 128), 0)
    sign = jnp.where(early, -1.0, 1.0)
    for i in range(4):
        at = jnp.where(core == i % 2, mine_ref[i // 2 : i // 2 + 1, :], theirs_ref[i // 2 : i // 2 + 1, :])
        split[i : i + 1, :] = at
        first = places < at
        here = places == at
        cosine, sine = cos_ref[...], sin_ref[...]
        cos_at = jnp.sum(jnp.where(here, cosine, 0.0), axis=0, keepdims=True)
        sin_at = jnp.sum(jnp.where(here, sine, 0.0), axis=0, keepdims=True)
        ctab[i] = jnp.where(first, cosine, cosine * cos_at + sine * sin_at)
        stab[i] = jnp.where(first, sine, sine * cos_at - cosine * sin_at) * sign

    @pl.when((section == 1) & (core == 0))
    def _():
        onward(0, 0).wait_recv()
        spread_own(0, 0)

    @pl.when(core == 0)
    def _():
        relay(0, 0)

    load_a.wait()
    load_b.wait()

    def forward_step(i, _):
        own = lax.rem(i, 2) == core

        @pl.when((section == 1) & (i < 3) & jnp.logical_not(own))
        def _():
            onward(0, (i + 1) // 2).wait_recv()
            spread_own(0, (i + 1) // 2)

        @pl.when(i < 4)
        def _():
            await_rows(0, i)
            forward_first(i)

        @pl.when((i < 3) & jnp.logical_not(own))
        def _():
            relay(0, i + 1)

        @pl.when((i >= 1) & (i < 5) & jnp.logical_not(own))
        def _():
            pair_sum(0, i - 1)

        @pl.when((i >= 2) & own)
        def _():
            finish_forward(i - 2)

        @pl.when(i < 4)
        def _():
            forward_second(i)
            keep(0, i).start()
            keep(1, i).start()

            @pl.when(jnp.logical_not(own))
            def _():
                to_pair(0, i).start()

        return 0

    lax.fori_loop(0, 6, forward_step, 0)

    @pl.when((section == 0) & (core == 0))
    def _():
        onward(1, 0).wait_recv()
        spread_own(1, 0)

    @pl.when(core == 0)
    def _():
        relay(1, 0)

    def backward_step(i, _):
        own = lax.rem(i, 2) == core

        @pl.when((section == 0) & (i < 3) & jnp.logical_not(own))
        def _():
            onward(1, (i + 1) // 2).wait_recv()
            spread_own(1, (i + 1) // 2)

        @pl.when(i < 4)
        def _():
            await_rows(1, i)
            backward_first(i)

        @pl.when((i < 3) & jnp.logical_not(own))
        def _():
            relay(1, i + 1)

        @pl.when((i >= 1) & (i < 5) & jnp.logical_not(own))
        def _():
            pair_sum(1, i - 1)

        @pl.when((i >= 2) & own)
        def _():
            finish_backward(i - 2)

        @pl.when(i < 4)
        def _():
            backward_second(i)
            keep(2, i).start()
            keep(3, i).start()

            @pl.when(jnp.logical_not(own))
            def _():
                to_pair(1, i).start()

        return 0

    lax.fori_loop(0, 6, backward_step, 0)

    for back in range(2):
        for m in range(2):
            mine = 2 * m + core
            for k in range(3):
                to_z(back, m, mine, k).wait_send()
                sum_to_z(back, m, mine, k).wait_send()
            for k in range(4):
                to_sibling(back, m, mine, k).wait_send()
            to_pair(back, 2 * m + 1 - core).wait_send()

        @pl.when(section == back)
        def _():
            for m in range(2):
                onward(back, m).wait_send()

    for which in range(4):
        for i in range(4):
            keep(which, i).wait()


def middle(rows_in, cotangent, w, bias_a, bias_b, gain, shift, mine, theirs):
    places = np.arange(SLOT, dtype=np.float32)
    frequency = (10000.0 ** (-(np.arange(ROT // 2, dtype=np.float32) * np.float32(2.0 / ROT)))).astype(np.float32)
    angles = (places[:, None] * frequency[None, :]).astype(np.float32).astype(np.float64)
    cosine = np.ones((SLOT, HD), np.float32)
    sine = np.zeros((SLOT, HD), np.float32)
    cosine[:, 0:ROT] = np.tile(np.cos(angles), (1, 2))
    sine[:, 0:ROT] = np.tile(np.sin(angles), (1, 2))
    cosine, sine = (jnp.asarray(np.tile(table, (1, 2))) for table in (cosine, sine))
    any_ = pl.BlockSpec(memory_space=pl.ANY)
    vmem = pl.BlockSpec(memory_space=pltpu.VMEM)
    dma = pltpu.SemaphoreType.DMA
    return pl.pallas_call(
        middle_kernel,
        out_shape=(
            jax.ShapeDtypeStruct((2, ROWS, D), BF),
            jax.ShapeDtypeStruct((2, ROWS, D), BF),
            jax.ShapeDtypeStruct((4, SLOT, D), BF),
            jax.ShapeDtypeStruct((4, SLOT, B_COLS), BF),
            jax.ShapeDtypeStruct((4, SLOT, D), BF),
            jax.ShapeDtypeStruct((4, SLOT, A_COLS), BF),
            jax.ShapeDtypeStruct((8, A_COLS), F32),
            jax.ShapeDtypeStruct((8, D), F32),
        ),
        in_specs=[vmem, vmem, any_] + [vmem] * 8,
        out_specs=[vmem, vmem] + [any_] * 4 + [vmem, vmem],
        scratch_shapes=[
            pltpu.VMEM((D, COLS), BF),
            pltpu.VMEM((4, SLOT, D), BF),
            pltpu.VMEM((4, SLOT, D), BF),
            pltpu.VMEM((4, SLOT, QKV), BF),
            pltpu.VMEM((4, SLOT, B_COLS), BF),
            pltpu.VMEM((4, SLOT, UP), BF),
            pltpu.VMEM((4, 4, SLOT, SLOT), BF),
            pltpu.VMEM((4, SLOT, A_COLS), BF),
            pltpu.VMEM((8, SLOT, D), BF),
            pltpu.VMEM((4, SLOT, D), BF),
            pltpu.VMEM((4, 3, ROWS, D), BF),
            pltpu.VMEM((2, ROWS, D), BF),
            pltpu.VMEM((2, ROWS, D), BF),
            pltpu.VMEM((4, SLOT, 128), F32),
            pltpu.VMEM((4, SLOT, 128), F32),
            pltpu.VMEM((8, 128), jnp.int32),
            dma((2,)),
            dma((2, 2, 3)),
            dma((2, 2, 3)),
            dma((2, 2, 4)),
            dma((2, 2, 4)),
            dma((2, 2)),
            dma((2, 2)),
            dma((2, 2, 3)),
            dma((2, 2, 3)),
            dma((2, 2)),
            dma((2, 2)),
            dma((4, 4)),
        ],
        compiler_params=pltpu.CompilerParams(
            collective_id=2, has_side_effects=True, vmem_limit_bytes=62 * MIB
        ),
        name="both_layers",
    )(rows_in, cotangent, w, bias_a, bias_b, gain, shift, mine, theirs, cosine, sine)


def weights_kernel(
    n_hbm, p_hbm, g_hbm, h_hbm, sa_ref, sb_ref, out, sums_ref,
    rows_n, rows_p, rows_g, rows_h, xb_out, xb_in, far_a, far_b, half_a, half_b, near_a, near_b, got_a, got_b,
    xa_out, xa_in, done, tally, came, lsem, xs, xr, fs, fr, ns, nr, ss, sr, osem, ts, tr,
):
    me = Place()
    x, y, core = me.x, me.y, me.core
    loads = [
        pltpu.make_async_copy(source, target, lsem.at[at])
        for at, (source, target) in enumerate(
            ((g_hbm, rows_g), (h_hbm, rows_h), (n_hbm, rows_n), (p_hbm, rows_p))
        )
    ]
    for load in loads:
        load.start()
    near_z = {"tensor": me.z + 1 - 2 * lax.rem(me.z, 2)}
    near_y = {"dp": me.at(y + 1 - 2 * lax.rem(y, 2), x, core)}
    greet([me.sibling, me.across, me.beside(1), me.beside(-1), me.beside(2), me.z_peer(1), me.z_peer(2), me.z_peer(3)])
    sent = []

    partners = (me.across, near_y, me.beside(2), near_z, me.z_peer(2), me.sibling)

    def exchange(step):
        return remote(tally.at[step], came.at[step], ts.at[step], tr.at[step], partners[step])

    def fold(step):
        exchange(step).wait_recv()
        total = tally[step] + came[step]
        if step < 3:
            tally[step + 1] = total
        else:
            tally[step + 1, 0:3] = total[0:3]
            tally[step + 1, 3:8] = tally[step, 3:8]
        if step < 5:
            start(exchange(step + 1))

    def start(copy):
        copy.start()
        sent.append(copy)

    tally[0, 0:3] = sb_ref[0:3]
    tally[0, 3:8] = jnp.zeros((5, D), F32)
    tally[0, 3:4, 0:A_COLS] = sa_ref[0:1]
    start(exchange(0))

    def chip(by, x_at):
        return pl.ds(pl.multiple_of((me.turn(by) * 2 + x_at) * 256, 256), 256)

    def term_a(by, x_at):
        return dot_tn(rows_n[:, chip(by, x_at)], rows_p[...])

    def term_b(by, x_at):
        return dot_tn(rows_g[:, chip(by, x_at)], rows_h[...])

    first_a, second_a = pl.ds(0, A_HALF), pl.ds(A_HALF, A_HALF)
    first_b, second_b = pl.ds(0, B_HALF), pl.ds(B_HALF, B_HALF)

    def cross(k):
        return remote(xb_out.at[k], xb_in.at[k], xs.at[k], xr.at[k], me.across)

    def cross_last():
        return remote(xa_out, xa_in, xs.at[4], xr.at[4], me.across)

    def far_piece(way, x_at):
        by = 1 - 2 * way
        return remote(
            far_a.at[x_at, :, (first_a, second_a)[way]], half_a.at[way, x_at], fs.at[way, x_at], fr.at[way, x_at], me.beside(by)
        )

    def far_piece_b(way):
        by = 1 - 2 * way
        return remote(far_b.at[:, (first_b, second_b)[way]], half_b.at[way], fs.at[way, 2], fr.at[way, 2], me.beside(by))

    def near_piece(way, x_at):
        by = 1 - 2 * way
        return remote(near_a.at[way, x_at], got_a.at[way, x_at], ns.at[way, x_at], nr.at[way, x_at], me.beside(by))

    def near_piece_b(way):
        by = 1 - 2 * way
        return remote(near_b.at[way], got_b.at[way], ns.at[way, 2], nr.at[way, 2], me.beside(by))

    loads[0].wait()
    loads[1].wait()
    turns = (2, 1, -1, 0)
    for k in (0, 1, 2, 3):
        xb_out[k] = term_b(turns[k], 1 - x).astype(BF)
        start(cross(k))
        if k > 0:
            fold(k - 1)
        if k == 0:
            loads[2].wait()
            loads[3].wait()
            for x_at in (1 - x, x):
                far_a[x_at] = term_a(2, x_at).astype(BF)
                for way in (0, 1):
                    start(far_piece(way, x_at))
    cross(0).wait_recv()
    far_b[...] = (term_b(2, x) + xb_in[0].astype(F32)).astype(BF)
    for way in (0, 1):
        start(far_piece_b(way))
    for x_at in (1 - x, x):
        for way in (0, 1):
            total = term_a(1 - 2 * way, x_at)
            far_piece(way, x_at).wait_recv()
            lo, hi = total[:, :A_HALF], total[:, A_HALF:]
            held = half_a[way, x_at].astype(F32)
            if way == 0:
                lo = lo + held
            else:
                hi = hi + held
            near_a[way, x_at, :, first_a] = lo.astype(BF)
            near_a[way, x_at, :, second_a] = hi.astype(BF)
            start(near_piece(way, x_at))
    fold(3)
    for way in (0, 1):
        total = term_b(1 - 2 * way, x)
        cross(1 + way).wait_recv()
        total = total + xb_in[1 + way].astype(F32)
        far_piece_b(way).wait_recv()
        lo, hi = total[:, :B_HALF], total[:, B_HALF:]
        held = half_b[way].astype(F32)
        if way == 0:
            lo = lo + held
        else:
            hi = hi + held
        near_b[way, :, first_b] = lo.astype(BF)
        near_b[way, :, second_b] = hi.astype(BF)
        start(near_piece_b(way))
    fold(4)
    total = term_a(0, 1 - x)
    for way in (0, 1):
        near_piece(way, 1 - x).wait_recv()
        total = total + got_a[way, 1 - x].astype(F32)
    xa_out[...] = total.astype(BF)
    start(cross_last())
    fold(5)
    sums_ref[...] = tally[6]
    sums_ref[4:5] = came[5, 3:4]
    total = term_b(0, x)
    cross(3).wait_recv()
    total = total + xb_in[3].astype(F32)
    for way in (0, 1):
        near_piece_b(way).wait_recv()
        total = total + got_b[way].astype(F32)
    done[:, pl.ds(A_COLS, B_COLS)] = total
    total = term_a(0, x)
    for way in (0, 1):
        near_piece(way, x).wait_recv()
        total = total + got_a[way, x].astype(F32)
    cross_last().wait_recv()
    done[:, pl.ds(0, A_COLS)] = total + xa_in[...].astype(F32)

    def half(at):
        return done.at[pl.ds(pl.multiple_of(at * 128, 128), 128)]

    give = remote(half(1 - core), out.at[core], ss, sr, me.sibling)
    give.start()
    keep = pltpu.make_async_copy(half(core), out.at[core], osem)
    keep.start()
    keep.wait()
    give.wait_send()
    remote(half(1 - core), out.at[1 - core], ss, sr, me.sibling).wait_recv()
    for copy in sent:
        copy.wait_send()


def weight_gradients(normed, gproj, grads, hcat, sums_a, sums_b):
    dma = pltpu.SemaphoreType.DMA
    rows = 4 * SLOT
    return pl.pallas_call(
        weights_kernel,
        out_shape=(jax.ShapeDtypeStruct((2, 128, COLS), F32), jax.ShapeDtypeStruct((8, D), F32)),
        in_specs=[pl.BlockSpec(memory_space=pl.ANY)] * 4 + [pl.BlockSpec(memory_space=pltpu.VMEM)] * 2,
        out_specs=[pl.BlockSpec(memory_space=pl.ANY), pl.BlockSpec(memory_space=pltpu.VMEM)],
        scratch_shapes=[
            pltpu.VMEM((rows, D), BF),
            pltpu.VMEM((rows, A_COLS), BF),
            pltpu.VMEM((rows, D), BF),
            pltpu.VMEM((rows, B_COLS), BF),
            pltpu.VMEM((4, 256, B_COLS), BF),
            pltpu.VMEM((4, 256, B_COLS), BF),
            pltpu.VMEM((2, 256, A_COLS), BF),
            pltpu.VMEM((256, B_COLS), BF),
            pltpu.VMEM((2, 2, 256, A_HALF), BF),
            pltpu.VMEM((2, 256, B_HALF), BF),
            pltpu.VMEM((2, 2, 256, A_COLS), BF),
            pltpu.VMEM((2, 256, B_COLS), BF),
            pltpu.VMEM((2, 2, 256, A_COLS), BF),
            pltpu.VMEM((2, 256, B_COLS), BF),
            pltpu.VMEM((256, A_COLS), BF),
            pltpu.VMEM((256, A_COLS), BF),
            pltpu.VMEM((256, COLS), F32),
            pltpu.VMEM((7, 8, D), F32),
            pltpu.VMEM((6, 8, D), F32),
            dma((4,)),
            dma((5,)),
            dma((5,)),
            dma((2, 3)),
            dma((2, 3)),
            dma((2, 3)),
            dma((2, 3)),
            dma,
            dma,
            dma,
            dma((6,)),
            dma((6,)),
        ],
        compiler_params=pltpu.CompilerParams(
            collective_id=3, has_side_effects=True, vmem_limit_bytes=60 * MIB
        ),
        name="weight_gradients",
    )(normed.reshape(rows, D), gproj.reshape(rows, A_COLS), grads.reshape(rows, D), hcat.reshape(rows, B_COLS), sums_a, sums_b)


def shards(
    inputs,
    cotangent,
    doc_split,
    qkv_weight,
    qkv_bias,
    out_weight,
    out_bias,
    fc1_weight,
    fc1_bias,
    fc2_weight,
    fc2_bias,
    ln_gain,
    ln_bias,
):
    core = lax.rem(lax.axis_index("dp"), 2)
    block = jnp.concatenate(
        [
            qkv_weight[0].reshape(128, 3, 2, MIX).transpose(2, 0, 1, 3).reshape(2, 128, QKV),
            fc1_weight[0].reshape(128, 2, UP).transpose(1, 0, 2),
            out_weight[0].reshape(2, MIX, 128).transpose(0, 2, 1),
            fc2_weight[0].reshape(2, UP, 128).transpose(0, 2, 1),
        ],
        axis=2,
    )
    mine = jnp.zeros((8, 128), jnp.int32).at[0:2].set(jnp.broadcast_to(doc_split, (2, 128)))
    bias_a = jnp.concatenate(
        [
            lax.dynamic_slice_in_dim(qkv_bias[0], core * MIX, MIX, 1).reshape(1, QKV),
            lax.dynamic_slice_in_dim(fc1_bias[0], core * UP, UP, 0).reshape(1, UP),
        ],
        axis=1,
    )
    bias_b = out_bias + fc2_bias
    w, theirs = gather_weights(block, mine)
    layer_out, input_grad, normed, hcat, grads, gproj, sums_a, sums_b = middle(
        inputs[:, 0], cotangent[:, 0], w, bias_a, bias_b, ln_gain, ln_bias, mine, theirs
    )
    total, sums = weight_gradients(normed, gproj, grads, hcat, sums_a, sums_b)
    sums_a = jnp.where(core == 0, sums[3:5], sums[4:2:-1])[:, 0:A_COLS]
    grad_qkv = total[:, :, 0:QKV].reshape(2, 128, 3, MIX).transpose(1, 2, 0, 3).reshape(128, 3, 2 * MIX)
    grad_fc1 = total[:, :, QKV:A_COLS].transpose(1, 0, 2).reshape(128, 2 * UP)
    grad_out = total[:, :, A_COLS : A_COLS + MIX].transpose(0, 2, 1).reshape(2 * MIX, 128)
    grad_fc2 = total[:, :, A_COLS + MIX :].transpose(0, 2, 1).reshape(2 * UP, 128)
    qkv_bias_grad = sums_a[:, 0:QKV].reshape(2, 3, MIX).transpose(1, 0, 2).reshape(3, 2 * MIX)
    fc1_bias_grad = sums_a[:, QKV:].reshape(2 * UP)
    return (
        layer_out[None, :, None],
        input_grad[None, :, None],
        grad_qkv[None],
        qkv_bias_grad[None],
        grad_out[None],
        sums[2][None],
        grad_fc1[None],
        fc1_bias_grad[None],
        grad_fc2[None],
        sums[2][None],
        sums[0][None],
        sums[1][None],
    )


def solution(mesh):
    rows = P(None, "dp", "tensor", None)
    placed_weights = (
        P("section", "dp", None, "tensor"),
        P("section", None, "tensor"),
        P("section", "tensor", "dp"),
        P("section", None),
        P("section", "dp", "tensor"),
        P("section", "tensor"),
        P("section", "tensor", "dp"),
        P("section", None),
        P("section", None),
        P("section", None),
    )
    out_rows = P("section", None, "dp", "tensor", None)
    return jax.shard_map(
        shards,
        mesh=mesh,
        in_specs=(rows, rows, P(None, "dp")) + placed_weights,
        out_specs=(out_rows, out_rows) + placed_weights,
        check_vma=False,
    )
```

```python
from functools import partial

import jax
import jax.numpy as jnp
import numpy as np
from jax import lax
from jax.experimental import pallas as pl
from jax.experimental.pallas import tpu as pltpu
from jax.sharding import PartitionSpec as P

HD = 64
ROT = 32
EPSILON = 1e-05
MESH = pl.DeviceIdType.MESH
BF = jnp.bfloat16
F32 = jnp.float32

D = 2048
SLOT = 256
ROWS = 64
QKV = 768
UP = 1024
A_COLS = QKV + UP
MIX = 256
B_COLS = MIX + UP
COLS = A_COLS + B_COLS
A_HALF = A_COLS // 2
B_HALF = B_COLS // 2
MIB = 2**20


def dot(a, b):
    return lax.dot_general(a, b, (((1,), (0,)), ((), ())), preferred_element_type=F32)


def dot_nt(a, b):
    return lax.dot_general(a, b, (((1,), (1,)), ((), ())), preferred_element_type=F32)


def dot_tn(a, b):
    return lax.dot_general(a, b, (((0,), (0,)), ((), ())), preferred_element_type=F32)


def remote(src, dst, send, recv, device):
    return pltpu.make_async_remote_copy(
        src_ref=src, dst_ref=dst, send_sem=send, recv_sem=recv, device_id=device, device_id_type=MESH
    )


def greet(peers):
    barrier = pltpu.get_barrier_semaphore()
    for peer in peers:
        pl.semaphore_signal(barrier, inc=1, device_id=peer, device_id_type=MESH)
    pl.semaphore_wait(barrier, len(peers))


class Place:
    def __init__(self):
        self.dp = lax.axis_index("dp")
        self.core = lax.rem(self.dp, 2)
        self.x = lax.rem(self.dp // 2, 2)
        self.y = self.dp // 4
        self.z = lax.axis_index("tensor")
        self.sibling = {"dp": self.dp + 1 - 2 * self.core}
        self.across = {"dp": self.at(self.y, 1 - self.x, self.core)}

    def at(self, y, x, core):
        return (y * 2 + x) * 2 + core

    def turn(self, by):
        return lax.rem(self.y + 4 + by, 4)

    def beside(self, by):
        return {"dp": self.at(self.turn(by), self.x, self.core)}

    def z_peer(self, by):
        return {"tensor": lax.rem(self.z + by, 4)}


STAGES = (
    ((0, 512), (512, 512), (1024, 384), (1408, 384)),
    ((1792, 384), (2176, 384), (2560, 256), (2816, 256)),
)


def layers_kernel(
    x_ref, cot_ref, block, qb_ref, ub_ref, ob_ref, db_ref, gain_ref, shift_ref, mine_ref, cos_ref, sin_ref,
    lo_ref, ig_ref, n_out, h_out, g_out, p_out, sa_ref, sb_ref,
    w, normed, grads, qkv, hcat, slope, probs, gproj, part, got, zgot, xrow, grow, ctab, stab, split, theirs, bias,
    own_sem, x_send, x_recv, y_send, y_recv, sib_send, sib_recv,
    agz_s, agz_r, ags_s, ags_r, par_s, par_r, rsz_s, rsz_r, sec_s, sec_r, osem,
):
    me = Place()
    section = lax.axis_index("section")
    core, z = me.core, me.z
    greet(
        [me.sibling, me.across, me.beside(1), me.beside(-1)]
        + [me.z_peer(1), me.z_peer(2), me.z_peer(3), {"section": 1 - section}]
    )

    def rows(dp):
        return pl.ds(pl.multiple_of(dp * 128, 128), 128)

    def chip(y_at, x_at):
        return pl.ds(pl.multiple_of((y_at * 2 + x_at) * 256, 256), 256)

    other = me.dp + 1 - 2 * core
    hold = pltpu.make_async_copy(block.at[core], w.at[rows(me.dp)], own_sem)
    give = remote(block.at[1 - core], w.at[rows(me.dp)], sib_send.at[0], sib_recv.at[0], me.sibling)
    take = remote(block.at[1 - core], w.at[rows(other)], sib_send.at[0], sib_recv.at[0], me.sibling)
    tell = remote(mine_ref, theirs, sib_send.at[1], sib_recv.at[1], me.sibling)
    y, x = me.y, me.x
    far = me.turn(2)

    def piece_of(stage, y_at, x_at, which):
        return w.at[chip(y_at, x_at), pl.ds(*STAGES[stage][which])]

    def over_x(stage, y_at, x_at, which, slot):
        piece = piece_of(stage, y_at, x_at, which)
        return remote(piece, piece, x_send.at[stage, slot], x_recv.at[stage, slot], me.across)

    def over_y(stage, by, y_at, x_at, which, slot):
        piece = piece_of(stage, y_at, x_at, which)
        way = 0 if by > 0 else 1
        return remote(piece, piece, y_send.at[stage, way, slot], y_recv.at[stage, way, slot], me.beside(by))

    sent = []

    def start(copy):
        copy.start()
        sent.append(copy)

    def own_first(stage):
        for which in (0, 1):
            start(over_x(stage, y, x, which, which))
        for which in (2, 3):
            for by in (1, -1):
                start(over_y(stage, by, y, x, which, which))

    def own_second(stage):
        for which in (2, 3):
            start(over_x(stage, y, x, which, which))
        for which in (0, 1):
            for by in (1, -1):
                start(over_y(stage, by, y, x, which, which))

    def pass_near(stage):
        for which in (2, 3):
            for by in (1, -1):
                source = me.turn(-by)
                over_y(stage, by, source, x, which, which).wait_recv()
                if (which == 2) == (by > 0):
                    start(over_y(stage, by, source, x, which, 6))
                start(over_x(stage, source, x, which, 2 * which + (0 if by > 0 else 1)))

    def pass_crossed(stage):
        for which in (0, 1):
            over_x(stage, y, 1 - x, which, which).wait_recv()
            for by in (1, -1):
                start(over_y(stage, by, y, 1 - x, which, 4 + which))

    def pass_far(stage):
        for which, by in ((2, 1), (3, -1)):
            over_y(stage, by, far, x, which, 6).wait_recv()
            start(over_x(stage, far, x, which, 6 + which))

    def pass_on(stage):
        for which, by in ((0, 1), (1, -1)):
            source = me.turn(-by)
            over_y(stage, by, source, x, which, which).wait_recv()
            start(over_y(stage, by, source, x, which, 7))

    def pass_on_crossed(stage):
        for which, by in ((0, 1), (1, -1)):
            source = me.turn(-by)
            over_y(stage, by, source, 1 - x, which, 4 + which).wait_recv()
            start(over_y(stage, by, source, 1 - x, which, 8))

    def settle(stage):
        for which, by in ((0, -1), (1, 1)):
            source = me.turn(-by)
            over_y(stage, by, source, x, which, which).wait_recv()
            over_y(stage, by, source, 1 - x, which, 4 + which).wait_recv()
        for which in (2, 3):
            over_x(stage, y, 1 - x, which, which).wait_recv()
            for by in (1, -1):
                over_x(stage, me.turn(-by), 1 - x, which, 2 * which + (0 if by > 0 else 1)).wait_recv()
            over_x(stage, far, 1 - x, which, 6 + which).wait_recv()
        for which, by in ((0, 1), (1, -1)):
            over_y(stage, by, far, x, which, 7).wait_recv()
            over_y(stage, by, far, 1 - x, which, 8).wait_recv()

    def band(at):
        return pl.ds(pl.multiple_of(at * ROWS, ROWS), ROWS)

    def standard(rows):
        average = jnp.mean(rows, axis=-1, keepdims=True)
        centred = rows - average
        variance = jnp.mean(centred * centred, axis=-1, keepdims=True)
        scale = lax.rsqrt(variance + EPSILON)
        return centred * scale, scale

    def spread_buffer(back):
        return grads if back else normed

    def to_z(back, m, i, k):
        piece = spread_buffer(back).at[i, band(z)]
        return remote(piece, piece, agz_s.at[back, m, k], agz_r.at[back, m, k], me.z_peer(1 + k))

    def from_z(back, m, i, k):
        piece = spread_buffer(back).at[i, band(lax.rem(z + 3 - k, 4))]
        return remote(piece, piece, agz_s.at[back, m, k], agz_r.at[back, m, k], me.z_peer(3 - k))

    def to_sibling(back, m, i, k):
        piece = spread_buffer(back).at[i, band(lax.rem(z + 3 - k, 4))]
        return remote(piece, piece, ags_s.at[back, m, k], ags_r.at[back, m, k], me.sibling)

    def spread_own(back, m):
        i = 2 * m + core
        if back:
            grads[i, band(z)] = grow[m]
        else:
            xhat, _ = standard(xrow[m].astype(F32))
            normed[i, band(z)] = (xhat * gain_ref[...] + shift_ref[...]).astype(BF)
        for k in range(3):
            to_z(back, m, i, k).start()
        to_sibling(back, m, i, 3).start()

    def relay(back, i):
        m = i // 2
        for k in range(3):
            from_z(back, m, i, k).wait_recv()
            to_sibling(back, m, i, k).start()

    def await_rows(back, i):
        m = i // 2

        @pl.when(lax.rem(i, 2) != core)
        def _():
            for k in range(4):
                to_sibling(back, m, i, k).wait_recv()

    def to_pair(back, i):
        m = i // 2
        return remote(part.at[back * 4 + i], got.at[back * 2 + m], par_s.at[back, m], par_r.at[back, m], me.sibling)

    def sum_to_z(back, m, i, k):
        peer = me.z_peer(1 + k)
        return remote(
            part.at[back * 4 + i, band(peer["tensor"])],
            zgot.at[back * 2 + m, k],
            rsz_s.at[back, m, k],
            rsz_r.at[back, m, k],
            peer,
        )

    def pair_sum(back, i):
        m = i // 2
        to_pair(back, i).wait_recv()
        at = back * 4 + i
        part[at] = (part[at].astype(F32) + got[back * 2 + m].astype(F32)).astype(BF)
        for k in range(3):
            sum_to_z(back, m, i, k).start()

    def row_sum(back, i):
        m = i // 2
        total = part[back * 4 + i, band(z)].astype(F32)
        for k in range(3):
            sum_to_z(back, m, i, k).wait_recv()
            total = total + zgot[back * 2 + m, k].astype(F32)
        return total

    def onward(back, m):
        source, target = (ig_ref, grow) if back else (lo_ref, xrow)
        return remote(source.at[m], target.at[m], sec_s.at[back, m], sec_r.at[back, m], {"section": 1 - back})

    def finish_forward(i):
        m = i // 2
        lo_ref[m] = (xrow[m].astype(F32) + row_sum(0, i) + (ob_ref[...] + db_ref[...])).astype(BF)

        @pl.when(section == 0)
        def _():
            onward(0, m).start()

    def finish_backward(i):
        m = i // 2
        grad = row_sum(1, i)
        xhat, scale = standard(xrow[m].astype(F32))
        above = grow[m].astype(F32)
        sb_ref[0:1, :] += jnp.sum(grad * xhat, axis=0, keepdims=True)
        sb_ref[1:2, :] += jnp.sum(grad, axis=0, keepdims=True)
        sb_ref[2:3, :] += jnp.sum(above, axis=0, keepdims=True)
        a = grad * gain_ref[...]
        inner = a - jnp.mean(a, axis=-1, keepdims=True) - xhat * jnp.mean(a * xhat, axis=-1, keepdims=True)
        ig_ref[m] = (above + inner * scale).astype(BF)

        @pl.when(section == 1)
        def _():
            onward(1, m).start()

    lanes = lax.broadcasted_iota(jnp.int32, (SLOT, 128), 1) % HD
    early = lanes < ROT // 2

    def turned(values, i, sign):
        halves = []
        for at in (0, 128):
            piece = values[:, at : at + 128]
            swapped = jnp.where(early, pltpu.roll(piece, 128 - ROT // 2, 1), pltpu.roll(piece, ROT // 2, 1))
            halves.append(piece * ctab[i] + swapped * (stab[i] * sign))
        return jnp.concatenate(halves, axis=1)

    def head_mask(head):
        lane = lax.broadcasted_iota(jnp.int32, (1, MIX), 1)
        return jnp.where(lane // HD == head, 1.0, 0.0).astype(BF)

    def forward_first(i):
        rows = normed[i]
        projected = dot(rows, w[:, 0:QKV]) + bias[0:1, 0:QKV]
        queries = turned(projected[:, 0:MIX], i, 1.0).astype(BF)
        keys = turned(projected[:, MIX : 2 * MIX], i, 1.0).astype(BF)
        values = projected[:, 2 * MIX : 3 * MIX].astype(BF)
        qkv[i, :, 0:MIX] = queries
        qkv[i, :, MIX : 2 * MIX] = keys
        qkv[i, :, 2 * MIX : 3 * MIX] = values
        at = split[pl.ds(i, 1), :]
        at = jnp.concatenate([at, at], axis=1)
        row_at = lax.broadcasted_iota(jnp.int32, (SLOT, SLOT), 0)
        key_at = lax.broadcasted_iota(jnp.int32, (SLOT, SLOT), 1)
        same = jnp.where(row_at < at, 1, 0) == jnp.where(key_at < at, 1, 0)
        allowed = (key_at <= row_at) & same
        mixed = jnp.zeros((SLOT, MIX), F32)
        for head in range(4):
            mask = head_mask(head)
            scores = jnp.where(allowed, dot_nt(queries * mask, keys) * HD**-0.5, -1e30)
            weights = jnp.exp(scores - jnp.max(scores, axis=-1, keepdims=True))
            chances = (weights / jnp.sum(weights, axis=-1, keepdims=True)).astype(BF)
            probs[i, head] = chances
            mixed = mixed + dot(chances, values * mask)
        hcat[i, :, 0:MIX] = mixed.astype(BF)
        v = dot(rows, w[:, QKV:A_COLS]) + bias[0:1, QKV:A_COLS]
        root = np.sqrt(2 / np.pi).astype(np.float32)
        square = v * v
        bent = jnp.tanh(root * (v + 0.044715 * (square * v)))
        half = 0.5 * (1.0 + bent)
        hcat[i, :, MIX:B_COLS] = (v * half).astype(BF)
        slope[i] = (half + 0.5 * v * (1.0 - bent * bent) * (root * (1.0 + 3 * 0.044715 * square))).astype(BF)

    def forward_second(i):
        part[i] = dot_nt(hcat[i], w[:, A_COLS:COLS]).astype(BF)

    def backward_first(i):
        grad_hidden = dot(grads[i], w[:, A_COLS:COLS])
        grad_pre = (grad_hidden[:, MIX:B_COLS] * slope[i].astype(F32)).astype(BF)
        gproj[i, :, QKV:A_COLS] = grad_pre
        sa_ref[0:1, QKV:A_COLS] += jnp.sum(grad_pre.astype(F32), axis=0, keepdims=True)
        grad_mixed = grad_hidden[:, 0:MIX].astype(BF)
        queries = qkv[i, :, 0:MIX]
        keys = qkv[i, :, MIX : 2 * MIX]
        values = qkv[i, :, 2 * MIX : 3 * MIX]
        zero = jnp.zeros((SLOT, MIX), F32)
        grad_queries, grad_keys, grad_values = zero, zero, zero
        for head in range(4):
            mask = head_mask(head)
            chances = probs[i, head]
            masked = grad_mixed * mask
            grad_values = grad_values + dot_tn(chances, masked)
            grad_probs = dot_nt(masked, values)
            wide = chances.astype(F32)
            centre = jnp.sum(wide * grad_probs, axis=-1, keepdims=True)
            grad_scores = (wide * (grad_probs - centre)).astype(BF)
            grad_queries = grad_queries + dot(grad_scores, keys * mask)
            grad_keys = grad_keys + dot_tn(grad_scores, queries * mask)
        pieces = (
            turned(grad_queries * HD**-0.5, i, -1.0).astype(BF),
            turned(grad_keys * HD**-0.5, i, -1.0).astype(BF),
            grad_values.astype(BF),
        )
        for at, piece in enumerate(pieces):
            span = slice(at * MIX, (at + 1) * MIX)
            gproj[i, :, span] = piece
            sa_ref[0:1, span] += jnp.sum(piece.astype(F32), axis=0, keepdims=True)

    def backward_second(i):
        part[4 + i] = dot_nt(gproj[i], w[:, 0:A_COLS]).astype(BF)

    def keep(which, i):
        source, target = ((normed, n_out), (hcat, h_out), (grads, g_out), (gproj, p_out))[which]
        return pltpu.make_async_copy(source.at[i], target.at[i], osem.at[which, i])

    hold.start()
    give.start()
    tell.start()
    sa_ref[...] = jnp.zeros_like(sa_ref)
    sb_ref[...] = jnp.zeros_like(sb_ref)
    hold.wait()
    take.wait_recv()
    own_first(0)
    own_second(0)

    @pl.when(section == 0)
    def _():
        xrow[...] = x_ref[...]
        for m in range(2):
            spread_own(0, m)

    @pl.when(section == 1)
    def _():
        grow[...] = cot_ref[...]
        for m in range(2):
            spread_own(1, m)

    for at in range(3):
        bias[0:1, at * MIX : (at + 1) * MIX] = jnp.where(
            core == 0, qb_ref[at : at + 1, 0:MIX], qb_ref[at : at + 1, MIX : 2 * MIX]
        )
    bias[0:1, QKV:A_COLS] = jnp.where(core == 0, ub_ref[0:1, 0:UP], ub_ref[0:1, UP : 2 * UP])
    tell.wait_recv()
    places = lax.broadcasted_iota(jnp.int32, (SLOT, 128), 0)
    sign = jnp.where(early, -1.0, 1.0)
    for i in range(4):
        at = jnp.where(core == i % 2, mine_ref[i // 2 : i // 2 + 1, :], theirs[i // 2 : i // 2 + 1, :])
        split[i : i + 1, :] = at
        first = places < at
        here = places == at
        cosine, sine = cos_ref[...], sin_ref[...]
        cos_at = jnp.sum(jnp.where(here, cosine, 0.0), axis=0, keepdims=True)
        sin_at = jnp.sum(jnp.where(here, sine, 0.0), axis=0, keepdims=True)
        ctab[i] = jnp.where(first, cosine, cosine * cos_at + sine * sin_at)
        stab[i] = jnp.where(first, sine, sine * cos_at - cosine * sin_at) * sign

    pass_near(0)
    pass_crossed(0)

    def relay_early(m):
        @pl.when(section == 0)
        def _():
            relay(0, 2 * m + core)

        @pl.when(section == 1)
        def _():
            relay(1, 2 * m + core)

    relay_early(0)
    pass_on(0)
    own_first(1)
    pass_far(0)
    relay_early(1)
    pass_on_crossed(0)
    own_second(1)
    settle(0)
    pass_near(1)

    def forward_early(i):
        @pl.when(section == 0)
        def _():
            await_rows(0, i)
            forward_first(i)

    forward_early(0)
    pass_crossed(1)
    forward_early(1)
    pass_on(1)
    pass_far(1)
    forward_early(2)
    forward_early(3)
    pass_on_crossed(1)
    settle(1)

    def forward_last(i):
        forward_second(i)
        keep(0, i).start()
        keep(1, i).start()

        @pl.when(lax.rem(i, 2) != core)
        def _():
            to_pair(0, i).start()

    def finish_forward_all():
        for m in range(2):
            finish_forward(2 * m + core)

    @pl.when(section == 0)
    def _():
        def step(i, _):
            forward_last(i)

            @pl.when(i == 1 + core)
            def _():
                pair_sum(0, core)

            return 0

        lax.fori_loop(0, 4, step, 0)
        pair_sum(0, 2 + core)
        finish_forward_all()

        @pl.when(core == 0)
        def _():
            onward(1, 0).wait_recv()
            spread_own(1, 0)
            relay(1, 0)

    @pl.when(section == 1)
    def _():
        @pl.when(core == 0)
        def _():
            onward(0, 0).wait_recv()
            spread_own(0, 0)
            relay(0, 0)

        def step(i, _):
            own = lax.rem(i, 2) == core

            @pl.when((i < 3) & jnp.logical_not(own))
            def _():
                onward(0, (i + 1) // 2).wait_recv()
                spread_own(0, (i + 1) // 2)

            await_rows(0, i)
            forward_first(i)

            @pl.when((i < 3) & jnp.logical_not(own))
            def _():
                relay(0, i + 1)

            forward_last(i)
            return 0

        lax.fori_loop(0, 4, step, 0)

    def backward_step(i, _):
        own = lax.rem(i, 2) == core

        @pl.when((section == 0) & (i < 3) & jnp.logical_not(own))
        def _():
            onward(1, (i + 1) // 2).wait_recv()
            spread_own(1, (i + 1) // 2)

        @pl.when(i < 4)
        def _():
            await_rows(1, i)
            backward_first(i)

        @pl.when((section == 0) & (i < 3) & jnp.logical_not(own))
        def _():
            relay(1, i + 1)

        @pl.when((i >= 1) & (i < 5) & jnp.logical_not(own))
        def _():
            pair_sum(1, i - 1)

        @pl.when((i >= 2) & own)
        def _():
            finish_backward(i - 2)

        @pl.when(i < 4)
        def _():
            backward_second(i)
            keep(2, i).start()
            keep(3, i).start()

            @pl.when(jnp.logical_not(own))
            def _():
                to_pair(1, i).start()

        return 0

    lax.fori_loop(0, 6, backward_step, 0)

    @pl.when(section == 1)
    def _():
        for m in range(2):
            pair_sum(0, 2 * m + core)
        finish_forward_all()

    for copy in sent:
        copy.wait_send()
    give.wait_send()
    tell.wait_send()
    for back in range(2):
        for m in range(2):
            mine = 2 * m + core
            for k in range(3):
                to_z(back, m, mine, k).wait_send()
                sum_to_z(back, m, mine, k).wait_send()
            for k in range(4):
                to_sibling(back, m, mine, k).wait_send()
            to_pair(back, 2 * m + 1 - core).wait_send()

        @pl.when(section == back)
        def _():
            for m in range(2):
                onward(back, m).wait_send()

    for which in range(4):
        for i in range(4):
            keep(which, i).wait()


def both_layers(rows_in, cotangent, block, bias_qkv, bias_up, bias_out, bias_down, gain, shift, mine):
    places = np.arange(SLOT, dtype=np.float32)
    frequency = (10000.0 ** (-(np.arange(ROT // 2, dtype=np.float32) * np.float32(2.0 / ROT)))).astype(np.float32)
    angles = (places[:, None] * frequency[None, :]).astype(np.float32).astype(np.float64)
    cosine = np.ones((SLOT, HD), np.float32)
    sine = np.zeros((SLOT, HD), np.float32)
    cosine[:, 0:ROT] = np.tile(np.cos(angles), (1, 2))
    sine[:, 0:ROT] = np.tile(np.sin(angles), (1, 2))
    cosine, sine = (jnp.asarray(np.tile(table, (1, 2))) for table in (cosine, sine))
    any_ = pl.BlockSpec(memory_space=pl.ANY)
    vmem = pl.BlockSpec(memory_space=pltpu.VMEM)
    dma = pltpu.SemaphoreType.DMA
    return pl.pallas_call(
        layers_kernel,
        out_shape=(
            jax.ShapeDtypeStruct((2, ROWS, D), BF),
            jax.ShapeDtypeStruct((2, ROWS, D), BF),
            jax.ShapeDtypeStruct((4, SLOT, D), BF),
            jax.ShapeDtypeStruct((4, SLOT, B_COLS), BF),
            jax.ShapeDtypeStruct((4, SLOT, D), BF),
            jax.ShapeDtypeStruct((4, SLOT, A_COLS), BF),
            jax.ShapeDtypeStruct((8, A_COLS), F32),
            jax.ShapeDtypeStruct((8, D), F32),
        ),
        in_specs=[vmem, vmem, any_] + [vmem] * 9,
        out_specs=[vmem, vmem] + [any_] * 4 + [vmem, vmem],
        scratch_shapes=[
            pltpu.VMEM((D, COLS), BF),
            pltpu.VMEM((4, SLOT, D), BF),
            pltpu.VMEM((4, SLOT, D), BF),
            pltpu.VMEM((4, SLOT, QKV), BF),
            pltpu.VMEM((4, SLOT, B_COLS), BF),
            pltpu.VMEM((4, SLOT, UP), BF),
            pltpu.VMEM((4, 4, SLOT, SLOT), BF),
            pltpu.VMEM((4, SLOT, A_COLS), BF),
            pltpu.VMEM((8, SLOT, D), BF),
            pltpu.VMEM((4, SLOT, D), BF),
            pltpu.VMEM((4, 3, ROWS, D), BF),
            pltpu.VMEM((2, ROWS, D), BF),
            pltpu.VMEM((2, ROWS, D), BF),
            pltpu.VMEM((4, SLOT, 128), F32),
            pltpu.VMEM((4, SLOT, 128), F32),
            pltpu.VMEM((8, 128), jnp.int32),
            pltpu.VMEM((8, 128), jnp.int32),
            pltpu.VMEM((8, A_COLS), F32),
            dma,
            dma((2, 10)),
            dma((2, 10)),
            dma((2, 2, 9)),
            dma((2, 2, 9)),
            dma((2,)),
            dma((2,)),
            dma((2, 2, 3)),
            dma((2, 2, 3)),
            dma((2, 2, 4)),
            dma((2, 2, 4)),
            dma((2, 2)),
            dma((2, 2)),
            dma((2, 2, 3)),
            dma((2, 2, 3)),
            dma((2, 2)),
            dma((2, 2)),
            dma((4, 4)),
        ],
        compiler_params=pltpu.CompilerParams(
            collective_id=2, has_side_effects=True, vmem_limit_bytes=62 * MIB
        ),
        name="both_layers",
    )(rows_in, cotangent, block, bias_qkv, bias_up, bias_out, bias_down, gain, shift, mine, cosine, sine)


def weights_kernel(
    n_hbm, p_hbm, g_hbm, h_hbm, sa_ref, sb_ref, out, sums_ref,
    rows_n, rows_p, rows_g, rows_h, xb_out, xb_in, far_a, far_b, half_a, half_b, near_a, near_b, got_a, got_b,
    xa_out, xa_in, done, tally, came, lsem, xs, xr, fs, fr, ns, nr, ss, sr, osem, ts, tr,
):
    me = Place()
    x, y, core = me.x, me.y, me.core
    loads = [
        pltpu.make_async_copy(source, target, lsem.at[at])
        for at, (source, target) in enumerate(
            ((g_hbm, rows_g), (h_hbm, rows_h), (n_hbm, rows_n), (p_hbm, rows_p))
        )
    ]
    for load in loads:
        load.start()
    near_z = {"tensor": me.z + 1 - 2 * lax.rem(me.z, 2)}
    near_y = {"dp": me.at(y + 1 - 2 * lax.rem(y, 2), x, core)}
    greet([me.sibling, me.across, me.beside(1), me.beside(-1), me.beside(2), me.z_peer(1), me.z_peer(2), me.z_peer(3)])
    sent = []

    partners = (me.across, near_y, me.beside(2), near_z, me.z_peer(2), me.sibling)

    def exchange(step):
        return remote(tally.at[step], came.at[step], ts.at[step], tr.at[step], partners[step])

    def fold(step):
        exchange(step).wait_recv()
        total = tally[step] + came[step]
        if step < 3:
            tally[step + 1] = total
        else:
            tally[step + 1, 0:3] = total[0:3]
            tally[step + 1, 3:8] = tally[step, 3:8]
        if step < 5:
            start(exchange(step + 1))

    def start(copy):
        copy.start()
        sent.append(copy)

    tally[0, 0:3] = sb_ref[0:3]
    tally[0, 3:8] = jnp.zeros((5, D), F32)
    tally[0, 3:4, 0:A_COLS] = sa_ref[0:1]
    start(exchange(0))

    def chip(by, x_at):
        return pl.ds(pl.multiple_of((me.turn(by) * 2 + x_at) * 256, 256), 256)

    def term_a(by, x_at):
        return dot_tn(rows_n[:, chip(by, x_at)], rows_p[...])

    def term_b(by, x_at):
        return dot_tn(rows_g[:, chip(by, x_at)], rows_h[...])

    first_a, second_a = pl.ds(0, A_HALF), pl.ds(A_HALF, A_HALF)
    first_b, second_b = pl.ds(0, B_HALF), pl.ds(B_HALF, B_HALF)

    def cross(k):
        return remote(xb_out.at[k], xb_in.at[k], xs.at[k], xr.at[k], me.across)

    def cross_last():
        return remote(xa_out, xa_in, xs.at[4], xr.at[4], me.across)

    def far_piece(way, x_at):
        by = 1 - 2 * way
        return remote(
            far_a.at[x_at, :, (first_a, second_a)[way]], half_a.at[way, x_at], fs.at[way, x_at], fr.at[way, x_at], me.beside(by)
        )

    def far_piece_b(way):
        by = 1 - 2 * way
        return remote(far_b.at[:, (first_b, second_b)[way]], half_b.at[way], fs.at[way, 2], fr.at[way, 2], me.beside(by))

    def near_piece(way, x_at):
        by = 1 - 2 * way
        return remote(near_a.at[way, x_at], got_a.at[way, x_at], ns.at[way, x_at], nr.at[way, x_at], me.beside(by))

    def near_piece_b(way):
        by = 1 - 2 * way
        return remote(near_b.at[way], got_b.at[way], ns.at[way, 2], nr.at[way, 2], me.beside(by))

    loads[0].wait()
    loads[1].wait()
    turns = (2, 1, -1, 0)
    for k in (0, 1, 2, 3):
        xb_out[k] = term_b(turns[k], 1 - x).astype(BF)
        start(cross(k))
        if k > 0:
            fold(k - 1)
        if k == 0:
            loads[2].wait()
            loads[3].wait()
            for x_at in (1 - x, x):
                far_a[x_at] = term_a(2, x_at).astype(BF)
                for way in (0, 1):
                    start(far_piece(way, x_at))
    cross(0).wait_recv()
    far_b[...] = (term_b(2, x) + xb_in[0].astype(F32)).astype(BF)
    for way in (0, 1):
        start(far_piece_b(way))
    for x_at in (1 - x, x):
        for way in (0, 1):
            total = term_a(1 - 2 * way, x_at)
            far_piece(way, x_at).wait_recv()
            lo, hi = total[:, :A_HALF], total[:, A_HALF:]
            held = half_a[way, x_at].astype(F32)
            if way == 0:
                lo = lo + held
            else:
                hi = hi + held
            near_a[way, x_at, :, first_a] = lo.astype(BF)
            near_a[way, x_at, :, second_a] = hi.astype(BF)
            start(near_piece(way, x_at))
    fold(3)
    for way in (0, 1):
        total = term_b(1 - 2 * way, x)
        cross(1 + way).wait_recv()
        total = total + xb_in[1 + way].astype(F32)
        far_piece_b(way).wait_recv()
        lo, hi = total[:, :B_HALF], total[:, B_HALF:]
        held = half_b[way].astype(F32)
        if way == 0:
            lo = lo + held
        else:
            hi = hi + held
        near_b[way, :, first_b] = lo.astype(BF)
        near_b[way, :, second_b] = hi.astype(BF)
        start(near_piece_b(way))
    fold(4)
    total = term_a(0, 1 - x)
    for way in (0, 1):
        near_piece(way, 1 - x).wait_recv()
        total = total + got_a[way, 1 - x].astype(F32)
    xa_out[...] = total.astype(BF)
    start(cross_last())
    fold(5)
    sums_ref[...] = tally[6]
    sums_ref[4:5] = came[5, 3:4]
    total = term_b(0, x)
    cross(3).wait_recv()
    total = total + xb_in[3].astype(F32)
    for way in (0, 1):
        near_piece_b(way).wait_recv()
        total = total + got_b[way].astype(F32)
    done[:, pl.ds(A_COLS, B_COLS)] = total
    total = term_a(0, x)
    for way in (0, 1):
        near_piece(way, x).wait_recv()
        total = total + got_a[way, x].astype(F32)
    cross_last().wait_recv()
    done[:, pl.ds(0, A_COLS)] = total + xa_in[...].astype(F32)

    def half(at):
        return done.at[pl.ds(pl.multiple_of(at * 128, 128), 128)]

    give = remote(half(1 - core), out.at[core], ss, sr, me.sibling)
    give.start()
    keep = pltpu.make_async_copy(half(core), out.at[core], osem)
    keep.start()
    keep.wait()
    give.wait_send()
    remote(half(1 - core), out.at[1 - core], ss, sr, me.sibling).wait_recv()
    for copy in sent:
        copy.wait_send()


def weight_gradients(normed, gproj, grads, hcat, sums_a, sums_b):
    dma = pltpu.SemaphoreType.DMA
    rows = 4 * SLOT
    return pl.pallas_call(
        weights_kernel,
        out_shape=(jax.ShapeDtypeStruct((2, 128, COLS), F32), jax.ShapeDtypeStruct((8, D), F32)),
        in_specs=[pl.BlockSpec(memory_space=pl.ANY)] * 4 + [pl.BlockSpec(memory_space=pltpu.VMEM)] * 2,
        out_specs=[pl.BlockSpec(memory_space=pl.ANY), pl.BlockSpec(memory_space=pltpu.VMEM)],
        scratch_shapes=[
            pltpu.VMEM((rows, D), BF),
            pltpu.VMEM((rows, A_COLS), BF),
            pltpu.VMEM((rows, D), BF),
            pltpu.VMEM((rows, B_COLS), BF),
            pltpu.VMEM((4, 256, B_COLS), BF),
            pltpu.VMEM((4, 256, B_COLS), BF),
            pltpu.VMEM((2, 256, A_COLS), BF),
            pltpu.VMEM((256, B_COLS), BF),
            pltpu.VMEM((2, 2, 256, A_HALF), BF),
            pltpu.VMEM((2, 256, B_HALF), BF),
            pltpu.VMEM((2, 2, 256, A_COLS), BF),
            pltpu.VMEM((2, 256, B_COLS), BF),
            pltpu.VMEM((2, 2, 256, A_COLS), BF),
            pltpu.VMEM((2, 256, B_COLS), BF),
            pltpu.VMEM((256, A_COLS), BF),
            pltpu.VMEM((256, A_COLS), BF),
            pltpu.VMEM((256, COLS), F32),
            pltpu.VMEM((7, 8, D), F32),
            pltpu.VMEM((6, 8, D), F32),
            dma((4,)),
            dma((5,)),
            dma((5,)),
            dma((2, 3)),
            dma((2, 3)),
            dma((2, 3)),
            dma((2, 3)),
            dma,
            dma,
            dma,
            dma((6,)),
            dma((6,)),
        ],
        compiler_params=pltpu.CompilerParams(
            collective_id=1, has_side_effects=True, vmem_limit_bytes=60 * MIB
        ),
        name="weight_gradients",
    )(normed.reshape(rows, D), gproj.reshape(rows, A_COLS), grads.reshape(rows, D), hcat.reshape(rows, B_COLS), sums_a, sums_b)


def shards(
    inputs,
    cotangent,
    doc_split,
    qkv_weight,
    qkv_bias,
    out_weight,
    out_bias,
    fc1_weight,
    fc1_bias,
    fc2_weight,
    fc2_bias,
    ln_gain,
    ln_bias,
):
    core = lax.rem(lax.axis_index("dp"), 2)
    block = jnp.concatenate(
        [
            qkv_weight[0].reshape(128, 3, 2, MIX).transpose(2, 0, 1, 3).reshape(2, 128, QKV),
            fc1_weight[0].reshape(128, 2, UP).transpose(1, 0, 2),
            out_weight[0].reshape(2, MIX, 128).transpose(0, 2, 1),
            fc2_weight[0].reshape(2, UP, 128).transpose(0, 2, 1),
        ],
        axis=2,
    )
    mine = jnp.broadcast_to(doc_split[None], (4, 2, 128)).reshape(8, 128)
    layer_out, input_grad, normed, hcat, grads, gproj, sums_a, sums_b = both_layers(
        inputs[:, 0],
        cotangent[:, 0],
        block,
        qkv_bias[0],
        fc1_bias,
        out_bias,
        fc2_bias,
        ln_gain,
        ln_bias,
        mine,
    )
    total, sums = weight_gradients(normed, gproj, grads, hcat, sums_a, sums_b)
    sums_a = jnp.where(core == 0, sums[3:5], sums[4:2:-1])[:, 0:A_COLS]
    grad_qkv = total[:, :, 0:QKV].reshape(2, 128, 3, MIX).transpose(1, 2, 0, 3).reshape(128, 3, 2 * MIX)
    grad_fc1 = total[:, :, QKV:A_COLS].transpose(1, 0, 2).reshape(128, 2 * UP)
    grad_out = total[:, :, A_COLS : A_COLS + MIX].transpose(0, 2, 1).reshape(2 * MIX, 128)
    grad_fc2 = total[:, :, A_COLS + MIX :].transpose(0, 2, 1).reshape(2 * UP, 128)
    qkv_bias_grad = sums_a[:, 0:QKV].reshape(2, 3, MIX).transpose(1, 0, 2).reshape(3, 2 * MIX)
    fc1_bias_grad = sums_a[:, QKV:].reshape(2 * UP)
    return (
        layer_out[None, :, None],
        input_grad[None, :, None],
        grad_qkv[None],
        qkv_bias_grad[None],
        grad_out[None],
        sums[2][None],
        grad_fc1[None],
        fc1_bias_grad[None],
        grad_fc2[None],
        sums[2][None],
        sums[0][None],
        sums[1][None],
    )


def solution(mesh):
    rows = P(None, "dp", "tensor", None)
    placed_weights = (
        P("section", "dp", None, "tensor"),
        P("section", None, "tensor"),
        P("section", "tensor", "dp"),
        P("section", None),
        P("section", "dp", "tensor"),
        P("section", "tensor"),
        P("section", "tensor", "dp"),
        P("section", None),
        P("section", None),
        P("section", None),
    )
    out_rows = P("section", None, "dp", "tensor", None)
    return jax.shard_map(
        shards,
        mesh=mesh,
        in_specs=(rows, rows, P(None, "dp")) + placed_weights,
        out_specs=(out_rows, out_rows) + placed_weights,
        check_vma=False,
    )
```

```python
from functools import partial

import jax
import jax.numpy as jnp
import numpy as np
from jax import lax
from jax.experimental import pallas as pl
from jax.experimental.pallas import tpu as pltpu
from jax.sharding import PartitionSpec as P

HD = 64
ROT = 32
EPSILON = 1e-05
MESH = pl.DeviceIdType.MESH
BF = jnp.bfloat16
F32 = jnp.float32

D = 2048
SLOT = 256
ROWS = 64
QKV = 768
UP = 1024
A_COLS = QKV + UP
MIX = 256
B_COLS = MIX + UP
A_HALF = A_COLS // 2
B_HALF = B_COLS // 2
ALL = 4 * SLOT
VMEM_LIMIT = 62 * 2**20


def dot(a, b):
    return lax.dot_general(a, b, (((1,), (0,)), ((), ())), preferred_element_type=F32)


def dot_nt(a, b):
    return lax.dot_general(a, b, (((1,), (1,)), ((), ())), preferred_element_type=F32)


def dot_tn(a, b):
    return lax.dot_general(a, b, (((0,), (0,)), ((), ())), preferred_element_type=F32)


def remote(src, dst, send, recv, device):
    return pltpu.make_async_remote_copy(
        src_ref=src, dst_ref=dst, send_sem=send, recv_sem=recv, device_id=device, device_id_type=MESH
    )


def greet(peers):
    barrier = pltpu.get_barrier_semaphore()
    for peer in peers:
        pl.semaphore_signal(barrier, inc=1, device_id=peer, device_id_type=MESH)
    pl.semaphore_wait(barrier, len(peers))


class Place:
    def __init__(self):
        self.dp = lax.axis_index("dp")
        self.core = lax.rem(self.dp, 2)
        self.x = lax.rem(self.dp // 2, 2)
        self.y = self.dp // 4
        self.z = lax.axis_index("tensor")
        self.sibling = {"dp": self.dp + 1 - 2 * self.core}
        self.across = {"dp": self.at(self.y, 1 - self.x, self.core)}

    def at(self, y, x, core):
        return (y * 2 + x) * 2 + core

    def turn(self, by):
        return lax.rem(self.y + 4 + by, 4)

    def beside(self, by):
        return {"dp": self.at(self.turn(by), self.x, self.core)}

    def z_peer(self, by):
        return {"tensor": lax.rem(self.z + by, 4)}


STAGES = (
    ((0, 512), (512, 512), (1024, 384), (1408, 384)),
    ((0, 384), (384, 384), (768, 256), (1024, 256)),
)


def layers_kernel(
    x_hbm, cot_hbm, qkv_hbm, up_hbm, ow_hbm, dw_hbm,
    qb_ref, ub_ref, ob_ref, db_ref, gain_ref, shift_ref, mine_ref, cos_ref, sin_ref,
    lo_out, ig_out, gq_out, gu_out, go_out, gd_out, sums_ref, gqb_ref, gub_ref, aside_out,
    wa, wb, normed, grads, qkv, hcat, slope, probs, gproj, part, got, zgot, xrow, grow, ctab, stab, split, theirs, bias,
    half_a, half_b, got_a, got_b, xa_in, sum_a, tally, came,
    own_sem, x_send, x_recv, y_send, y_recv, sib_send, sib_recv,
    agz_s, agz_r, ags_s, ags_r, par_s, par_r, rsz_s, rsz_r, sec_s, sec_r,
    xs, xr, fs, fr, ns, nr, ts, tr, end_s, end_r, end_k, keep_s, free_sem, pair_free, aside_s,
):
    me = Place()
    section = lax.axis_index("section")
    core, z = me.core, me.z
    greet(
        [me.sibling, me.across, me.beside(1), me.beside(-1), me.beside(2)]
        + [me.z_peer(1), me.z_peer(2), me.z_peer(3), {"section": 1 - section}]
    )

    def device_span(dp):
        return pl.ds(pl.multiple_of(dp * 128, 128), 128)

    def chip_span(y_at, x_at):
        return pl.ds(pl.multiple_of((y_at * 2 + x_at) * 256, 256), 256)

    def place(at, size):
        return pl.ds(pl.multiple_of(at * size, size), size)

    def blocks(dp, half):
        span = device_span(dp)
        pairs = [
            (qkv_hbm.at[k, :, place(half, MIX)], wa.at[span, pl.ds(k * MIX, MIX)]) for k in range(3)
        ]
        pairs.append((up_hbm.at[:, place(half, UP)], wa.at[span, pl.ds(QKV, UP)]))
        pairs.append((ow_hbm.at[place(half, MIX), :], wb.at[pl.ds(0, MIX), span]))
        pairs.append((dw_hbm.at[place(half, UP), :], wb.at[pl.ds(MIX, UP), span]))
        return pairs

    other = me.dp + 1 - 2 * core
    holds = [
        pltpu.make_async_copy(source, target, own_sem.at[at])
        for at, (source, target) in enumerate(blocks(me.dp, core))
    ]
    gives = [
        remote(source, target, sib_send.at[at], sib_recv.at[at], me.sibling)
        for at, (source, target) in enumerate(blocks(me.dp, 1 - core))
    ]
    takes = [
        remote(source, target, sib_send.at[at], sib_recv.at[at], me.sibling)
        for at, (source, target) in enumerate(blocks(other, 1 - core))
    ]
    tell = remote(mine_ref, theirs, sib_send.at[6], sib_recv.at[6], me.sibling)
    rows_in = [
        pltpu.make_async_copy(x_hbm, xrow, own_sem.at[6]),
        pltpu.make_async_copy(cot_hbm, grow, own_sem.at[6]),
    ]
    y, x = me.y, me.x
    far = me.turn(2)

    def piece_of(stage, y_at, x_at, which):
        span = pl.ds(*STAGES[stage][which])
        if stage == 0:
            return wa.at[chip_span(y_at, x_at), span]
        return wb.at[span, chip_span(y_at, x_at)]

    def over_x(stage, y_at, x_at, which, slot):
        piece = piece_of(stage, y_at, x_at, which)
        return remote(piece, piece, x_send.at[stage, slot], x_recv.at[stage, slot], me.across)

    def over_y(stage, by, y_at, x_at, which, slot):
        piece = piece_of(stage, y_at, x_at, which)
        way = 0 if by > 0 else 1
        return remote(piece, piece, y_send.at[stage, way, slot], y_recv.at[stage, way, slot], me.beside(by))

    sent = []

    def start(copy):
        copy.start()
        sent.append(copy)

    def own_first(stage):
        for which in (0, 1):
            start(over_x(stage, y, x, which, which))
        for which in (2, 3):
            for by in (1, -1):
                start(over_y(stage, by, y, x, which, which))

    def own_second(stage):
        for which in (2, 3):
            start(over_x(stage, y, x, which, which))
        for which in (0, 1):
            for by in (1, -1):
                start(over_y(stage, by, y, x, which, which))

    def pass_near(stage):
        for which in (2, 3):
            for by in (1, -1):
                source = me.turn(-by)
                over_y(stage, by, source, x, which, which).wait_recv()
                if (which == 2) == (by > 0):
                    start(over_y(stage, by, source, x, which, 6))
                start(over_x(stage, source, x, which, 2 * which + (0 if by > 0 else 1)))

    def pass_crossed(stage):
        for which in (0, 1):
            over_x(stage, y, 1 - x, which, which).wait_recv()
            for by in (1, -1):
                start(over_y(stage, by, y, 1 - x, which, 4 + which))

    def pass_far(stage):
        for which, by in ((2, 1), (3, -1)):
            over_y(stage, by, far, x, which, 6).wait_recv()
            start(over_x(stage, far, x, which, 6 + which))

    def pass_on(stage):
        for which, by in ((0, 1), (1, -1)):
            source = me.turn(-by)
            over_y(stage, by, source, x, which, which).wait_recv()
            start(over_y(stage, by, source, x, which, 7))

    def pass_on_crossed(stage):
        for which, by in ((0, 1), (1, -1)):
            source = me.turn(-by)
            over_y(stage, by, source, 1 - x, which, 4 + which).wait_recv()
            start(over_y(stage, by, source, 1 - x, which, 8))

    def settle(stage):
        for which, by in ((0, -1), (1, 1)):
            source = me.turn(-by)
            over_y(stage, by, source, x, which, which).wait_recv()
            over_y(stage, by, source, 1 - x, which, 4 + which).wait_recv()
        for which in (2, 3):
            over_x(stage, y, 1 - x, which, which).wait_recv()
            for by in (1, -1):
                over_x(stage, me.turn(-by), 1 - x, which, 2 * which + (0 if by > 0 else 1)).wait_recv()
            over_x(stage, far, 1 - x, which, 6 + which).wait_recv()
        for which, by in ((0, 1), (1, -1)):
            over_y(stage, by, far, x, which, 7).wait_recv()
            over_y(stage, by, far, 1 - x, which, 8).wait_recv()

    def band(at):
        return pl.ds(pl.multiple_of(at * ROWS, ROWS), ROWS)

    def slot(i):
        return pl.ds(pl.multiple_of(i * SLOT, SLOT), SLOT)

    def slot_band(i, at):
        return pl.ds(pl.multiple_of(i * SLOT + at * ROWS, ROWS), ROWS)

    def standard(rows):
        average = jnp.mean(rows, axis=-1, keepdims=True)
        centred = rows - average
        variance = jnp.mean(centred * centred, axis=-1, keepdims=True)
        scale = lax.rsqrt(variance + EPSILON)
        return centred * scale, scale

    def spread_buffer(back):
        return grads if back else normed

    def to_z(back, m, i, k):
        piece = spread_buffer(back).at[slot_band(i, z)]
        return remote(piece, piece, agz_s.at[back, m, k], agz_r.at[back, m, k], me.z_peer(1 + k))

    def from_z(back, m, i, k):
        piece = spread_buffer(back).at[slot_band(i, lax.rem(z + 3 - k, 4))]
        return remote(piece, piece, agz_s.at[back, m, k], agz_r.at[back, m, k], me.z_peer(3 - k))

    def to_sibling(back, m, i, k):
        piece = spread_buffer(back).at[slot_band(i, lax.rem(z + 3 - k, 4))]
        return remote(piece, piece, ags_s.at[back, m, k], ags_r.at[back, m, k], me.sibling)

    def spread_own(back, m):
        i = 2 * m + core
        if back:
            grads[slot_band(i, z)] = grow[m]
        else:
            xhat, _ = standard(xrow[m].astype(F32))
            normed[slot_band(i, z)] = (xhat * gain_ref[...] + shift_ref[...]).astype(BF)
        for k in range(3):
            to_z(back, m, i, k).start()
        to_sibling(back, m, i, 3).start()

    def relay(back, i):
        m = i // 2
        for k in range(3):
            from_z(back, m, i, k).wait_recv()
            to_sibling(back, m, i, k).start()

    def await_rows(back, i):
        m = i // 2

        @pl.when(lax.rem(i, 2) != core)
        def _():
            for k in range(4):
                to_sibling(back, m, i, k).wait_recv()

    def part_at(i):
        return (1 - lax.rem(i + core, 2)) * (i // 2) + lax.rem(i + core, 2) * (2 + i // 2)

    def to_pair(back, i):
        m = i // 2
        return remote(part.at[2 + m], got.at[m], par_s.at[back, m], par_r.at[back, m], me.sibling)

    def sum_to_z(back, m, k):
        peer = me.z_peer(1 + k)
        return remote(
            part.at[m, band(peer["tensor"])],
            zgot.at[back * 2 + m, k],
            rsz_s.at[back, m, k],
            rsz_r.at[back, m, k],
            peer,
        )

    def pair_add(back, m):
        to_pair(back, 2 * m + core).wait_recv()
        part[m] = (part[m].astype(F32) + got[m].astype(F32)).astype(BF)
        if back == 0:
            pl.semaphore_signal(pair_free.at[m], inc=1, device_id=me.sibling, device_id_type=MESH)

    def pair_spread(back, m):
        for k in range(3):
            sum_to_z(back, m, k).start()

    def pair_sum(back, m):
        pair_add(back, m)
        pair_spread(back, m)

    def pair_sent(back, m):
        for k in range(3):
            sum_to_z(back, m, k).wait_send()

    def aside(m):
        return pltpu.make_async_copy(part.at[m], aside_out.at[m], aside_s.at[0, m])

    def back_again(m):
        return pltpu.make_async_copy(aside_out.at[m], part.at[m], aside_s.at[1, m])

    def row_sum(back, m):
        total = part[m, band(z)].astype(F32)
        for k in range(3):
            sum_to_z(back, m, k).wait_recv()
            total = total + zgot[back * 2 + m, k].astype(F32)
        return total

    def onward(back, m):
        target = grow if back else xrow
        return remote(zgot.at[back * 2 + m, 0], target.at[m], sec_s.at[back, m], sec_r.at[back, m], {"section": 1 - back})

    def keep(back, m):
        target = ig_out if back else lo_out
        return pltpu.make_async_copy(zgot.at[back * 2 + m, 0], target.at[m], keep_s.at[back, m])

    def finish_forward(m):
        zgot[m, 0] = (xrow[m].astype(F32) + row_sum(0, m) + (ob_ref[...] + db_ref[...])).astype(BF)
        keep(0, m).start()

        @pl.when(section == 0)
        def _():
            onward(0, m).start()

    def finish_backward(m):
        grad = row_sum(1, m)
        xhat, scale = standard(xrow[m].astype(F32))
        above = grow[m].astype(F32)
        tally[0, 0:1, :] += jnp.sum(grad * xhat, axis=0, keepdims=True)
        tally[0, 1:2, :] += jnp.sum(grad, axis=0, keepdims=True)
        tally[0, 2:3, :] += jnp.sum(above, axis=0, keepdims=True)
        a = grad * gain_ref[...]
        inner = a - jnp.mean(a, axis=-1, keepdims=True) - xhat * jnp.mean(a * xhat, axis=-1, keepdims=True)
        zgot[2 + m, 0] = (above + inner * scale).astype(BF)
        keep(1, m).start()

        @pl.when(section == 1)
        def _():
            onward(1, m).start()

    lanes = lax.broadcasted_iota(jnp.int32, (SLOT, 128), 1) % HD
    early = lanes < ROT // 2

    places = lax.broadcasted_iota(jnp.int32, (SLOT, 128), 0)

    def tables(i):
        first = places < split[pl.ds(i, 1), :]
        cosine, sine = cos_ref[...], sin_ref[...]
        cos_at, sin_at = ctab[pl.ds(i, 1), :], stab[pl.ds(i, 1), :]
        return (
            jnp.where(first, cosine, cosine * cos_at + sine * sin_at),
            jnp.where(first, sine, sine * cos_at - cosine * sin_at) * jnp.where(early, -1.0, 1.0),
        )

    def turned(values, table, sign):
        halves = []
        for at in (0, 128):
            piece = values[:, at : at + 128]
            swapped = jnp.where(early, pltpu.roll(piece, 128 - ROT // 2, 1), pltpu.roll(piece, ROT // 2, 1))
            halves.append(piece * table[0] + swapped * (table[1] * sign))
        return jnp.concatenate(halves, axis=1)

    def head_mask(head):
        lane = lax.broadcasted_iota(jnp.int32, (1, MIX), 1)
        return jnp.where(lane // HD == head, 1.0, 0.0).astype(BF)

    def forward_first(i):
        rows = normed[slot(i)]
        projected = dot(rows, wa[:, 0:QKV]) + bias[0:1, 0:QKV]
        table = tables(i)
        queries = turned(projected[:, 0:MIX], table, 1.0).astype(BF)
        keys = turned(projected[:, MIX : 2 * MIX], table, 1.0).astype(BF)
        values = projected[:, 2 * MIX : 3 * MIX].astype(BF)
        qkv[slot(i), 0:MIX] = queries
        qkv[slot(i), MIX : 2 * MIX] = keys
        qkv[slot(i), 2 * MIX : 3 * MIX] = values
        at = split[pl.ds(i, 1), :]
        at = jnp.concatenate([at, at], axis=1)
        row_at = lax.broadcasted_iota(jnp.int32, (SLOT, SLOT), 0)
        key_at = lax.broadcasted_iota(jnp.int32, (SLOT, SLOT), 1)
        same = jnp.where(row_at < at, 1, 0) == jnp.where(key_at < at, 1, 0)
        allowed = (key_at <= row_at) & same
        mixed = jnp.zeros((SLOT, MIX), F32)
        for head in range(4):
            mask = head_mask(head)
            scores = jnp.where(allowed, dot_nt(queries * mask, keys) * HD**-0.5, -1e30)
            weights = jnp.exp(scores - jnp.max(scores, axis=-1, keepdims=True))
            chances = (weights / jnp.sum(weights, axis=-1, keepdims=True)).astype(BF)
            probs[i, head] = chances
            mixed = mixed + dot(chances, values * mask)
        hcat[slot(i), 0:MIX] = mixed.astype(BF)
        v = dot(rows, wa[:, QKV:A_COLS]) + bias[0:1, QKV:A_COLS]
        root = np.sqrt(2 / np.pi).astype(np.float32)
        square = v * v
        bent = jnp.tanh(root * (v + 0.044715 * (square * v)))
        half = 0.5 * (1.0 + bent)
        hcat[slot(i), MIX:B_COLS] = (v * half).astype(BF)
        slope[slot(i)] = (half + 0.5 * v * (1.0 - bent * bent) * (root * (1.0 + 3 * 0.044715 * square))).astype(BF)

    def forward_second(i):
        for at in (0, D // 2):
            span = slice(at, at + D // 2)
            part[part_at(i), :, span] = dot(hcat[slot(i)], wb[:, span]).astype(BF)

    def backward_first(i):
        grad_hidden = dot_nt(grads[slot(i)], wb[...])
        grad_pre = (grad_hidden[:, MIX:B_COLS] * slope[slot(i)].astype(F32)).astype(BF)
        gproj[slot(i), QKV:A_COLS] = grad_pre
        sum_a[0:1, QKV:A_COLS] += jnp.sum(grad_pre.astype(F32), axis=0, keepdims=True)
        grad_mixed = grad_hidden[:, 0:MIX].astype(BF)
        queries = qkv[slot(i), 0:MIX]
        keys = qkv[slot(i), MIX : 2 * MIX]
        values = qkv[slot(i), 2 * MIX : 3 * MIX]
        zero = jnp.zeros((SLOT, MIX), F32)
        grad_queries, grad_keys, grad_values = zero, zero, zero
        for head in range(4):
            mask = head_mask(head)
            chances = probs[i, head]
            masked = grad_mixed * mask
            grad_values = grad_values + dot_tn(chances, masked)
            grad_probs = dot_nt(masked, values)
            wide = chances.astype(F32)
            centre = jnp.sum(wide * grad_probs, axis=-1, keepdims=True)
            grad_scores = (wide * (grad_probs - centre)).astype(BF)
            grad_queries = grad_queries + dot(grad_scores, keys * mask)
            grad_keys = grad_keys + dot_tn(grad_scores, queries * mask)
        table = tables(i)
        pieces = (
            turned(grad_queries * HD**-0.5, table, -1.0).astype(BF),
            turned(grad_keys * HD**-0.5, table, -1.0).astype(BF),
            grad_values.astype(BF),
        )
        for at, piece in enumerate(pieces):
            span = slice(at * MIX, (at + 1) * MIX)
            gproj[slot(i), span] = piece
            sum_a[0:1, span] += jnp.sum(piece.astype(F32), axis=0, keepdims=True)

    def backward_second(i):
        for at in (0, D // 2):
            span = slice(at, at + D // 2)
            part[part_at(i), :, span] = dot_nt(gproj[slot(i)], wa[span, :]).astype(BF)

    for copy in holds + gives:
        copy.start()
    tell.start()

    @pl.when(section == 0)
    def _():
        rows_in[0].start()

    @pl.when(section == 1)
    def _():
        rows_in[1].start()

    sum_a[...] = jnp.zeros_like(sum_a)
    tally[0] = jnp.zeros((8, D), F32)
    for at in range(4):
        holds[at].wait()
        takes[at].wait_recv()
    own_first(0)
    own_second(0)

    @pl.when(section == 0)
    def _():
        rows_in[0].wait()
        for m in range(2):
            spread_own(0, m)

    @pl.when(section == 1)
    def _():
        rows_in[1].wait()
        for m in range(2):
            spread_own(1, m)

    for at in (4, 5):
        holds[at].wait()
        takes[at].wait_recv()
    for at in range(3):
        bias[0:1, at * MIX : (at + 1) * MIX] = jnp.where(
            core == 0, qb_ref[at : at + 1, 0:MIX], qb_ref[at : at + 1, MIX : 2 * MIX]
        )
    bias[0:1, QKV:A_COLS] = jnp.where(core == 0, ub_ref[0:1, 0:UP], ub_ref[0:1, UP : 2 * UP])
    tell.wait_recv()
    for i in range(4):
        at = jnp.where(core == i % 2, mine_ref[i // 2 : i // 2 + 1, :], theirs[i // 2 : i // 2 + 1, :])
        split[i : i + 1, :] = at
        here = places == at
        ctab[i : i + 1, :] = jnp.sum(jnp.where(here, cos_ref[...], 0.0), axis=0, keepdims=True)
        stab[i : i + 1, :] = jnp.sum(jnp.where(here, sin_ref[...], 0.0), axis=0, keepdims=True)

    pass_near(0)
    pass_crossed(0)

    def relay_early(m):
        @pl.when(section == 0)
        def _():
            relay(0, 2 * m + core)

        @pl.when(section == 1)
        def _():
            relay(1, 2 * m + core)

    relay_early(0)
    pass_on(0)
    own_first(1)
    pass_far(0)
    relay_early(1)
    pass_on_crossed(0)
    own_second(1)
    settle(0)
    pass_near(1)

    def forward_early(i):
        @pl.when(section == 0)
        def _():
            await_rows(0, i)
            forward_first(i)

    forward_early(0)
    pass_crossed(1)
    forward_early(1)
    pass_on(1)
    pass_far(1)
    forward_early(2)
    forward_early(3)
    pass_on_crossed(1)
    settle(1)

    def forward_last(i):
        forward_second(i)

        @pl.when(lax.rem(i, 2) != core)
        def _():
            to_pair(0, i).start()

    def finish_forward_all():
        for m in range(2):
            finish_forward(m)

    @pl.when(section == 0)
    def _():
        def step(i, _):
            forward_last(i)

            @pl.when(i == 1 + core)
            def _():
                pair_sum(0, 0)

            return 0

        lax.fori_loop(0, 4, step, 0)
        pair_sum(0, 1)
        finish_forward_all()

        @pl.when(core == 0)
        def _():
            onward(1, 0).wait_recv()
            spread_own(1, 0)
            relay(1, 0)

    @pl.when(section == 1)
    def _():
        def arrive(m):
            onward(0, m).wait_recv()
            spread_own(0, m)

        arrive(0)

        @pl.when(core == 0)
        def _():
            relay(0, 0)

        def step(i, _):
            await_rows(0, i)
            forward_first(i)

            @pl.when((i == 0) & (core == 0))
            def _():
                arrive(1)

            @pl.when((i < 3) & (lax.rem(i, 2) != core))
            def _():
                relay(0, i + 1)

            @pl.when((i > 0) & (lax.rem(i, 2) != core))
            def _():
                pair_add(0, (i - 1) // 2)
                aside((i - 1) // 2).start()

            forward_last(i)

            @pl.when((i == 0) & (core == 1))
            def _():
                arrive(1)

            return 0

        lax.fori_loop(0, 4, step, 0)

    def turn_of(k):
        return lax.rem(y + 2 - k + 4, 4)

    a_cuts = ((0, A_HALF), (A_HALF, A_COLS))
    b_cuts = ((0, B_HALF), (B_HALF, B_COLS))

    def term_a(y_at, x_at, half):
        lo, hi = a_cuts[half]
        return dot_tn(normed[:, chip_span(y_at, x_at)], gproj[:, lo:hi])

    def term_b(y_at, x_at, half):
        lo, hi = b_cuts[half]
        return dot_tn(hcat[:, lo:hi], grads[:, chip_span(y_at, x_at)])

    def cross(k):
        span = pl.ds(pl.multiple_of(k * MIX, MIX), MIX)
        there = pl.ds(pl.multiple_of((4 + k) * 256, 256), 256)
        return (
            remote(probs.at[k, 0], wb.at[pl.ds(0, MIX), there], xs.at[k, 0], xr.at[k, 0], me.across),
            remote(slope.at[:, span], wb.at[pl.ds(MIX, UP), there], xs.at[k, 1], xr.at[k, 1], me.across),
        )

    def cross_all():
        pl.semaphore_wait(free_sem, 1)

        def step(k, _):
            span = pl.ds(pl.multiple_of(k * MIX, MIX), MIX)
            total = term_b(turn_of(k), 1 - x, 0).astype(BF)
            probs[k, 0] = total[0:MIX]
            slope[0 : B_HALF - MIX, span] = total[MIX:B_HALF]
            slope[B_HALF - MIX : UP, span] = term_b(turn_of(k), 1 - x, 1).astype(BF)
            for copy in cross(k):
                copy.start()
            return 0

        lax.fori_loop(0, 4, step, 0)

    def crossed(k):
        for copy in cross(k):
            copy.wait_recv()

    def from_across(k, half):
        lo, hi = b_cuts[half]
        return wb[lo:hi, (4 + k) * 256 : (5 + k) * 256].astype(F32)

    def a_place(at):
        return wa.at[pl.ds(pl.multiple_of(at * 256, 256), 256)]

    def b_place(at):
        return wb.at[:, pl.ds(at * 256, 256)]

    a_spans = (pl.ds(0, A_HALF), pl.ds(A_HALF, A_HALF))
    b_spans = (pl.ds(0, B_HALF), pl.ds(B_HALF, B_HALF))

    def far_piece(way, x_at):
        source = wa.at[pl.ds(pl.multiple_of(x_at * 256, 256), 256), a_spans[way]]
        return remote(source, half_a.at[way, x_at], fs.at[way, x_at], fr.at[way, x_at], me.beside(1 - 2 * way))

    def far_piece_b(way):
        source = wb.at[b_spans[way], pl.ds(0, 256)]
        return remote(source, half_b.at[way], fs.at[way, 2], fr.at[way, 2], me.beside(1 - 2 * way))

    def near_piece(way, x_at):
        source = a_place(2 + 2 * way + x_at)
        return remote(source, got_a.at[way, x_at], ns.at[way, x_at], nr.at[way, x_at], me.beside(1 - 2 * way))

    def near_piece_b(way):
        return remote(b_place(1 + way), got_b.at[way], ns.at[way, 2], nr.at[way, 2], me.beside(1 - 2 * way))

    def cross_last():
        return remote(a_place(6), xa_in, xs.at[4, 0], xr.at[4, 0], me.across)

    def send_far(x_at):
        target = pl.ds(pl.multiple_of(x_at * 256, 256), 256)
        for way, (lo, hi) in enumerate(a_cuts):
            wa[target, lo:hi] = term_a(far, x_at, way).astype(BF)
            start(far_piece(way, x_at))

    def send_near(way, x_at):
        target = pl.ds(pl.multiple_of((2 + 2 * way + x_at) * 256, 256), 256)
        for half in (1 - way, way):
            lo, hi = a_cuts[half]
            total = term_a(me.turn(1 - 2 * way), x_at, half)
            if half == way:
                far_piece(way, x_at).wait_recv()
                total = total + half_a[way, x_at].astype(F32)
            wa[target, lo:hi] = total.astype(BF)
        start(near_piece(way, x_at))

    def send_far_b():
        crossed(0)
        for way, (lo, hi) in enumerate(b_cuts):
            wb[lo:hi, 0:256] = (term_b(far, x, way) + from_across(0, way)).astype(BF)
            start(far_piece_b(way))

    def send_near_b(way):
        crossed(1 + 2 * way)
        span = slice((1 + way) * 256, (2 + way) * 256)
        for half in (1 - way, way):
            lo, hi = b_cuts[half]
            total = term_b(me.turn(1 - 2 * way), x, half) + from_across(1 + 2 * way, half)
            if half == way:
                far_piece_b(way).wait_recv()
                total = total + half_b[way].astype(F32)
            wb[lo:hi, span] = total.astype(BF)
        start(near_piece_b(way))

    def arrived_a(x_at, at):
        for half, (lo, hi) in enumerate(a_cuts):
            total = term_a(y, x_at, half)
            for way in (0, 1):
                if half == 0:
                    near_piece(way, x_at).wait_recv()
                total = total + got_a[way, x_at, :, lo:hi].astype(F32)
            wa[at * 256 : (at + 1) * 256, lo:hi] = total.astype(BF)

    def arrived_b(at):
        crossed(2)
        for half, (lo, hi) in enumerate(b_cuts):
            total = term_b(y, x, half) + from_across(2, half)
            for way in (0, 1):
                if half == 0:
                    near_piece_b(way).wait_recv()
                total = total + got_b[way, lo:hi].astype(F32)
            wb[lo:hi, at * 256 : (at + 1) * 256] = total.astype(BF)

    near_z = {"tensor": z + 1 - 2 * lax.rem(z, 2)}
    near_y = {"dp": me.at(y + 1 - 2 * lax.rem(y, 2), x, core)}
    partners = (me.across, near_y, me.beside(2), near_z, me.z_peer(2), me.sibling)

    def exchange(step):
        return remote(tally.at[step], came.at[step], ts.at[step], tr.at[step], partners[step])

    def fold(step):
        exchange(step).wait_recv()
        total = tally[step] + came[step]
        if step < 3:
            tally[step + 1] = total
        else:
            tally[step + 1, 0:3] = total[0:3]
            tally[step + 1, 3:8] = tally[step, 3:8]
        if step < 5:
            start(exchange(step + 1))

    for copy in sent:
        copy.wait_send()
    sent.clear()

    def backward_step(i, _):
        own = lax.rem(i, 2) == core

        @pl.when((section == 0) & (i < 3) & jnp.logical_not(own))
        def _():
            onward(1, (i + 1) // 2).wait_recv()
            spread_own(1, (i + 1) // 2)

        await_rows(1, i)
        backward_first(i)

        @pl.when((section == 0) & (i < 3) & jnp.logical_not(own))
        def _():
            relay(1, i + 1)

        @pl.when(i == 3)
        def _():
            pl.semaphore_signal(free_sem, inc=1, device_id=me.across, device_id_type=MESH)

        @pl.when((section == 0) & (i == 3))
        def _():
            cross_all()

        @pl.when((i >= 1) & jnp.logical_not(own))
        def _():
            pair_sum(1, (i - 1) // 2)

        @pl.when((i >= 2) & own)
        def _():
            finish_backward(0)

        @pl.when((section == 1) & (core == 1) & (i == 0))
        def _():
            pair_add(0, 1)
            aside(1).start()

        @pl.when((section == 0) & own)
        def _():
            pair_sent(0, i // 2)

        @pl.when((section == 1) & own)
        def _():
            aside(i // 2).wait()

        @pl.when(jnp.logical_not(own))
        def _():
            to_pair(0, i).wait_send()

        backward_second(i)

        @pl.when(jnp.logical_not(own))
        def _():
            pl.semaphore_wait(pair_free.at[i // 2], 1)
            to_pair(1, i).start()

        return 0

    lax.fori_loop(0, 4, backward_step, 0)

    @pl.when(section == 1)
    def _():
        @pl.when(core == 1)
        def _():
            pair_sum(1, 1)

        finish_backward(1)
        cross_all()

    send_far(1 - x)
    send_far(x)

    @pl.when((section == 0) & (core == 1))
    def _():
        pair_sum(1, 1)

    @pl.when(section == 1)
    def _():
        for m in range(2):
            pair_sent(1, m)
            back_again(m).start()

    send_far_b()

    @pl.when(section == 1)
    def _():
        for m in range(2):
            back_again(m).wait()
            pair_spread(0, m)

    for way in (0, 1):
        send_near(way, 1 - x)

    @pl.when(section == 0)
    def _():
        finish_backward(1)

    tally[0, 3:4, 0:A_COLS] = sum_a[0:1]
    start(exchange(0))
    for way in (0, 1):
        send_near(way, x)
    fold(0)
    for way in (0, 1):
        send_near_b(way)
    fold(1)

    @pl.when(section == 1)
    def _():
        finish_forward_all()

    arrived_a(1 - x, 6)
    start(cross_last())
    fold(2)
    arrived_b(3)
    fold(3)

    def result(half, peer, at):
        rows = pl.ds(pl.multiple_of(7 * 256 + half * 128, 128), 128)
        cols = pl.ds(pl.multiple_of(3 * 256 + half * 128, 128), 128)
        sources = [wa.at[rows, pl.ds(k * MIX, MIX)] for k in range(3)]
        sources += [wa.at[rows, pl.ds(QKV, UP)], wb.at[pl.ds(0, MIX), cols], wb.at[pl.ds(MIX, UP), cols]]
        targets = [gq_out.at[k, :, place(at, MIX)] for k in range(3)]
        targets += [gu_out.at[:, place(at, UP)], go_out.at[place(at, MIX), :], gd_out.at[place(at, UP), :]]
        if peer:
            return [
                remote(source, target, end_s.at[k], end_r.at[k], me.sibling)
                for k, (source, target) in enumerate(zip(sources, targets))
            ]
        return [
            pltpu.make_async_copy(source, target, end_k.at[k])
            for k, (source, target) in enumerate(zip(sources, targets))
        ]

    outgoing, staying = result(1 - core, True, core), result(core, False, core)
    incoming = result(1 - core, True, 1 - core)
    for at in (4, 5):
        outgoing[at].start()
        staying[at].start()
    fold(4)
    arrived_a(x, 7)
    fold(5)
    sums_ref[...] = tally[6]
    for at in range(3):
        span = slice(at * MIX, (at + 1) * MIX)
        ours, others = tally[6, 3:4, span], came[5, 3:4, span]
        gqb_ref[at : at + 1, 0:MIX] = jnp.where(core == 0, ours, others)
        gqb_ref[at : at + 1, MIX : 2 * MIX] = jnp.where(core == 0, others, ours)
    ours, others = tally[6, 3:4, QKV:A_COLS], came[5, 3:4, QKV:A_COLS]
    gub_ref[0:1, 0:UP] = jnp.where(core == 0, ours, others)
    gub_ref[0:1, UP : 2 * UP] = jnp.where(core == 0, others, ours)
    cross_last().wait_recv()
    wa[7 * 256 : 8 * 256] = (wa[7 * 256 : 8 * 256].astype(F32) + xa_in[...].astype(F32)).astype(BF)
    for at in range(4):
        outgoing[at].start()
        staying[at].start()

    for copy in sent + gives + [tell]:
        copy.wait_send()
    for k in range(4):
        for copy in cross(k):
            copy.wait_send()
    for back in range(2):
        for m in range(2):
            mine = 2 * m + core
            for k in range(3):
                to_z(back, m, mine, k).wait_send()
            for k in range(4):
                to_sibling(back, m, mine, k).wait_send()
            keep(back, m).wait()

        @pl.when(section == back)
        def _():
            for m in range(2):
                onward(back, m).wait_send()

        @pl.when(section != back)
        def _():
            for m in range(2):
                pair_sent(back, m)

    for m in range(2):
        to_pair(1, 2 * m + 1 - core).wait_send()
    for at in range(6):
        staying[at].wait()
        outgoing[at].wait_send()
        incoming[at].wait_recv()


def both_layers(rows_in, cotangent, qkv_w, up_w, out_w, down_w, bias_qkv, bias_up, bias_out, bias_down, gain, shift, mine):
    places = np.arange(SLOT, dtype=np.float32)
    frequency = (10000.0 ** (-(np.arange(ROT // 2, dtype=np.float32) * np.float32(2.0 / ROT)))).astype(np.float32)
    angles = (places[:, None] * frequency[None, :]).astype(np.float32).astype(np.float64)
    cosine = np.ones((SLOT, HD), np.float32)
    sine = np.zeros((SLOT, HD), np.float32)
    cosine[:, 0:ROT] = np.tile(np.cos(angles), (1, 2))
    sine[:, 0:ROT] = np.tile(np.sin(angles), (1, 2))
    cosine, sine = (jnp.asarray(np.tile(table, (1, 2))) for table in (cosine, sine))
    any_ = pl.BlockSpec(memory_space=pl.ANY)
    vmem = pl.BlockSpec(memory_space=pltpu.VMEM)
    dma = pltpu.SemaphoreType.DMA
    shape = jax.ShapeDtypeStruct
    return pl.pallas_call(
        layers_kernel,
        out_shape=(
            shape((2, ROWS, D), BF),
            shape((2, ROWS, D), BF),
            shape((3, 128, 2 * MIX), BF),
            shape((128, 2 * UP), BF),
            shape((2 * MIX, 128), BF),
            shape((2 * UP, 128), BF),
            shape((8, D), F32),
            shape((3, 2 * MIX), F32),
            shape((1, 2 * UP), F32),
            shape((2, SLOT, D), BF),
        ),
        in_specs=[any_] * 6 + [vmem] * 9,
        out_specs=[any_] * 6 + [vmem] * 3 + [any_],
        scratch_shapes=[
            pltpu.VMEM((D, A_COLS), BF),
            pltpu.VMEM((B_COLS, D), BF),
            pltpu.VMEM((ALL, D), BF),
            pltpu.VMEM((ALL, D), BF),
            pltpu.VMEM((ALL, QKV), BF),
            pltpu.VMEM((ALL, B_COLS), BF),
            pltpu.VMEM((ALL, UP), BF),
            pltpu.VMEM((4, 4, SLOT, SLOT), BF),
            pltpu.VMEM((ALL, A_COLS), BF),
            pltpu.VMEM((4, SLOT, D), BF),
            pltpu.VMEM((2, SLOT, D), BF),
            pltpu.VMEM((4, 3, ROWS, D), BF),
            pltpu.VMEM((2, ROWS, D), BF),
            pltpu.VMEM((2, ROWS, D), BF),
            pltpu.VMEM((8, 128), F32),
            pltpu.VMEM((8, 128), F32),
            pltpu.VMEM((8, 128), jnp.int32),
            pltpu.VMEM((8, 128), jnp.int32),
            pltpu.VMEM((8, A_COLS), F32),
            pltpu.VMEM((2, 2, 256, A_HALF), BF),
            pltpu.VMEM((2, B_HALF, 256), BF),
            pltpu.VMEM((2, 2, 256, A_COLS), BF),
            pltpu.VMEM((2, B_COLS, 256), BF),
            pltpu.VMEM((256, A_COLS), BF),
            pltpu.VMEM((8, A_COLS), F32),
            pltpu.VMEM((7, 8, D), F32),
            pltpu.VMEM((6, 8, D), F32),
            dma((7,)),
            dma((2, 10)),
            dma((2, 10)),
            dma((2, 2, 9)),
            dma((2, 2, 9)),
            dma((7,)),
            dma((7,)),
            dma((2, 2, 3)),
            dma((2, 2, 3)),
            dma((2, 2, 4)),
            dma((2, 2, 4)),
            dma((2, 2)),
            dma((2, 2)),
            dma((2, 2, 3)),
            dma((2, 2, 3)),
            dma((2, 2)),
            dma((2, 2)),
            dma((5, 2)),
            dma((5, 2)),
            dma((2, 3)),
            dma((2, 3)),
            dma((2, 3)),
            dma((2, 3)),
            dma((6,)),
            dma((6,)),
            dma((6,)),
            dma((6,)),
            dma((6,)),
            dma((2, 2)),
            pltpu.SemaphoreType.REGULAR,
            pltpu.SemaphoreType.REGULAR((2,)),
            dma((2, 2)),
        ],
        compiler_params=pltpu.CompilerParams(
            collective_id=1, has_side_effects=True, vmem_limit_bytes=VMEM_LIMIT
        ),
        name="both_layers",
    )(
        rows_in, cotangent, qkv_w, up_w, out_w, down_w,
        bias_qkv, bias_up, bias_out, bias_down, gain, shift, mine, cosine, sine,
    )


def shards(
    inputs,
    cotangent,
    doc_split,
    qkv_weight,
    qkv_bias,
    out_weight,
    out_bias,
    fc1_weight,
    fc1_bias,
    fc2_weight,
    fc2_bias,
    ln_gain,
    ln_bias,
):
    mine = jnp.broadcast_to(doc_split[None], (4, 2, 128)).reshape(8, 128)
    layer_out, input_grad, grad_qkv, grad_up, grad_out, grad_down, sums, grad_qkv_bias, grad_up_bias, _ = both_layers(
        inputs[:, 0],
        cotangent[:, 0],
        qkv_weight[0].transpose(1, 0, 2),
        fc1_weight[0],
        out_weight[0],
        fc2_weight[0],
        qkv_bias[0],
        fc1_bias,
        out_bias,
        fc2_bias,
        ln_gain,
        ln_bias,
        mine,
    )
    return (
        layer_out[None, :, None],
        input_grad[None, :, None],
        grad_qkv.transpose(1, 0, 2).astype(F32)[None],
        grad_qkv_bias[None],
        grad_out.astype(F32)[None],
        sums[2:3],
        grad_up.astype(F32)[None],
        grad_up_bias,
        grad_down.astype(F32)[None],
        sums[2:3],
        sums[0:1],
        sums[1:2],
    )


def solution(mesh):
    rows = P(None, "dp", "tensor", None)
    placed_weights = (
        P("section", "dp", None, "tensor"),
        P("section", None, "tensor"),
        P("section", "tensor", "dp"),
        P("section", None),
        P("section", "dp", "tensor"),
        P("section", "tensor"),
        P("section", "tensor", "dp"),
        P("section", None),
        P("section", None),
        P("section", None),
    )
    out_rows = P("section", None, "dp", "tensor", None)
    return jax.shard_map(
        shards,
        mesh=mesh,
        in_specs=(rows, rows, P(None, "dp")) + placed_weights,
        out_specs=(out_rows, out_rows) + placed_weights,
        check_vma=False,
    )
```

```python
from functools import partial

import jax
import jax.numpy as jnp
import numpy as np
from jax import lax
from jax.experimental import pallas as pl
from jax.experimental.pallas import tpu as pltpu
from jax.sharding import PartitionSpec as P

HD = 64
ROT = 32
EPSILON = 1e-05
MESH = pl.DeviceIdType.MESH
BF = jnp.bfloat16
F32 = jnp.float32

D = 2048
SLOT = 256
ROWS = 64
PART = ROWS // 2
QKV = 768
UP = 1024
A_COLS = QKV + UP
MIX = 256
B_COLS = MIX + UP
A_HALF = A_COLS // 2
B_HALF = B_COLS // 2
ALL = 4 * SLOT
VMEM_LIMIT = 62 * 2**20


def dot(a, b):
    return lax.dot_general(a, b, (((1,), (0,)), ((), ())), preferred_element_type=F32)


def dot_nt(a, b):
    return lax.dot_general(a, b, (((1,), (1,)), ((), ())), preferred_element_type=F32)


def dot_tn(a, b):
    return lax.dot_general(a, b, (((0,), (0,)), ((), ())), preferred_element_type=F32)


def remote(src, dst, send, recv, device):
    return pltpu.make_async_remote_copy(
        src_ref=src, dst_ref=dst, send_sem=send, recv_sem=recv, device_id=device, device_id_type=MESH
    )


def greet(peers):
    barrier = pltpu.get_barrier_semaphore()
    for peer in peers:
        pl.semaphore_signal(barrier, inc=1, device_id=peer, device_id_type=MESH)
    pl.semaphore_wait(barrier, len(peers))


class Place:
    def __init__(self):
        self.dp = lax.axis_index("dp")
        self.core = lax.rem(self.dp, 2)
        self.x = lax.rem(self.dp // 2, 2)
        self.y = self.dp // 4
        self.z = lax.axis_index("tensor")
        self.sibling = {"dp": self.dp + 1 - 2 * self.core}
        self.across = {"dp": self.at(self.y, 1 - self.x, self.core)}

    def at(self, y, x, core):
        return (y * 2 + x) * 2 + core

    def turn(self, by):
        return lax.rem(self.y + 4 + by, 4)

    def beside(self, by):
        return {"dp": self.at(self.turn(by), self.x, self.core)}

    def z_peer(self, by):
        return {"tensor": lax.rem(self.z + by, 4)}


STAGES = (
    ((0, 512), (512, 512), (1024, 384), (1408, 384)),
    ((0, 384), (384, 384), (768, 256), (1024, 256)),
)


def layers_kernel(
    x_hbm, cot_hbm, qkv_hbm, up_hbm, ow_hbm, dw_hbm,
    qb_ref, ub_ref, ob_ref, db_ref, gain_ref, shift_ref, mine_ref, cos_ref, sin_ref,
    lo_out, ig_out, gq_out, gu_out, go_out, gd_out, sums_ref, gqb_ref, gub_ref, aside_out,
    wa, wb, normed, grads, qkv, hcat, slope, probs, gproj, part, got, zgot, xrow, grow, ctab, stab, split, theirs, bias,
    far_a, half_a, half_b, got_a, got_b, xa_in, sum_a, tally, came,
    own_sem, x_send, x_recv, y_send, y_recv, sib_send, sib_recv,
    agz_s, agz_r, ags_s, ags_r, par_s, par_r, rsz_s, rsz_r, sec_s, sec_r,
    xs, xr, fs, fr, ns, nr, ts, tr, end_s, end_r, end_k, keep_s, free_sem, pair_free, aside_s,
):
    me = Place()
    section = lax.axis_index("section")
    core, z = me.core, me.z
    greet(
        [me.sibling, me.across, me.beside(1), me.beside(-1), me.beside(2)]
        + [me.z_peer(1), me.z_peer(2), me.z_peer(3), {"section": 1 - section}]
    )

    def device_span(dp):
        return pl.ds(pl.multiple_of(dp * 128, 128), 128)

    def chip_span(y_at, x_at):
        return pl.ds(pl.multiple_of((y_at * 2 + x_at) * 256, 256), 256)

    def place(at, size):
        return pl.ds(pl.multiple_of(at * size, size), size)

    def blocks(dp, half):
        span = device_span(dp)
        pairs = [
            (qkv_hbm.at[k, :, place(half, MIX)], wa.at[span, pl.ds(k * MIX, MIX)]) for k in range(3)
        ]
        pairs.append((up_hbm.at[:, place(half, UP)], wa.at[span, pl.ds(QKV, UP)]))
        pairs.append((ow_hbm.at[place(half, MIX), :], wb.at[pl.ds(0, MIX), span]))
        pairs.append((dw_hbm.at[place(half, UP), :], wb.at[pl.ds(MIX, UP), span]))
        return pairs

    other = me.dp + 1 - 2 * core
    holds = [
        pltpu.make_async_copy(source, target, own_sem.at[at])
        for at, (source, target) in enumerate(blocks(me.dp, core))
    ]
    gives = [
        remote(source, target, sib_send.at[at], sib_recv.at[at], me.sibling)
        for at, (source, target) in enumerate(blocks(me.dp, 1 - core))
    ]
    takes = [
        remote(source, target, sib_send.at[at], sib_recv.at[at], me.sibling)
        for at, (source, target) in enumerate(blocks(other, 1 - core))
    ]
    tell = remote(mine_ref, theirs, sib_send.at[6], sib_recv.at[6], me.sibling)
    rows_in = [
        pltpu.make_async_copy(x_hbm, xrow, own_sem.at[6]),
        pltpu.make_async_copy(cot_hbm, grow, own_sem.at[6]),
    ]
    y, x = me.y, me.x
    far = me.turn(2)

    def piece_of(stage, y_at, x_at, which):
        span = pl.ds(*STAGES[stage][which])
        if stage == 0:
            return wa.at[chip_span(y_at, x_at), span]
        return wb.at[span, chip_span(y_at, x_at)]

    def over_x(stage, y_at, x_at, which, slot):
        piece = piece_of(stage, y_at, x_at, which)
        return remote(piece, piece, x_send.at[stage, slot], x_recv.at[stage, slot], me.across)

    def over_y(stage, by, y_at, x_at, which, slot):
        piece = piece_of(stage, y_at, x_at, which)
        way = 0 if by > 0 else 1
        return remote(piece, piece, y_send.at[stage, way, slot], y_recv.at[stage, way, slot], me.beside(by))

    sent = []

    def start(copy):
        copy.start()
        sent.append(copy)

    def own_first(stage):
        for which in (0, 1):
            start(over_x(stage, y, x, which, which))
        for which in (2, 3):
            for by in (1, -1):
                start(over_y(stage, by, y, x, which, which))

    def own_second(stage):
        for which in (2, 3):
            start(over_x(stage, y, x, which, which))
        for which in (0, 1):
            for by in (1, -1):
                start(over_y(stage, by, y, x, which, which))

    def pass_near(stage):
        for which in (2, 3):
            for by in (1, -1):
                source = me.turn(-by)
                over_y(stage, by, source, x, which, which).wait_recv()
                if (which == 2) == (by > 0):
                    start(over_y(stage, by, source, x, which, 6))
                start(over_x(stage, source, x, which, 2 * which + (0 if by > 0 else 1)))

    def pass_crossed(stage):
        for which in (0, 1):
            over_x(stage, y, 1 - x, which, which).wait_recv()
            for by in (1, -1):
                start(over_y(stage, by, y, 1 - x, which, 4 + which))

    def pass_far(stage):
        for which, by in ((2, 1), (3, -1)):
            over_y(stage, by, far, x, which, 6).wait_recv()
            start(over_x(stage, far, x, which, 6 + which))

    def pass_on(stage):
        for which, by in ((0, 1), (1, -1)):
            source = me.turn(-by)
            over_y(stage, by, source, x, which, which).wait_recv()
            start(over_y(stage, by, source, x, which, 7))

    def pass_on_crossed(stage):
        for which, by in ((0, 1), (1, -1)):
            source = me.turn(-by)
            over_y(stage, by, source, 1 - x, which, 4 + which).wait_recv()
            start(over_y(stage, by, source, 1 - x, which, 8))

    def settle(stage):
        for which, by in ((0, -1), (1, 1)):
            source = me.turn(-by)
            over_y(stage, by, source, x, which, which).wait_recv()
            over_y(stage, by, source, 1 - x, which, 4 + which).wait_recv()
        for which in (2, 3):
            over_x(stage, y, 1 - x, which, which).wait_recv()
            for by in (1, -1):
                over_x(stage, me.turn(-by), 1 - x, which, 2 * which + (0 if by > 0 else 1)).wait_recv()
            over_x(stage, far, 1 - x, which, 6 + which).wait_recv()
        for which, by in ((0, 1), (1, -1)):
            over_y(stage, by, far, x, which, 7).wait_recv()
            over_y(stage, by, far, 1 - x, which, 8).wait_recv()

    def band(at, h):
        return pl.ds(pl.multiple_of(at * ROWS + h * PART, PART), PART)

    def slot(i):
        return pl.ds(pl.multiple_of(i * SLOT, SLOT), SLOT)

    def slot_band(i, at, h):
        return pl.ds(pl.multiple_of(i * SLOT + at * ROWS + h * PART, PART), PART)

    halves = (slice(0, PART), slice(PART, ROWS))

    def standard(rows):
        average = jnp.mean(rows, axis=-1, keepdims=True)
        centred = rows - average
        variance = jnp.mean(centred * centred, axis=-1, keepdims=True)
        scale = lax.rsqrt(variance + EPSILON)
        return centred * scale, scale

    def spread_buffer(back):
        return grads if back else normed

    def to_z(back, m, i, k, h):
        piece = spread_buffer(back).at[slot_band(i, z, h)]
        at = 2 * k + h
        return remote(piece, piece, agz_s.at[back, m, at], agz_r.at[back, m, at], me.z_peer(1 + k))

    def from_z(back, m, i, k, h):
        piece = spread_buffer(back).at[slot_band(i, lax.rem(z + 3 - k, 4), h)]
        at = 2 * k + h
        return remote(piece, piece, agz_s.at[back, m, at], agz_r.at[back, m, at], me.z_peer(3 - k))

    def to_sibling(back, m, i, k, h):
        piece = spread_buffer(back).at[slot_band(i, lax.rem(z + 3 - k, 4), h)]
        at = 2 * k + h
        return remote(piece, piece, ags_s.at[back, m, at], ags_r.at[back, m, at], me.sibling)

    def spread_own(back, m, wait):
        i = 2 * m + core
        for h in range(2):
            if wait:
                onward(1 if back else 0, m, h).wait_recv()
            if back:
                grads[slot_band(i, z, h)] = grow[m, halves[h]]
            else:
                xhat, _ = standard(xrow[m, halves[h]].astype(F32))
                normed[slot_band(i, z, h)] = (xhat * gain_ref[...] + shift_ref[...]).astype(BF)
            for k in range(3):
                to_z(back, m, i, k, h).start()
            to_sibling(back, m, i, 3, h).start()

    def relay(back, i):
        m = i // 2
        for h in range(2):
            for k in range(3):
                from_z(back, m, i, k, h).wait_recv()
                to_sibling(back, m, i, k, h).start()

    def await_rows(back, i):
        m = i // 2

        @pl.when(lax.rem(i, 2) != core)
        def _():
            for h in range(2):
                for k in range(4):
                    to_sibling(back, m, i, k, h).wait_recv()

    def part_at(i):
        return (1 - lax.rem(i + core, 2)) * (i // 2) + lax.rem(i + core, 2) * (2 + i // 2)

    def to_pair(back, i, q):
        m = i // 2
        span = pl.ds(q * (D // 2), D // 2)
        return remote(
            part.at[2 + m, :, span], got.at[m, :, span], par_s.at[back, m, q], par_r.at[back, m, q], me.sibling
        )

    def sum_to_z(back, m, k, h):
        peer = me.z_peer(1 + k)
        at = 2 * k + h
        return remote(
            part.at[m, band(peer["tensor"], h)],
            zgot.at[back * 2 + m, k, pl.ds(h * PART, PART)],
            rsz_s.at[back, m, at],
            rsz_r.at[back, m, at],
            peer,
        )

    def pair_add(back, m):
        for q in range(2):
            span = slice(q * (D // 2), (q + 1) * (D // 2))
            to_pair(back, 2 * m + core, q).wait_recv()
            part[m, :, span] = (part[m, :, span].astype(F32) + got[m, :, span].astype(F32)).astype(BF)
        if back == 0:
            pl.semaphore_signal(pair_free.at[m], inc=1, device_id=me.sibling, device_id_type=MESH)

    def pair_spread(back, m):
        for h in range(2):
            for k in range(3):
                sum_to_z(back, m, k, h).start()

    def pair_sum(back, m):
        pair_add(back, m)
        pair_spread(back, m)

    def pair_sent(back, m):
        for h in range(2):
            for k in range(3):
                sum_to_z(back, m, k, h).wait_send()

    def aside(m):
        return pltpu.make_async_copy(part.at[m], aside_out.at[m], aside_s.at[0, m])

    def back_again(m):
        return pltpu.make_async_copy(aside_out.at[m], part.at[m], aside_s.at[1, m])

    def row_sum(back, m, h):
        total = part[m, band(z, h)].astype(F32)
        for k in range(3):
            sum_to_z(back, m, k, h).wait_recv()
            total = total + zgot[back * 2 + m, k, halves[h]].astype(F32)
        return total

    def onward(back, m, h):
        target = grow if back else xrow
        span = pl.ds(h * PART, PART)
        return remote(
            zgot.at[back * 2 + m, 0, span],
            target.at[m, span],
            sec_s.at[back, m, h],
            sec_r.at[back, m, h],
            {"section": 1 - back},
        )

    def keep(back, m):
        target = ig_out if back else lo_out
        return pltpu.make_async_copy(zgot.at[back * 2 + m, 0], target.at[m], keep_s.at[back, m])

    def finish_forward(m):
        for h in range(2):
            total = row_sum(0, m, h) + (ob_ref[...] + db_ref[...])
            zgot[m, 0, halves[h]] = (xrow[m, halves[h]].astype(F32) + total).astype(BF)

            @pl.when(section == 0)
            def _():
                onward(0, m, h).start()

        keep(0, m).start()

    def finish_backward(m):
        for h in range(2):
            grad = row_sum(1, m, h)
            xhat, scale = standard(xrow[m, halves[h]].astype(F32))
            above = grow[m, halves[h]].astype(F32)
            a = grad * gain_ref[...]
            inner = a - jnp.mean(a, axis=-1, keepdims=True) - xhat * jnp.mean(a * xhat, axis=-1, keepdims=True)
            zgot[2 + m, 0, halves[h]] = (above + inner * scale).astype(BF)

            @pl.when(section == 1)
            def _():
                onward(1, m, h).start()

            tally[0, 0:1, :] += jnp.sum(grad * xhat, axis=0, keepdims=True)
            tally[0, 1:2, :] += jnp.sum(grad, axis=0, keepdims=True)
            tally[0, 2:3, :] += jnp.sum(above, axis=0, keepdims=True)

        keep(1, m).start()

    lanes = lax.broadcasted_iota(jnp.int32, (SLOT, 128), 1) % HD
    early = lanes < ROT // 2

    places = lax.broadcasted_iota(jnp.int32, (SLOT, 128), 0)

    def tables(i):
        first = places < split[pl.ds(i, 1), :]
        cosine, sine = cos_ref[...], sin_ref[...]
        cos_at, sin_at = ctab[pl.ds(i, 1), :], stab[pl.ds(i, 1), :]
        return (
            jnp.where(first, cosine, cosine * cos_at + sine * sin_at),
            jnp.where(first, sine, sine * cos_at - cosine * sin_at) * jnp.where(early, -1.0, 1.0),
        )

    def turned(values, table, sign):
        halves = []
        for at in (0, 128):
            piece = values[:, at : at + 128]
            swapped = jnp.where(early, pltpu.roll(piece, 128 - ROT // 2, 1), pltpu.roll(piece, ROT // 2, 1))
            halves.append(piece * table[0] + swapped * (table[1] * sign))
        return jnp.concatenate(halves, axis=1)

    def head_mask(head):
        lane = lax.broadcasted_iota(jnp.int32, (1, MIX), 1)
        return jnp.where(lane // HD == head, 1.0, 0.0).astype(BF)

    def forward_first(i):
        rows = normed[slot(i)]
        projected = dot(rows, wa[:, 0:QKV]) + bias[0:1, 0:QKV]
        table = tables(i)
        queries = turned(projected[:, 0:MIX], table, 1.0).astype(BF)
        keys = turned(projected[:, MIX : 2 * MIX], table, 1.0).astype(BF)
        values = projected[:, 2 * MIX : 3 * MIX].astype(BF)
        qkv[slot(i), 0:MIX] = queries
        qkv[slot(i), MIX : 2 * MIX] = keys
        qkv[slot(i), 2 * MIX : 3 * MIX] = values
        at = split[pl.ds(i, 1), :]
        at = jnp.concatenate([at, at], axis=1)
        row_at = lax.broadcasted_iota(jnp.int32, (SLOT, SLOT), 0)
        key_at = lax.broadcasted_iota(jnp.int32, (SLOT, SLOT), 1)
        same = jnp.where(row_at < at, 1, 0) == jnp.where(key_at < at, 1, 0)
        allowed = (key_at <= row_at) & same
        mixed = jnp.zeros((SLOT, MIX), F32)
        for head in range(4):
            mask = head_mask(head)
            scores = jnp.where(allowed, dot_nt(queries * mask, keys) * HD**-0.5, -1e30)
            weights = jnp.exp(scores - jnp.max(scores, axis=-1, keepdims=True))
            chances = (weights / jnp.sum(weights, axis=-1, keepdims=True)).astype(BF)
            probs[i, head] = chances
            mixed = mixed + dot(chances, values * mask)
        hcat[slot(i), 0:MIX] = mixed.astype(BF)
        v = dot(rows, wa[:, QKV:A_COLS]) + bias[0:1, QKV:A_COLS]
        root = np.sqrt(2 / np.pi).astype(np.float32)
        square = v * v
        bent = jnp.tanh(root * (v + 0.044715 * (square * v)))
        half = 0.5 * (1.0 + bent)
        hcat[slot(i), MIX:B_COLS] = (v * half).astype(BF)
        slope[slot(i)] = (half + 0.5 * v * (1.0 - bent * bent) * (root * (1.0 + 3 * 0.044715 * square))).astype(BF)

    def forward_second(i):
        for q in range(2):
            span = slice(q * (D // 2), (q + 1) * (D // 2))
            part[part_at(i), :, span] = dot(hcat[slot(i)], wb[:, span]).astype(BF)

            @pl.when(lax.rem(i, 2) != core)
            def _():
                to_pair(0, i, q).start()

    def backward_first(i):
        grad_hidden = dot_nt(grads[slot(i)], wb[...])
        grad_pre = (grad_hidden[:, MIX:B_COLS] * slope[slot(i)].astype(F32)).astype(BF)
        gproj[slot(i), QKV:A_COLS] = grad_pre
        sum_a[0:1, QKV:A_COLS] += jnp.sum(grad_pre.astype(F32), axis=0, keepdims=True)
        grad_mixed = grad_hidden[:, 0:MIX].astype(BF)
        queries = qkv[slot(i), 0:MIX]
        keys = qkv[slot(i), MIX : 2 * MIX]
        values = qkv[slot(i), 2 * MIX : 3 * MIX]
        zero = jnp.zeros((SLOT, MIX), F32)
        grad_queries, grad_keys, grad_values = zero, zero, zero
        for head in range(4):
            mask = head_mask(head)
            chances = probs[i, head]
            masked = grad_mixed * mask
            grad_values = grad_values + dot_tn(chances, masked)
            grad_probs = dot_nt(masked, values)
            wide = chances.astype(F32)
            centre = jnp.sum(wide * grad_probs, axis=-1, keepdims=True)
            grad_scores = (wide * (grad_probs - centre)).astype(BF)
            grad_queries = grad_queries + dot(grad_scores, keys * mask)
            grad_keys = grad_keys + dot_tn(grad_scores, queries * mask)
        table = tables(i)
        pieces = (
            turned(grad_queries * HD**-0.5, table, -1.0).astype(BF),
            turned(grad_keys * HD**-0.5, table, -1.0).astype(BF),
            grad_values.astype(BF),
        )
        for at, piece in enumerate(pieces):
            span = slice(at * MIX, (at + 1) * MIX)
            gproj[slot(i), span] = piece
            sum_a[0:1, span] += jnp.sum(piece.astype(F32), axis=0, keepdims=True)

    def backward_second(i):
        other_slot = lax.rem(i, 2) != core

        @pl.when(other_slot)
        def _():
            pl.semaphore_wait(pair_free.at[i // 2], 1)
            for q in range(2):
                to_pair(0, i, q).wait_send()

        for q in range(2):
            span = slice(q * (D // 2), (q + 1) * (D // 2))
            part[part_at(i), :, span] = dot_nt(gproj[slot(i)], wa[span, :]).astype(BF)

            @pl.when(other_slot)
            def _():
                to_pair(1, i, q).start()

    for copy in holds + gives:
        copy.start()
    tell.start()

    @pl.when(section == 0)
    def _():
        rows_in[0].start()

    @pl.when(section == 1)
    def _():
        rows_in[1].start()

    sum_a[...] = jnp.zeros_like(sum_a)
    tally[0] = jnp.zeros((8, D), F32)
    for at in range(4):
        holds[at].wait()
        takes[at].wait_recv()
    own_first(0)
    own_second(0)

    @pl.when(section == 0)
    def _():
        rows_in[0].wait()
        for m in range(2):
            spread_own(0, m, False)

    @pl.when(section == 1)
    def _():
        rows_in[1].wait()
        for m in range(2):
            spread_own(1, m, False)

    for at in (4, 5):
        holds[at].wait()
        takes[at].wait_recv()
    for at in range(3):
        bias[0:1, at * MIX : (at + 1) * MIX] = jnp.where(
            core == 0, qb_ref[at : at + 1, 0:MIX], qb_ref[at : at + 1, MIX : 2 * MIX]
        )
    bias[0:1, QKV:A_COLS] = jnp.where(core == 0, ub_ref[0:1, 0:UP], ub_ref[0:1, UP : 2 * UP])
    tell.wait_recv()
    for i in range(4):
        at = jnp.where(core == i % 2, mine_ref[i // 2 : i // 2 + 1, :], theirs[i // 2 : i // 2 + 1, :])
        split[i : i + 1, :] = at
        here = places == at
        ctab[i : i + 1, :] = jnp.sum(jnp.where(here, cos_ref[...], 0.0), axis=0, keepdims=True)
        stab[i : i + 1, :] = jnp.sum(jnp.where(here, sin_ref[...], 0.0), axis=0, keepdims=True)

    pass_near(0)
    pass_crossed(0)

    def relay_early(m):
        @pl.when(section == 0)
        def _():
            relay(0, 2 * m + core)

        @pl.when(section == 1)
        def _():
            relay(1, 2 * m + core)

    relay_early(0)
    pass_on(0)
    own_first(1)
    pass_far(0)
    relay_early(1)
    pass_on_crossed(0)
    own_second(1)
    settle(0)
    pass_near(1)

    def forward_early(i):
        @pl.when(section == 0)
        def _():
            await_rows(0, i)
            forward_first(i)

    forward_early(0)
    pass_crossed(1)
    forward_early(1)
    pass_on(1)
    pass_far(1)
    forward_early(2)
    forward_early(3)
    pass_on_crossed(1)
    settle(1)

    def finish_forward_all():
        for m in range(2):
            finish_forward(m)

    @pl.when(section == 0)
    def _():
        def step(i, _):
            forward_second(i)

            @pl.when(i == 1 + core)
            def _():
                pair_sum(0, 0)

            return 0

        lax.fori_loop(0, 4, step, 0)
        pair_sum(0, 1)
        finish_forward_all()

        @pl.when(core == 0)
        def _():
            spread_own(1, 0, True)
            relay(1, 0)

    @pl.when(section == 1)
    def _():
        spread_own(0, 0, True)

        @pl.when(core == 0)
        def _():
            relay(0, 0)

        def step(i, _):
            await_rows(0, i)
            forward_first(i)

            @pl.when((i == 0) & (core == 0))
            def _():
                spread_own(0, 1, True)

            @pl.when((i < 3) & (lax.rem(i, 2) != core))
            def _():
                relay(0, i + 1)

            @pl.when((i > 0) & (lax.rem(i, 2) != core))
            def _():
                pair_add(0, (i - 1) // 2)
                aside((i - 1) // 2).start()

            forward_second(i)

            @pl.when((i == 0) & (core == 1))
            def _():
                spread_own(0, 1, True)

            return 0

        lax.fori_loop(0, 4, step, 0)

    def turn_of(k):
        return lax.rem(y + 2 - k + 4, 4)

    a_cuts = ((0, A_HALF), (A_HALF, A_COLS))
    b_cuts = ((0, B_HALF), (B_HALF, B_COLS))

    def term_a(y_at, x_at, half):
        lo, hi = a_cuts[half]
        return dot_tn(normed[:, chip_span(y_at, x_at)], gproj[:, lo:hi])

    def term_b(y_at, x_at, half):
        lo, hi = b_cuts[half]
        return dot_tn(hcat[:, lo:hi], grads[:, chip_span(y_at, x_at)])

    def cross(k):
        span = pl.ds(pl.multiple_of(k * MIX, MIX), MIX)
        there = pl.ds(pl.multiple_of((4 + k) * 256, 256), 256)
        return (
            remote(probs.at[k, 0], wb.at[pl.ds(0, MIX), there], xs.at[k, 0], xr.at[k, 0], me.across),
            remote(slope.at[:, span], wb.at[pl.ds(MIX, UP), there], xs.at[k, 1], xr.at[k, 1], me.across),
        )

    def cross_all():
        pl.semaphore_wait(free_sem, 1)

        def step(k, _):
            span = pl.ds(pl.multiple_of(k * MIX, MIX), MIX)
            total = term_b(turn_of(k), 1 - x, 0).astype(BF)
            probs[k, 0] = total[0:MIX]
            slope[0 : B_HALF - MIX, span] = total[MIX:B_HALF]
            slope[B_HALF - MIX : UP, span] = term_b(turn_of(k), 1 - x, 1).astype(BF)
            for copy in cross(k):
                copy.start()
            return 0

        lax.fori_loop(0, 4, step, 0)

    def crossed(k):
        for copy in cross(k):
            copy.wait_recv()

    def from_across(k, half):
        lo, hi = b_cuts[half]
        return wb[lo:hi, (4 + k) * 256 : (5 + k) * 256].astype(F32)

    def a_place(at):
        return wa.at[pl.ds(pl.multiple_of(at * 256, 256), 256)]

    def b_place(at):
        return wb.at[:, pl.ds(at * 256, 256)]

    a_spans = (pl.ds(0, A_HALF), pl.ds(A_HALF, A_HALF))
    b_spans = (pl.ds(0, B_HALF), pl.ds(B_HALF, B_HALF))

    def far_piece(way, x_at):
        source = far_a.at[x_at, :, a_spans[way]]
        return remote(source, half_a.at[way, x_at], fs.at[way, x_at], fr.at[way, x_at], me.beside(1 - 2 * way))

    def far_piece_b(way):
        source = wb.at[b_spans[way], pl.ds(0, 256)]
        return remote(source, half_b.at[way], fs.at[way, 2], fr.at[way, 2], me.beside(1 - 2 * way))

    def near_piece(way, x_at):
        source = a_place(2 + 2 * way + x_at)
        return remote(source, got_a.at[way, x_at], ns.at[way, x_at], nr.at[way, x_at], me.beside(1 - 2 * way))

    def near_piece_b(way):
        return remote(b_place(1 + way), got_b.at[way], ns.at[way, 2], nr.at[way, 2], me.beside(1 - 2 * way))

    def cross_last():
        return remote(a_place(6), xa_in, xs.at[4, 0], xr.at[4, 0], me.across)

    def send_far_all():
        def step(k, _):
            x_at = (1 - k) * (1 - x) + k * x
            for way, (lo, hi) in enumerate(a_cuts):
                far_a[x_at, :, lo:hi] = term_a(far, x_at, way).astype(BF)
                far_piece(way, x_at).start()
            return 0

        lax.fori_loop(0, 2, step, 0)

    def send_near(way, x_at):
        target = pl.ds(pl.multiple_of((2 + 2 * way + x_at) * 256, 256), 256)
        for half in (1 - way, way):
            lo, hi = a_cuts[half]
            total = term_a(me.turn(1 - 2 * way), x_at, half)
            if half == way:
                far_piece(way, x_at).wait_recv()
                total = total + half_a[way, x_at].astype(F32)
            wa[target, lo:hi] = total.astype(BF)
        start(near_piece(way, x_at))

    def send_far_b():
        crossed(0)
        for way, (lo, hi) in enumerate(b_cuts):
            wb[lo:hi, 0:256] = (term_b(far, x, way) + from_across(0, way)).astype(BF)
            start(far_piece_b(way))

    def send_near_b(way):
        crossed(1 + 2 * way)
        span = slice((1 + way) * 256, (2 + way) * 256)
        for half in (1 - way, way):
            lo, hi = b_cuts[half]
            total = term_b(me.turn(1 - 2 * way), x, half) + from_across(1 + 2 * way, half)
            if half == way:
                far_piece_b(way).wait_recv()
                total = total + half_b[way].astype(F32)
            wb[lo:hi, span] = total.astype(BF)
        start(near_piece_b(way))

    def arrived_a(x_at, at):
        for half, (lo, hi) in enumerate(a_cuts):
            total = term_a(y, x_at, half)
            for way in (0, 1):
                if half == 0:
                    near_piece(way, x_at).wait_recv()
                total = total + got_a[way, x_at, :, lo:hi].astype(F32)
            wa[at * 256 : (at + 1) * 256, lo:hi] = total.astype(BF)

    def arrived_b(at):
        crossed(2)
        for half, (lo, hi) in enumerate(b_cuts):
            total = term_b(y, x, half) + from_across(2, half)
            for way in (0, 1):
                if half == 0:
                    near_piece_b(way).wait_recv()
                total = total + got_b[way, lo:hi].astype(F32)
            wb[lo:hi, at * 256 : (at + 1) * 256] = total.astype(BF)

    near_z = {"tensor": z + 1 - 2 * lax.rem(z, 2)}
    near_y = {"dp": me.at(y + 1 - 2 * lax.rem(y, 2), x, core)}
    partners = (me.across, near_y, me.beside(2), near_z, me.z_peer(2), me.sibling)

    def exchange(step):
        return remote(tally.at[step], came.at[step], ts.at[step], tr.at[step], partners[step])

    def fold(step):
        exchange(step).wait_recv()
        total = tally[step] + came[step]
        if step < 3:
            tally[step + 1] = total
        else:
            tally[step + 1, 0:3] = total[0:3]
            tally[step + 1, 3:8] = tally[step, 3:8]
        if step < 5:
            start(exchange(step + 1))

    for copy in sent:
        copy.wait_send()
    sent.clear()

    def backward_step(i, _):
        own = lax.rem(i, 2) == core

        @pl.when((section == 0) & (i < 3) & jnp.logical_not(own))
        def _():
            spread_own(1, (i + 1) // 2, True)

        await_rows(1, i)
        backward_first(i)

        @pl.when((section == 0) & (i < 3) & jnp.logical_not(own))
        def _():
            relay(1, i + 1)

        @pl.when(i == 3)
        def _():
            pl.semaphore_signal(free_sem, inc=1, device_id=me.across, device_id_type=MESH)

        @pl.when((section == 0) & (i == 3))
        def _():
            send_far_all()
            cross_all()

        @pl.when((i >= 1) & jnp.logical_not(own))
        def _():
            pair_sum(1, (i - 1) // 2)

        @pl.when((i >= 2) & own)
        def _():
            finish_backward(0)

        @pl.when((section == 1) & (core == 1) & (i == 0))
        def _():
            pair_add(0, 1)
            aside(1).start()

        @pl.when((section == 0) & own)
        def _():
            pair_sent(0, i // 2)

        @pl.when((section == 1) & own)
        def _():
            aside(i // 2).wait()

        backward_second(i)
        return 0

    lax.fori_loop(0, 4, backward_step, 0)

    @pl.when(section == 1)
    def _():
        @pl.when(core == 1)
        def _():
            pair_sum(1, 1)

        finish_backward(1)
        send_far_all()
        cross_all()

    @pl.when((section == 0) & (core == 1))
    def _():
        pair_sum(1, 1)

    @pl.when(section == 1)
    def _():
        for m in range(2):
            pair_sent(1, m)
            back_again(m).start()

    send_far_b()

    @pl.when(section == 1)
    def _():
        for m in range(2):
            back_again(m).wait()
            pair_spread(0, m)

    for way in (0, 1):
        send_near(way, 1 - x)

    @pl.when(section == 0)
    def _():
        finish_backward(1)

    tally[0, 3:4, 0:A_COLS] = sum_a[0:1]
    start(exchange(0))
    for way in (0, 1):
        send_near(way, x)
    fold(0)
    for way in (0, 1):
        send_near_b(way)
    fold(1)

    @pl.when(section == 1)
    def _():
        finish_forward_all()

    arrived_a(1 - x, 6)
    start(cross_last())
    fold(2)
    arrived_b(3)
    fold(3)

    def result(half, peer, at):
        rows = pl.ds(pl.multiple_of(7 * 256 + half * 128, 128), 128)
        cols = pl.ds(pl.multiple_of(3 * 256 + half * 128, 128), 128)
        sources = [wa.at[rows, pl.ds(k * MIX, MIX)] for k in range(3)]
        sources += [wa.at[rows, pl.ds(QKV, UP)], wb.at[pl.ds(0, MIX), cols], wb.at[pl.ds(MIX, UP), cols]]
        targets = [gq_out.at[k, :, place(at, MIX)] for k in range(3)]
        targets += [gu_out.at[:, place(at, UP)], go_out.at[place(at, MIX), :], gd_out.at[place(at, UP), :]]
        if peer:
            return [
                remote(source, target, end_s.at[k], end_r.at[k], me.sibling)
                for k, (source, target) in enumerate(zip(sources, targets))
            ]
        return [
            pltpu.make_async_copy(source, target, end_k.at[k])
            for k, (source, target) in enumerate(zip(sources, targets))
        ]

    outgoing, staying = result(1 - core, True, core), result(core, False, core)
    incoming = result(1 - core, True, 1 - core)
    for at in (4, 5):
        outgoing[at].start()
        staying[at].start()
    fold(4)
    arrived_a(x, 7)
    fold(5)
    sums_ref[...] = tally[6]
    for at in range(3):
        span = slice(at * MIX, (at + 1) * MIX)
        ours, others = tally[6, 3:4, span], came[5, 3:4, span]
        gqb_ref[at : at + 1, 0:MIX] = jnp.where(core == 0, ours, others)
        gqb_ref[at : at + 1, MIX : 2 * MIX] = jnp.where(core == 0, others, ours)
    ours, others = tally[6, 3:4, QKV:A_COLS], came[5, 3:4, QKV:A_COLS]
    gub_ref[0:1, 0:UP] = jnp.where(core == 0, ours, others)
    gub_ref[0:1, UP : 2 * UP] = jnp.where(core == 0, others, ours)
    cross_last().wait_recv()
    wa[7 * 256 : 8 * 256] = (wa[7 * 256 : 8 * 256].astype(F32) + xa_in[...].astype(F32)).astype(BF)
    for at in range(4):
        outgoing[at].start()
        staying[at].start()

    for copy in sent + gives + [tell]:
        copy.wait_send()
    for k in range(4):
        for copy in cross(k):
            copy.wait_send()
    for way in range(2):
        for x_at in range(2):
            far_piece(way, x_at).wait_send()
    for back in range(2):
        for m in range(2):
            mine = 2 * m + core
            for h in range(2):
                for k in range(3):
                    to_z(back, m, mine, k, h).wait_send()
                for k in range(4):
                    to_sibling(back, m, mine, k, h).wait_send()
            keep(back, m).wait()

        @pl.when(section == back)
        def _():
            for m in range(2):
                for h in range(2):
                    onward(back, m, h).wait_send()

        @pl.when(section != back)
        def _():
            for m in range(2):
                pair_sent(back, m)

    for m in range(2):
        for q in range(2):
            to_pair(1, 2 * m + 1 - core, q).wait_send()
    for at in range(6):
        staying[at].wait()
        outgoing[at].wait_send()
        incoming[at].wait_recv()


def both_layers(rows_in, cotangent, qkv_w, up_w, out_w, down_w, bias_qkv, bias_up, bias_out, bias_down, gain, shift, mine):
    places = np.arange(SLOT, dtype=np.float32)
    frequency = (10000.0 ** (-(np.arange(ROT // 2, dtype=np.float32) * np.float32(2.0 / ROT)))).astype(np.float32)
    angles = (places[:, None] * frequency[None, :]).astype(np.float32).astype(np.float64)
    cosine = np.ones((SLOT, HD), np.float32)
    sine = np.zeros((SLOT, HD), np.float32)
    cosine[:, 0:ROT] = np.tile(np.cos(angles), (1, 2))
    sine[:, 0:ROT] = np.tile(np.sin(angles), (1, 2))
    cosine, sine = (jnp.asarray(np.tile(table, (1, 2))) for table in (cosine, sine))
    any_ = pl.BlockSpec(memory_space=pl.ANY)
    vmem = pl.BlockSpec(memory_space=pltpu.VMEM)
    dma = pltpu.SemaphoreType.DMA
    shape = jax.ShapeDtypeStruct
    return pl.pallas_call(
        layers_kernel,
        out_shape=(
            shape((2, ROWS, D), BF),
            shape((2, ROWS, D), BF),
            shape((3, 128, 2 * MIX), BF),
            shape((128, 2 * UP), BF),
            shape((2 * MIX, 128), BF),
            shape((2 * UP, 128), BF),
            shape((8, D), F32),
            shape((3, 2 * MIX), F32),
            shape((1, 2 * UP), F32),
            shape((2, SLOT, D), BF),
        ),
        in_specs=[any_] * 6 + [vmem] * 9,
        out_specs=[any_] * 6 + [vmem] * 3 + [any_],
        scratch_shapes=[
            pltpu.VMEM((D, A_COLS), BF),
            pltpu.VMEM((B_COLS, D), BF),
            pltpu.VMEM((ALL, D), BF),
            pltpu.VMEM((ALL, D), BF),
            pltpu.VMEM((ALL, QKV), BF),
            pltpu.VMEM((ALL, B_COLS), BF),
            pltpu.VMEM((ALL, UP), BF),
            pltpu.VMEM((4, 4, SLOT, SLOT), BF),
            pltpu.VMEM((ALL, A_COLS), BF),
            pltpu.VMEM((4, SLOT, D), BF),
            pltpu.VMEM((2, SLOT, D), BF),
            pltpu.VMEM((4, 3, ROWS, D), BF),
            pltpu.VMEM((2, ROWS, D), BF),
            pltpu.VMEM((2, ROWS, D), BF),
            pltpu.VMEM((8, 128), F32),
            pltpu.VMEM((8, 128), F32),
            pltpu.VMEM((8, 128), jnp.int32),
            pltpu.VMEM((8, 128), jnp.int32),
            pltpu.VMEM((8, A_COLS), F32),
            pltpu.VMEM((2, 256, A_COLS), BF),
            pltpu.VMEM((2, 2, 256, A_HALF), BF),
            pltpu.VMEM((2, B_HALF, 256), BF),
            pltpu.VMEM((2, 2, 256, A_COLS), BF),
            pltpu.VMEM((2, B_COLS, 256), BF),
            pltpu.VMEM((256, A_COLS), BF),
            pltpu.VMEM((8, A_COLS), F32),
            pltpu.VMEM((7, 8, D), F32),
            pltpu.VMEM((6, 8, D), F32),
            dma((7,)),
            dma((2, 10)),
            dma((2, 10)),
            dma((2, 2, 9)),
            dma((2, 2, 9)),
            dma((7,)),
            dma((7,)),
            dma((2, 2, 6)),
            dma((2, 2, 6)),
            dma((2, 2, 8)),
            dma((2, 2, 8)),
            dma((2, 2, 2)),
            dma((2, 2, 2)),
            dma((2, 2, 6)),
            dma((2, 2, 6)),
            dma((2, 2, 2)),
            dma((2, 2, 2)),
            dma((5, 2)),
            dma((5, 2)),
            dma((2, 3)),
            dma((2, 3)),
            dma((2, 3)),
            dma((2, 3)),
            dma((6,)),
            dma((6,)),
            dma((6,)),
            dma((6,)),
            dma((6,)),
            dma((2, 2)),
            pltpu.SemaphoreType.REGULAR,
            pltpu.SemaphoreType.REGULAR((2,)),
            dma((2, 2)),
        ],
        compiler_params=pltpu.CompilerParams(
            collective_id=1, has_side_effects=True, vmem_limit_bytes=VMEM_LIMIT
        ),
        name="both_layers",
    )(
        rows_in, cotangent, qkv_w, up_w, out_w, down_w,
        bias_qkv, bias_up, bias_out, bias_down, gain, shift, mine, cosine, sine,
    )


def shards(
    inputs,
    cotangent,
    doc_split,
    qkv_weight,
    qkv_bias,
    out_weight,
    out_bias,
    fc1_weight,
    fc1_bias,
    fc2_weight,
    fc2_bias,
    ln_gain,
    ln_bias,
):
    mine = jnp.broadcast_to(doc_split[None], (4, 2, 128)).reshape(8, 128)
    layer_out, input_grad, grad_qkv, grad_up, grad_out, grad_down, sums, grad_qkv_bias, grad_up_bias, _ = both_layers(
        inputs[:, 0],
        cotangent[:, 0],
        qkv_weight[0].transpose(1, 0, 2),
        fc1_weight[0],
        out_weight[0],
        fc2_weight[0],
        qkv_bias[0],
        fc1_bias,
        out_bias,
        fc2_bias,
        ln_gain,
        ln_bias,
        mine,
    )
    return (
        layer_out[None, :, None],
        input_grad[None, :, None],
        grad_qkv.transpose(1, 0, 2).astype(F32)[None],
        grad_qkv_bias[None],
        grad_out.astype(F32)[None],
        sums[2:3],
        grad_up.astype(F32)[None],
        grad_up_bias,
        grad_down.astype(F32)[None],
        sums[2:3],
        sums[0:1],
        sums[1:2],
    )


def solution(mesh):
    rows = P(None, "dp", "tensor", None)
    placed_weights = (
        P("section", "dp", None, "tensor"),
        P("section", None, "tensor"),
        P("section", "tensor", "dp"),
        P("section", None),
        P("section", "dp", "tensor"),
        P("section", "tensor"),
        P("section", "tensor", "dp"),
        P("section", None),
        P("section", None),
        P("section", None),
    )
    out_rows = P("section", None, "dp", "tensor", None)
    return jax.shard_map(
        shards,
        mesh=mesh,
        in_specs=(rows, rows, P(None, "dp")) + placed_weights,
        out_specs=(out_rows, out_rows) + placed_weights,
        check_vma=False,
    )
```

```python
from functools import partial

import jax
import jax.numpy as jnp
import numpy as np
from jax import lax
from jax.experimental import pallas as pl
from jax.experimental.pallas import tpu as pltpu
from jax.sharding import PartitionSpec as P

HD = 64
ROT = 32
EPSILON = 1e-05
MESH = pl.DeviceIdType.MESH
BF = jnp.bfloat16
F32 = jnp.float32

D = 2048
SLOT = 256
ROWS = 64
PART = ROWS // 2
QKV = 768
UP = 1024
A_COLS = QKV + UP
MIX = 256
B_COLS = MIX + UP
A_HALF = A_COLS // 2
B_HALF = B_COLS // 2
ALL = 4 * SLOT
VMEM_LIMIT = 62 * 2**20


def dot(a, b):
    return lax.dot_general(a, b, (((1,), (0,)), ((), ())), preferred_element_type=F32)


def dot_nt(a, b):
    return lax.dot_general(a, b, (((1,), (1,)), ((), ())), preferred_element_type=F32)


def dot_tn(a, b):
    return lax.dot_general(a, b, (((0,), (0,)), ((), ())), preferred_element_type=F32)


def remote(src, dst, send, recv, device):
    return pltpu.make_async_remote_copy(
        src_ref=src, dst_ref=dst, send_sem=send, recv_sem=recv, device_id=device, device_id_type=MESH
    )


def greet(peers):
    barrier = pltpu.get_barrier_semaphore()
    for peer in peers:
        pl.semaphore_signal(barrier, inc=1, device_id=peer, device_id_type=MESH)
    pl.semaphore_wait(barrier, len(peers))


class Place:
    def __init__(self):
        self.dp = lax.axis_index("dp")
        self.core = lax.rem(self.dp, 2)
        self.x = lax.rem(self.dp // 2, 2)
        self.y = self.dp // 4
        self.z = lax.axis_index("tensor")
        self.sibling = {"dp": self.dp + 1 - 2 * self.core}
        self.across = {"dp": self.at(self.y, 1 - self.x, self.core)}

    def at(self, y, x, core):
        return (y * 2 + x) * 2 + core

    def turn(self, by):
        return lax.rem(self.y + 4 + by, 4)

    def beside(self, by):
        return {"dp": self.at(self.turn(by), self.x, self.core)}

    def z_peer(self, by):
        return {"tensor": lax.rem(self.z + by, 4)}


STAGES = (
    ((0, 512), (512, 512), (1024, 384), (1408, 384)),
    ((0, 384), (384, 384), (768, 256), (1024, 256)),
)


def layers_kernel(
    x_hbm, cot_hbm, qkv_hbm, up_hbm, ow_hbm, dw_hbm,
    qb_ref, ub_ref, ob_ref, db_ref, gain_ref, shift_ref, mine_ref, cos_ref, sin_ref,
    lo_out, ig_out, gq_out, gu_out, go_out, gd_out, sums_ref, gqb_ref, gub_ref, aside_out,
    wa, wb, normed, grads, qkv, hcat, slope, probs, gproj, part, got, zgot, xrow, grow, ctab, stab, split, ours, theirs, bias,
    far_a, half_a, half_b, got_a, got_b, xa_in, sum_a, tally, came,
    own_sem, x_send, x_recv, y_send, y_recv, sib_send, sib_recv,
    agz_s, agz_r, ags_s, ags_r, par_s, par_r, rsz_s, rsz_r, sec_s, sec_r,
    xs, xr, fs, fr, ns, nr, ts, tr, end_s, end_r, end_k, keep_s, free_sem, pair_free, aside_s,
):
    me = Place()
    section = lax.axis_index("section")
    core, z = me.core, me.z
    greet(
        [me.sibling, me.across, me.beside(1), me.beside(-1), me.beside(2)]
        + [me.z_peer(1), me.z_peer(2), me.z_peer(3), {"section": 1 - section}]
    )

    def device_span(dp):
        return pl.ds(pl.multiple_of(dp * 128, 128), 128)

    def chip_span(y_at, x_at):
        return pl.ds(pl.multiple_of((y_at * 2 + x_at) * 256, 256), 256)

    def place(at, size):
        return pl.ds(pl.multiple_of(at * size, size), size)

    def blocks(dp, half):
        span = device_span(dp)
        pairs = [
            (qkv_hbm.at[k, :, place(half, MIX)], wa.at[span, pl.ds(k * MIX, MIX)]) for k in range(3)
        ]
        pairs.append((up_hbm.at[:, place(half, UP)], wa.at[span, pl.ds(QKV, UP)]))
        pairs.append((ow_hbm.at[place(half, MIX), :], wb.at[pl.ds(0, MIX), span]))
        pairs.append((dw_hbm.at[place(half, UP), :], wb.at[pl.ds(MIX, UP), span]))
        return pairs

    other = me.dp + 1 - 2 * core
    holds = [
        pltpu.make_async_copy(source, target, own_sem.at[at])
        for at, (source, target) in enumerate(blocks(me.dp, core))
    ]
    gives = [
        remote(source, target, sib_send.at[at], sib_recv.at[at], me.sibling)
        for at, (source, target) in enumerate(blocks(me.dp, 1 - core))
    ]
    takes = [
        remote(source, target, sib_send.at[at], sib_recv.at[at], me.sibling)
        for at, (source, target) in enumerate(blocks(other, 1 - core))
    ]
    tell = remote(ours, theirs, sib_send.at[6], sib_recv.at[6], me.sibling)
    rows_in = [
        pltpu.make_async_copy(x_hbm, xrow, own_sem.at[6]),
        pltpu.make_async_copy(cot_hbm, grow, own_sem.at[6]),
    ]
    y, x = me.y, me.x
    far = me.turn(2)

    def piece_of(stage, y_at, x_at, which):
        span = pl.ds(*STAGES[stage][which])
        if stage == 0:
            return wa.at[chip_span(y_at, x_at), span]
        return wb.at[span, chip_span(y_at, x_at)]

    def over_x(stage, y_at, x_at, which, slot):
        piece = piece_of(stage, y_at, x_at, which)
        return remote(piece, piece, x_send.at[stage, slot], x_recv.at[stage, slot], me.across)

    def over_y(stage, by, y_at, x_at, which, slot):
        piece = piece_of(stage, y_at, x_at, which)
        way = 0 if by > 0 else 1
        return remote(piece, piece, y_send.at[stage, way, slot], y_recv.at[stage, way, slot], me.beside(by))

    sent = []

    def start(copy):
        copy.start()
        sent.append(copy)

    def own_first(stage):
        for which in (0, 1):
            start(over_x(stage, y, x, which, which))
        for which in (2, 3):
            for by in (1, -1):
                start(over_y(stage, by, y, x, which, which))

    def own_second(stage):
        for which in (2, 3):
            start(over_x(stage, y, x, which, which))
        for which in (0, 1):
            for by in (1, -1):
                start(over_y(stage, by, y, x, which, which))

    def pass_near(stage):
        for which in (2, 3):
            for by in (1, -1):
                source = me.turn(-by)
                over_y(stage, by, source, x, which, which).wait_recv()
                if (which == 2) == (by > 0):
                    start(over_y(stage, by, source, x, which, 6))
                start(over_x(stage, source, x, which, 2 * which + (0 if by > 0 else 1)))

    def pass_crossed(stage):
        for which in (0, 1):
            over_x(stage, y, 1 - x, which, which).wait_recv()
            for by in (1, -1):
                start(over_y(stage, by, y, 1 - x, which, 4 + which))

    def pass_far(stage):
        for which, by in ((2, 1), (3, -1)):
            over_y(stage, by, far, x, which, 6).wait_recv()
            start(over_x(stage, far, x, which, 6 + which))

    def pass_on(stage):
        for which, by in ((0, 1), (1, -1)):
            source = me.turn(-by)
            over_y(stage, by, source, x, which, which).wait_recv()
            start(over_y(stage, by, source, x, which, 7))

    def pass_on_crossed(stage):
        for which, by in ((0, 1), (1, -1)):
            source = me.turn(-by)
            over_y(stage, by, source, 1 - x, which, 4 + which).wait_recv()
            start(over_y(stage, by, source, 1 - x, which, 8))

    def settle(stage):
        for which, by in ((0, -1), (1, 1)):
            source = me.turn(-by)
            over_y(stage, by, source, x, which, which).wait_recv()
            over_y(stage, by, source, 1 - x, which, 4 + which).wait_recv()
        for which in (2, 3):
            over_x(stage, y, 1 - x, which, which).wait_recv()
            for by in (1, -1):
                over_x(stage, me.turn(-by), 1 - x, which, 2 * which + (0 if by > 0 else 1)).wait_recv()
            over_x(stage, far, 1 - x, which, 6 + which).wait_recv()
        for which, by in ((0, 1), (1, -1)):
            over_y(stage, by, far, x, which, 7).wait_recv()
            over_y(stage, by, far, 1 - x, which, 8).wait_recv()

    def band(at, h):
        return pl.ds(pl.multiple_of(at * ROWS + h * PART, PART), PART)

    def slot(i):
        return pl.ds(pl.multiple_of(i * SLOT, SLOT), SLOT)

    def slot_band(i, at, h):
        return pl.ds(pl.multiple_of(i * SLOT + at * ROWS + h * PART, PART), PART)

    halves = (slice(0, PART), slice(PART, ROWS))

    def standard(rows):
        average = jnp.mean(rows, axis=-1, keepdims=True)
        centred = rows - average
        variance = jnp.mean(centred * centred, axis=-1, keepdims=True)
        scale = lax.rsqrt(variance + EPSILON)
        return centred * scale, scale

    def spread_buffer(back):
        return grads if back else normed

    def to_z(back, m, i, k, h):
        piece = spread_buffer(back).at[slot_band(i, z, h)]
        at = 2 * k + h
        return remote(piece, piece, agz_s.at[back, m, at], agz_r.at[back, m, at], me.z_peer(1 + k))

    def from_z(back, m, i, k, h):
        piece = spread_buffer(back).at[slot_band(i, lax.rem(z + 3 - k, 4), h)]
        at = 2 * k + h
        return remote(piece, piece, agz_s.at[back, m, at], agz_r.at[back, m, at], me.z_peer(3 - k))

    def to_sibling(back, m, i, k, h):
        piece = spread_buffer(back).at[slot_band(i, lax.rem(z + 3 - k, 4), h)]
        at = 2 * k + h
        return remote(piece, piece, ags_s.at[back, m, at], ags_r.at[back, m, at], me.sibling)

    def spread_own(back, m, wait):
        i = 2 * m + core
        for h in range(2):
            if wait:
                onward(1 if back else 0, m, h).wait_recv()
            if back:
                grads[slot_band(i, z, h)] = grow[m, halves[h]]
            else:
                xhat, _ = standard(xrow[m, halves[h]].astype(F32))
                normed[slot_band(i, z, h)] = (xhat * gain_ref[...] + shift_ref[...]).astype(BF)
            for k in range(3):
                to_z(back, m, i, k, h).start()
            to_sibling(back, m, i, 3, h).start()

    def relay(back, i):
        m = i // 2
        for h in range(2):
            for k in range(3):
                from_z(back, m, i, k, h).wait_recv()
                to_sibling(back, m, i, k, h).start()

    def await_rows(back, i):
        m = i // 2

        @pl.when(lax.rem(i, 2) != core)
        def _():
            for h in range(2):
                for k in range(4):
                    to_sibling(back, m, i, k, h).wait_recv()

    def part_at(i):
        return (1 - lax.rem(i + core, 2)) * (i // 2) + lax.rem(i + core, 2) * (2 + i // 2)

    def to_pair(back, i, q):
        m = i // 2
        span = pl.ds(q * (D // 2), D // 2)
        return remote(
            part.at[2 + m, :, span], got.at[m, :, span], par_s.at[back, m, q], par_r.at[back, m, q], me.sibling
        )

    def sum_to_z(back, m, k, h):
        peer = me.z_peer(1 + k)
        at = 2 * k + h
        return remote(
            part.at[m, band(peer["tensor"], h)],
            zgot.at[back * 2 + m, k, pl.ds(h * PART, PART)],
            rsz_s.at[back, m, at],
            rsz_r.at[back, m, at],
            peer,
        )

    def pair_add(back, m):
        for q in range(2):
            span = slice(q * (D // 2), (q + 1) * (D // 2))
            to_pair(back, 2 * m + core, q).wait_recv()
            part[m, :, span] = (part[m, :, span].astype(F32) + got[m, :, span].astype(F32)).astype(BF)
        if back == 0:
            pl.semaphore_signal(pair_free.at[m], inc=1, device_id=me.sibling, device_id_type=MESH)

    def pair_spread(back, m):
        for h in range(2):
            for k in range(3):
                sum_to_z(back, m, k, h).start()

    def pair_sum(back, m):
        pair_add(back, m)
        pair_spread(back, m)

    def pair_sent(back, m):
        for h in range(2):
            for k in range(3):
                sum_to_z(back, m, k, h).wait_send()

    def aside(m):
        return pltpu.make_async_copy(part.at[m], aside_out.at[m], aside_s.at[0, m])

    def back_again(m):
        return pltpu.make_async_copy(aside_out.at[m], part.at[m], aside_s.at[1, m])

    def row_sum(back, m, h):
        total = part[m, band(z, h)].astype(F32)
        for k in range(3):
            sum_to_z(back, m, k, h).wait_recv()
            total = total + zgot[back * 2 + m, k, halves[h]].astype(F32)
        return total

    def onward(back, m, h):
        target = grow if back else xrow
        span = pl.ds(h * PART, PART)
        return remote(
            zgot.at[back * 2 + m, 0, span],
            target.at[m, span],
            sec_s.at[back, m, h],
            sec_r.at[back, m, h],
            {"section": 1 - back},
        )

    def keep(back, m):
        target = ig_out if back else lo_out
        return pltpu.make_async_copy(zgot.at[back * 2 + m, 0], target.at[m], keep_s.at[back, m])

    def finish_forward(m):
        for h in range(2):
            total = row_sum(0, m, h) + (ob_ref[...] + db_ref[...])
            zgot[m, 0, halves[h]] = (xrow[m, halves[h]].astype(F32) + total).astype(BF)

            @pl.when(section == 0)
            def _():
                onward(0, m, h).start()

        keep(0, m).start()

    def finish_backward(m):
        for h in range(2):
            grad = row_sum(1, m, h)
            xhat, scale = standard(xrow[m, halves[h]].astype(F32))
            above = grow[m, halves[h]].astype(F32)
            a = grad * gain_ref[...]
            inner = a - jnp.mean(a, axis=-1, keepdims=True) - xhat * jnp.mean(a * xhat, axis=-1, keepdims=True)
            zgot[2 + m, 0, halves[h]] = (above + inner * scale).astype(BF)

            @pl.when(section == 1)
            def _():
                onward(1, m, h).start()

            tally[0, 0:1, :] += jnp.sum(grad * xhat, axis=0, keepdims=True)
            tally[0, 1:2, :] += jnp.sum(grad, axis=0, keepdims=True)
            tally[0, 2:3, :] += jnp.sum(above, axis=0, keepdims=True)

        keep(1, m).start()

    lanes = lax.broadcasted_iota(jnp.int32, (SLOT, 128), 1) % HD
    early = lanes < ROT // 2

    places = lax.broadcasted_iota(jnp.int32, (SLOT, 128), 0)

    def tables(i):
        first = places < split[pl.ds(i, 1), :]
        cosine, sine = cos_ref[...], sin_ref[...]
        cos_at, sin_at = ctab[pl.ds(i, 1), :], stab[pl.ds(i, 1), :]
        return (
            jnp.where(first, cosine, cosine * cos_at + sine * sin_at),
            jnp.where(first, sine, sine * cos_at - cosine * sin_at) * jnp.where(early, -1.0, 1.0),
        )

    def turned(values, table, sign):
        halves = []
        for at in (0, 128):
            piece = values[:, at : at + 128]
            swapped = jnp.where(early, pltpu.roll(piece, 128 - ROT // 2, 1), pltpu.roll(piece, ROT // 2, 1))
            halves.append(piece * table[0] + swapped * (table[1] * sign))
        return jnp.concatenate(halves, axis=1)

    def head_mask(head):
        lane = lax.broadcasted_iota(jnp.int32, (1, MIX), 1)
        return jnp.where(lane // HD == head, 1.0, 0.0).astype(BF)

    def forward_first(i):
        rows = normed[slot(i)]
        projected = dot(rows, wa[:, 0:QKV]) + bias[0:1, 0:QKV]
        table = tables(i)
        queries = turned(projected[:, 0:MIX], table, 1.0).astype(BF)
        keys = turned(projected[:, MIX : 2 * MIX], table, 1.0).astype(BF)
        values = projected[:, 2 * MIX : 3 * MIX].astype(BF)
        qkv[slot(i), 0:MIX] = queries
        qkv[slot(i), MIX : 2 * MIX] = keys
        qkv[slot(i), 2 * MIX : 3 * MIX] = values
        at = split[pl.ds(i, 1), :]
        at = jnp.concatenate([at, at], axis=1)
        row_at = lax.broadcasted_iota(jnp.int32, (SLOT, SLOT), 0)
        key_at = lax.broadcasted_iota(jnp.int32, (SLOT, SLOT), 1)
        same = jnp.where(row_at < at, 1, 0) == jnp.where(key_at < at, 1, 0)
        allowed = (key_at <= row_at) & same
        mixed = jnp.zeros((SLOT, MIX), F32)
        for head in range(4):
            mask = head_mask(head)
            scores = jnp.where(allowed, dot_nt(queries * mask, keys) * HD**-0.5, -1e30)
            weights = jnp.exp(scores - jnp.max(scores, axis=-1, keepdims=True))
            chances = (weights / jnp.sum(weights, axis=-1, keepdims=True)).astype(BF)
            probs[i, head] = chances
            mixed = mixed + dot(chances, values * mask)
        hcat[slot(i), 0:MIX] = mixed.astype(BF)
        v = dot(rows, wa[:, QKV:A_COLS]) + bias[0:1, QKV:A_COLS]
        root = np.sqrt(2 / np.pi).astype(np.float32)
        square = v * v
        bent = jnp.tanh(root * (v + 0.044715 * (square * v)))
        half = 0.5 * (1.0 + bent)
        hcat[slot(i), MIX:B_COLS] = (v * half).astype(BF)
        slope[slot(i)] = (half + 0.5 * v * (1.0 - bent * bent) * (root * (1.0 + 3 * 0.044715 * square))).astype(BF)

    def forward_second(i):
        for q in range(2):
            span = slice(q * (D // 2), (q + 1) * (D // 2))
            part[part_at(i), :, span] = dot(hcat[slot(i)], wb[:, span]).astype(BF)

            @pl.when(lax.rem(i, 2) != core)
            def _():
                to_pair(0, i, q).start()

    def backward_first(i):
        grad_hidden = dot_nt(grads[slot(i)], wb[...])
        grad_pre = (grad_hidden[:, MIX:B_COLS] * slope[slot(i)].astype(F32)).astype(BF)
        gproj[slot(i), QKV:A_COLS] = grad_pre
        sum_a[0:1, QKV:A_COLS] += jnp.sum(grad_pre.astype(F32), axis=0, keepdims=True)
        grad_mixed = grad_hidden[:, 0:MIX].astype(BF)
        queries = qkv[slot(i), 0:MIX]
        keys = qkv[slot(i), MIX : 2 * MIX]
        values = qkv[slot(i), 2 * MIX : 3 * MIX]
        zero = jnp.zeros((SLOT, MIX), F32)
        grad_queries, grad_keys, grad_values = zero, zero, zero
        for head in range(4):
            mask = head_mask(head)
            chances = probs[i, head]
            masked = grad_mixed * mask
            grad_values = grad_values + dot_tn(chances, masked)
            grad_probs = dot_nt(masked, values)
            wide = chances.astype(F32)
            centre = jnp.sum(wide * grad_probs, axis=-1, keepdims=True)
            grad_scores = (wide * (grad_probs - centre)).astype(BF)
            grad_queries = grad_queries + dot(grad_scores, keys * mask)
            grad_keys = grad_keys + dot_tn(grad_scores, queries * mask)
        table = tables(i)
        pieces = (
            turned(grad_queries * HD**-0.5, table, -1.0).astype(BF),
            turned(grad_keys * HD**-0.5, table, -1.0).astype(BF),
            grad_values.astype(BF),
        )
        for at, piece in enumerate(pieces):
            span = slice(at * MIX, (at + 1) * MIX)
            gproj[slot(i), span] = piece
            sum_a[0:1, span] += jnp.sum(piece.astype(F32), axis=0, keepdims=True)

    def backward_second(i):
        other_slot = lax.rem(i, 2) != core

        @pl.when(other_slot)
        def _():
            pl.semaphore_wait(pair_free.at[i // 2], 1)
            for q in range(2):
                to_pair(0, i, q).wait_send()

        for q in range(2):
            span = slice(q * (D // 2), (q + 1) * (D // 2))
            part[part_at(i), :, span] = dot_nt(gproj[slot(i)], wa[span, :]).astype(BF)

            @pl.when(other_slot)
            def _():
                to_pair(1, i, q).start()

    for copy in holds + gives:
        copy.start()
    ours[...] = jnp.zeros_like(ours)
    for m in range(2):
        ours[m : m + 1, :] = jnp.broadcast_to(mine_ref[0:1, m : m + 1], (1, 128))
    tell.start()

    @pl.when(section == 0)
    def _():
        rows_in[0].start()

    @pl.when(section == 1)
    def _():
        rows_in[1].start()

    sum_a[...] = jnp.zeros_like(sum_a)
    tally[0] = jnp.zeros((8, D), F32)
    for at in range(4):
        holds[at].wait()
        takes[at].wait_recv()
    own_first(0)
    own_second(0)

    @pl.when(section == 0)
    def _():
        rows_in[0].wait()
        for m in range(2):
            spread_own(0, m, False)

    @pl.when(section == 1)
    def _():
        rows_in[1].wait()
        for m in range(2):
            spread_own(1, m, False)

    for at in (4, 5):
        holds[at].wait()
        takes[at].wait_recv()
    for at in range(3):
        bias[0:1, at * MIX : (at + 1) * MIX] = jnp.where(
            core == 0, qb_ref[at, 0:1, 0:MIX], qb_ref[at, 0:1, MIX : 2 * MIX]
        )
    bias[0:1, QKV:A_COLS] = jnp.where(core == 0, ub_ref[0:1, 0:UP], ub_ref[0:1, UP : 2 * UP])
    tell.wait_recv()
    for i in range(4):
        at = jnp.where(core == i % 2, ours[i // 2 : i // 2 + 1, :], theirs[i // 2 : i // 2 + 1, :])
        split[i : i + 1, :] = at
        here = places == at
        ctab[i : i + 1, :] = jnp.sum(jnp.where(here, cos_ref[...], 0.0), axis=0, keepdims=True)
        stab[i : i + 1, :] = jnp.sum(jnp.where(here, sin_ref[...], 0.0), axis=0, keepdims=True)

    pass_near(0)
    pass_crossed(0)

    def relay_early(m):
        @pl.when(section == 0)
        def _():
            relay(0, 2 * m + core)

        @pl.when(section == 1)
        def _():
            relay(1, 2 * m + core)

    relay_early(0)
    pass_on(0)
    own_first(1)
    pass_far(0)
    relay_early(1)
    pass_on_crossed(0)
    own_second(1)
    settle(0)
    pass_near(1)

    def forward_early(i):
        @pl.when(section == 0)
        def _():
            await_rows(0, i)
            forward_first(i)

    forward_early(0)
    pass_crossed(1)
    forward_early(1)
    pass_on(1)
    pass_far(1)
    forward_early(2)
    forward_early(3)
    pass_on_crossed(1)
    settle(1)

    def finish_forward_all():
        for m in range(2):
            finish_forward(m)

    @pl.when(section == 0)
    def _():
        def step(i, _):
            forward_second(i)

            @pl.when(i == 1 + core)
            def _():
                pair_sum(0, 0)

            return 0

        lax.fori_loop(0, 4, step, 0)
        pair_sum(0, 1)
        finish_forward_all()

        @pl.when(core == 0)
        def _():
            spread_own(1, 0, True)
            relay(1, 0)

    @pl.when(section == 1)
    def _():
        spread_own(0, 0, True)

        @pl.when(core == 0)
        def _():
            relay(0, 0)

        def step(i, _):
            await_rows(0, i)
            forward_first(i)

            @pl.when(i == core)
            def _():
                spread_own(0, 1, True)

            @pl.when((i < 3) & (lax.rem(i, 2) != core))
            def _():
                relay(0, i + 1)

            @pl.when((i > 0) & (lax.rem(i, 2) != core))
            def _():
                pair_add(0, (i - 1) // 2)
                aside((i - 1) // 2).start()

            forward_second(i)
            return 0

        lax.fori_loop(0, 4, step, 0)

    def turn_of(k):
        return lax.rem(y + 2 + 3 * k + 3 * (k // 2) + 2 * (k // 3), 4)

    a_cuts = ((0, A_HALF), (A_HALF, A_COLS))
    b_cuts = ((0, B_HALF), (B_HALF, B_COLS))

    def term_a(y_at, x_at, half):
        lo, hi = a_cuts[half]
        return dot_tn(normed[:, chip_span(y_at, x_at)], gproj[:, lo:hi])

    def term_b(y_at, x_at, half):
        lo, hi = b_cuts[half]
        return dot_tn(hcat[:, lo:hi], grads[:, chip_span(y_at, x_at)])

    def cross(k):
        span = pl.ds(pl.multiple_of(k * MIX, MIX), MIX)
        there = pl.ds(pl.multiple_of((4 + k) * 256, 256), 256)
        return (
            remote(probs.at[k, 0], wb.at[pl.ds(0, MIX), there], xs.at[k, 0], xr.at[k, 0], me.across),
            remote(slope.at[:, span], wb.at[pl.ds(MIX, UP), there], xs.at[k, 1], xr.at[k, 1], me.across),
        )

    def cross_all():
        pl.semaphore_wait(free_sem, 1)

        def step(k, _):
            span = pl.ds(pl.multiple_of(k * MIX, MIX), MIX)
            total = term_b(turn_of(k), 1 - x, 0).astype(BF)
            probs[k, 0] = total[0:MIX]
            slope[0 : B_HALF - MIX, span] = total[MIX:B_HALF]
            slope[B_HALF - MIX : UP, span] = term_b(turn_of(k), 1 - x, 1).astype(BF)
            for copy in cross(k):
                copy.start()
            return 0

        lax.fori_loop(0, 4, step, 0)

    def crossed(k):
        for copy in cross(k):
            copy.wait_recv()

    def from_across(k, half):
        lo, hi = b_cuts[half]
        return wb[lo:hi, (4 + k) * 256 : (5 + k) * 256].astype(F32)

    def a_place(at):
        return wa.at[pl.ds(pl.multiple_of(at * 256, 256), 256)]

    def b_place(at):
        return wb.at[:, pl.ds(at * 256, 256)]

    a_spans = (pl.ds(0, A_HALF), pl.ds(A_HALF, A_HALF))
    b_spans = (pl.ds(0, B_HALF), pl.ds(B_HALF, B_HALF))

    def far_piece(way, x_at):
        source = far_a.at[x_at, :, a_spans[way]]
        return remote(source, half_a.at[way, x_at], fs.at[way, x_at], fr.at[way, x_at], me.beside(1 - 2 * way))

    def far_piece_b(way):
        source = wb.at[b_spans[way], pl.ds(0, 256)]
        return remote(source, half_b.at[way], fs.at[way, 2], fr.at[way, 2], me.beside(1 - 2 * way))

    def near_piece(way, x_at):
        source = a_place(2 + 2 * way + x_at)
        return remote(source, got_a.at[way, x_at], ns.at[way, x_at], nr.at[way, x_at], me.beside(1 - 2 * way))

    def near_piece_b(way):
        return remote(b_place(1 + way), got_b.at[way], ns.at[way, 2], nr.at[way, 2], me.beside(1 - 2 * way))

    def cross_last():
        return remote(a_place(6), xa_in, xs.at[4, 0], xr.at[4, 0], me.across)

    def send_far_all():
        def step(k, _):
            x_at = (1 - k) * (1 - x) + k * x
            for way, (lo, hi) in enumerate(a_cuts):
                far_a[x_at, :, lo:hi] = term_a(far, x_at, way).astype(BF)
                far_piece(way, x_at).start()
            return 0

        lax.fori_loop(0, 2, step, 0)

    def send_near(way, x_at):
        target = pl.ds(pl.multiple_of((2 + 2 * way + x_at) * 256, 256), 256)
        for half in (1 - way, way):
            lo, hi = a_cuts[half]
            total = term_a(me.turn(1 - 2 * way), x_at, half)
            if half == way:
                far_piece(way, x_at).wait_recv()
                total = total + half_a[way, x_at].astype(F32)
            wa[target, lo:hi] = total.astype(BF)
        start(near_piece(way, x_at))

    def send_far_b():
        for way, (lo, hi) in enumerate(b_cuts):
            total = term_b(far, x, way)
            if way == 0:
                crossed(0)
            wb[lo:hi, 0:256] = (total + from_across(0, way)).astype(BF)
            start(far_piece_b(way))

    def send_near_b(way):
        span = slice((1 + way) * 256, (2 + way) * 256)
        for half in (1 - way, way):
            lo, hi = b_cuts[half]
            total = term_b(me.turn(1 - 2 * way), x, half)
            if half != way:
                crossed(1 + way)
            total = total + from_across(1 + way, half)
            if half == way:
                far_piece_b(way).wait_recv()
                total = total + half_b[way].astype(F32)
            wb[lo:hi, span] = total.astype(BF)
        start(near_piece_b(way))

    def arrived_a(x_at, at):
        for half, (lo, hi) in enumerate(a_cuts):
            total = term_a(y, x_at, half)
            for way in (0, 1):
                if half == 0:
                    near_piece(way, x_at).wait_recv()
                total = total + got_a[way, x_at, :, lo:hi].astype(F32)
            wa[at * 256 : (at + 1) * 256, lo:hi] = total.astype(BF)

    def begun_b(at):
        crossed(3)
        for half, (lo, hi) in enumerate(b_cuts):
            wb[lo:hi, at * 256 : (at + 1) * 256] = (term_b(y, x, half) + from_across(3, half)).astype(BF)

    def arrived_b(at):
        span = slice(at * 256, (at + 1) * 256)
        total = wb[:, span].astype(F32)
        for way in (0, 1):
            near_piece_b(way).wait_recv()
            total = total + got_b[way].astype(F32)
        wb[:, span] = total.astype(BF)

    near_z = {"tensor": z + 1 - 2 * lax.rem(z, 2)}
    near_y = {"dp": me.at(y + 1 - 2 * lax.rem(y, 2), x, core)}
    partners = (near_z, me.z_peer(2), me.sibling, me.across, near_y, me.beside(2))

    def exchange(step):
        return remote(tally.at[step], came.at[step], ts.at[step], tr.at[step], partners[step])

    def fold(step):
        exchange(step).wait_recv()
        total = tally[step] + came[step]
        if step < 3:
            tally[step + 1, 0:3] = total[0:3]
            tally[step + 1, 3:8] = tally[step, 3:8]
            if step == 2:
                tally[step + 1, 4:5] = came[step, 3:4]
        else:
            tally[step + 1] = total
        if step < 5:
            start(exchange(step + 1))

    for copy in sent:
        copy.wait_send()
    sent.clear()

    def backward_step(i, _):
        own = lax.rem(i, 2) == core

        @pl.when((section == 0) & (i + core == 1))
        def _():
            spread_own(1, 1 - core, True)

        await_rows(1, i)
        backward_first(i)

        @pl.when((section == 0) & (i == 1) & (core == 1))
        def _():
            spread_own(1, 1, True)

        @pl.when((section == 0) & (lax.rem(i, 2) == 0) & (i < 3) & jnp.logical_not(own))
        def _():
            relay(1, i + 1)

        @pl.when(i == 3)
        def _():
            pl.semaphore_signal(free_sem, inc=1, device_id=me.across, device_id_type=MESH)

        @pl.when((section == 0) & (i == 3))
        def _():
            send_far_all()
            cross_all()

        @pl.when((section == 1) & (i >= 1) & jnp.logical_not(own))
        def _():
            pair_sum(1, (i - 1) // 2)

        @pl.when((section == 1) & (i >= 2) & own)
        def _():
            finish_backward(0)

        @pl.when((section == 1) & (core == 1) & (i == 0))
        def _():
            pair_add(0, 1)
            aside(1).start()

        @pl.when((section == 0) & own)
        def _():
            pair_sent(0, i // 2)

        @pl.when((section == 1) & own)
        def _():
            aside(i // 2).wait()

        backward_second(i)

        @pl.when((section == 0) & (i == 1) & jnp.logical_not(own))
        def _():
            relay(1, 2)

        return 0

    lax.fori_loop(0, 4, backward_step, 0)

    @pl.when(section == 1)
    def _():
        @pl.when(core == 1)
        def _():
            pair_sum(1, 1)

        finish_backward(1)
        send_far_all()
        cross_all()

    @pl.when(section == 0)
    def _():
        for m in range(2):
            pair_sum(1, m)

    @pl.when(section == 1)
    def _():
        for m in range(2):
            pair_sent(1, m)
            back_again(m).start()
        for m in range(2):
            back_again(m).wait()
            pair_spread(0, m)

    send_far_b()
    for x_at in (1 - x, x):
        for way in (0, 1):
            send_near(way, x_at)

    @pl.when(section == 0)
    def _():
        for m in range(2):
            finish_backward(m)

    @pl.when(section == 1)
    def _():
        finish_forward_all()

    tally[0, 3:4, 0:A_COLS] = sum_a[0:1]
    start(exchange(0))
    send_near_b(0)
    fold(0)
    fold(1)
    send_near_b(1)
    fold(2)
    arrived_a(1 - x, 6)
    start(cross_last())
    arrived_a(x, 7)
    begun_b(3)
    fold(3)

    def result(half, peer, at):
        rows = pl.ds(pl.multiple_of(7 * 256 + half * 128, 128), 128)
        cols = pl.ds(pl.multiple_of(3 * 256 + half * 128, 128), 128)
        sources = [wa.at[rows, pl.ds(k * MIX, MIX)] for k in range(3)]
        sources += [wa.at[rows, pl.ds(QKV, UP)], wb.at[pl.ds(0, MIX), cols], wb.at[pl.ds(MIX, UP), cols]]
        targets = [gq_out.at[k, :, place(at, MIX)] for k in range(3)]
        targets += [gu_out.at[:, place(at, UP)], go_out.at[place(at, MIX), :], gd_out.at[place(at, UP), :]]
        if peer:
            return [
                remote(source, target, end_s.at[k], end_r.at[k], me.sibling)
                for k, (source, target) in enumerate(zip(sources, targets))
            ]
        return [
            pltpu.make_async_copy(source, target, end_k.at[k])
            for k, (source, target) in enumerate(zip(sources, targets))
        ]

    outgoing, staying = result(1 - core, True, core), result(core, False, core)
    incoming = result(1 - core, True, 1 - core)
    cross_last().wait_recv()
    wa[7 * 256 : 8 * 256] = (wa[7 * 256 : 8 * 256].astype(F32) + xa_in[...].astype(F32)).astype(BF)
    for at in range(4):
        outgoing[at].start()
        staying[at].start()
    fold(4)
    arrived_b(3)
    for at in (4, 5):
        outgoing[at].start()
        staying[at].start()
    fold(5)
    sums_ref[...] = tally[6]
    for at in range(3):
        span = slice(at * MIX, (at + 1) * MIX)
        ours_a, others_a = tally[6, 3:4, span], tally[6, 4:5, span]
        gqb_ref[at : at + 1, 0:MIX] = jnp.where(core == 0, ours_a, others_a)
        gqb_ref[at : at + 1, MIX : 2 * MIX] = jnp.where(core == 0, others_a, ours_a)
    ours_a, others_a = tally[6, 3:4, QKV:A_COLS], tally[6, 4:5, QKV:A_COLS]
    gub_ref[0:1, 0:UP] = jnp.where(core == 0, ours_a, others_a)
    gub_ref[0:1, UP : 2 * UP] = jnp.where(core == 0, others_a, ours_a)

    for copy in sent + gives + [tell]:
        copy.wait_send()
    for k in range(4):
        for copy in cross(k):
            copy.wait_send()
    for way in range(2):
        for x_at in range(2):
            far_piece(way, x_at).wait_send()
    for back in range(2):
        for m in range(2):
            mine = 2 * m + core
            for h in range(2):
                for k in range(3):
                    to_z(back, m, mine, k, h).wait_send()
                for k in range(4):
                    to_sibling(back, m, mine, k, h).wait_send()
            keep(back, m).wait()

        @pl.when(section == back)
        def _():
            for m in range(2):
                for h in range(2):
                    onward(back, m, h).wait_send()

        @pl.when(section != back)
        def _():
            for m in range(2):
                pair_sent(back, m)

    for m in range(2):
        for q in range(2):
            to_pair(1, 2 * m + 1 - core, q).wait_send()
    for at in range(6):
        staying[at].wait()
        outgoing[at].wait_send()
        incoming[at].wait_recv()


def both_layers(rows_in, cotangent, qkv_w, up_w, out_w, down_w, bias_qkv, bias_up, bias_out, bias_down, gain, shift, mine):
    places = np.arange(SLOT, dtype=np.float32)
    frequency = (10000.0 ** (-(np.arange(ROT // 2, dtype=np.float32) * np.float32(2.0 / ROT)))).astype(np.float32)
    angles = (places[:, None] * frequency[None, :]).astype(np.float32).astype(np.float64)
    cosine = np.ones((SLOT, HD), np.float32)
    sine = np.zeros((SLOT, HD), np.float32)
    cosine[:, 0:ROT] = np.tile(np.cos(angles), (1, 2))
    sine[:, 0:ROT] = np.tile(np.sin(angles), (1, 2))
    cosine, sine = (jnp.asarray(np.tile(table, (1, 2))) for table in (cosine, sine))
    any_ = pl.BlockSpec(memory_space=pl.ANY)
    vmem = pl.BlockSpec(memory_space=pltpu.VMEM)
    dma = pltpu.SemaphoreType.DMA
    shape = jax.ShapeDtypeStruct
    return pl.pallas_call(
        layers_kernel,
        out_shape=(
            shape((2, ROWS, D), BF),
            shape((2, ROWS, D), BF),
            shape((3, 128, 2 * MIX), BF),
            shape((128, 2 * UP), BF),
            shape((2 * MIX, 128), BF),
            shape((2 * UP, 128), BF),
            shape((8, D), F32),
            shape((3, 2 * MIX), F32),
            shape((1, 2 * UP), F32),
            shape((2, SLOT, D), BF),
        ),
        in_specs=[any_] * 6 + [vmem] * 9,
        out_specs=[any_] * 6 + [vmem] * 3 + [any_],
        scratch_shapes=[
            pltpu.VMEM((D, A_COLS), BF),
            pltpu.VMEM((B_COLS, D), BF),
            pltpu.VMEM((ALL, D), BF),
            pltpu.VMEM((ALL, D), BF),
            pltpu.VMEM((ALL, QKV), BF),
            pltpu.VMEM((ALL, B_COLS), BF),
            pltpu.VMEM((ALL, UP), BF),
            pltpu.VMEM((4, 4, SLOT, SLOT), BF),
            pltpu.VMEM((ALL, A_COLS), BF),
            pltpu.VMEM((4, SLOT, D), BF),
            pltpu.VMEM((2, SLOT, D), BF),
            pltpu.VMEM((4, 3, ROWS, D), BF),
            pltpu.VMEM((2, ROWS, D), BF),
            pltpu.VMEM((2, ROWS, D), BF),
            pltpu.VMEM((8, 128), F32),
            pltpu.VMEM((8, 128), F32),
            pltpu.VMEM((8, 128), jnp.int32),
            pltpu.VMEM((8, 128), jnp.int32),
            pltpu.VMEM((8, 128), jnp.int32),
            pltpu.VMEM((8, A_COLS), F32),
            pltpu.VMEM((2, 256, A_COLS), BF),
            pltpu.VMEM((2, 2, 256, A_HALF), BF),
            pltpu.VMEM((2, B_HALF, 256), BF),
            pltpu.VMEM((2, 2, 256, A_COLS), BF),
            pltpu.VMEM((2, B_COLS, 256), BF),
            pltpu.VMEM((256, A_COLS), BF),
            pltpu.VMEM((8, A_COLS), F32),
            pltpu.VMEM((7, 8, D), F32),
            pltpu.VMEM((6, 8, D), F32),
            dma((7,)),
            dma((2, 10)),
            dma((2, 10)),
            dma((2, 2, 9)),
            dma((2, 2, 9)),
            dma((7,)),
            dma((7,)),
            dma((2, 2, 6)),
            dma((2, 2, 6)),
            dma((2, 2, 8)),
            dma((2, 2, 8)),
            dma((2, 2, 2)),
            dma((2, 2, 2)),
            dma((2, 2, 6)),
            dma((2, 2, 6)),
            dma((2, 2, 2)),
            dma((2, 2, 2)),
            dma((5, 2)),
            dma((5, 2)),
            dma((2, 3)),
            dma((2, 3)),
            dma((2, 3)),
            dma((2, 3)),
            dma((6,)),
            dma((6,)),
            dma((6,)),
            dma((6,)),
            dma((6,)),
            dma((2, 2)),
            pltpu.SemaphoreType.REGULAR,
            pltpu.SemaphoreType.REGULAR((2,)),
            dma((2, 2)),
        ],
        compiler_params=pltpu.CompilerParams(
            collective_id=1, has_side_effects=True, vmem_limit_bytes=VMEM_LIMIT
        ),
        name="both_layers",
    )(
        rows_in, cotangent, qkv_w, up_w, out_w, down_w,
        bias_qkv, bias_up, bias_out, bias_down, gain, shift, mine, cosine, sine,
    )


def widen_kernel(lo, ig, gq, gu, go, gd, sums, gqb, gub, *outs):
    lo_out, ig_out, gq_out, gu_out, go_out, gd_out, gain, shift, out_b, down_b, qkv_b, up_b = outs
    lo_out[...] = lo[...]
    ig_out[...] = ig[...]
    gq_out[...] = gq[...].astype(F32)
    gu_out[...] = gu[...].astype(F32)
    go_out[...] = go[...].astype(F32)
    gd_out[...] = gd[...].astype(F32)
    gain[...] = sums[0:1]
    shift[...] = sums[1:2]
    out_b[...] = sums[2:3]
    down_b[...] = sums[2:3]
    for k in range(3):
        qkv_b[k] = gqb[k : k + 1]
    up_b[...] = gub[...]


def widened(lo, ig, gq, gu, go, gd, sums, gqb, gub):
    steps = 4
    shape = jax.ShapeDtypeStruct

    def cut(whole, dim):
        block = tuple(size // steps if at == dim else size for at, size in enumerate(whole))
        return pl.BlockSpec(block, lambda i: tuple(i if at == dim else 0 for at in range(len(whole))))

    def same(whole):
        return pl.BlockSpec(whole, lambda i: (0,) * len(whole))

    large = [cut(lo.shape, 1), cut(ig.shape, 1), cut(gq.shape, 1), cut(gu.shape, 0), cut(go.shape, 0), cut(gd.shape, 0)]
    small = [(1, D)] * 4 + [(3, 1, 2 * MIX), (1, 2 * UP)]
    return pl.pallas_call(
        widen_kernel,
        grid=(steps,),
        out_shape=(
            [shape(lo.shape, BF), shape(ig.shape, BF)]
            + [shape(each.shape, F32) for each in (gq, gu, go, gd)]
            + [shape(each, F32) for each in small]
        ),
        in_specs=large + [same(sums.shape), same(gqb.shape), same(gub.shape)],
        out_specs=large + [same(each) for each in small],
        compiler_params=pltpu.CompilerParams(vmem_limit_bytes=VMEM_LIMIT),
        name="widened",
    )(lo, ig, gq, gu, go, gd, sums, gqb, gub)


def shards(
    inputs,
    cotangent,
    doc_split,
    qkv_weight,
    qkv_bias,
    out_weight,
    out_bias,
    fc1_weight,
    fc1_bias,
    fc2_weight,
    fc2_bias,
    ln_gain,
    ln_bias,
):
    results = both_layers(
        inputs[:, 0],
        cotangent[:, 0],
        qkv_weight[0].transpose(1, 0, 2),
        fc1_weight[0],
        out_weight[0],
        fc2_weight[0],
        qkv_bias[0][:, None, :],
        fc1_bias,
        out_bias,
        fc2_bias,
        ln_gain,
        ln_bias,
        doc_split.reshape(1, 2),
    )
    layer_out, input_grad, grad_qkv, grad_up, grad_out, grad_down, gain, shift, out_b, down_b, qkv_b, up_b = widened(
        *results[:9]
    )
    return (
        layer_out[None, :, None],
        input_grad[None, :, None],
        grad_qkv.transpose(1, 0, 2)[None],
        qkv_b.transpose(1, 0, 2),
        grad_out[None],
        out_b,
        grad_up[None],
        up_b,
        grad_down[None],
        down_b,
        gain,
        shift,
    )


def solution(mesh):
    rows = P(None, "dp", "tensor", None)
    placed_weights = (
        P("section", "dp", None, "tensor"),
        P("section", None, "tensor"),
        P("section", "tensor", "dp"),
        P("section", None),
        P("section", "dp", "tensor"),
        P("section", "tensor"),
        P("section", "tensor", "dp"),
        P("section", None),
        P("section", None),
        P("section", None),
    )
    out_rows = P("section", None, "dp", "tensor", None)
    return jax.shard_map(
        shards,
        mesh=mesh,
        in_specs=(rows, rows, P(None, "dp")) + placed_weights,
        out_specs=(out_rows, out_rows) + placed_weights,
        check_vma=False,
    )
```

```python
from functools import partial

import jax
import jax.numpy as jnp
import numpy as np
from jax import lax
from jax.experimental import pallas as pl
from jax.experimental.pallas import tpu as pltpu
from jax.sharding import PartitionSpec as P

HD = 64
ROT = 32
EPSILON = 1e-05
MESH = pl.DeviceIdType.MESH
BF = jnp.bfloat16
F32 = jnp.float32

D = 2048
SLOT = 256
ROWS = 64
PARTS = 4
PART = ROWS // PARTS
QKV = 768
UP = 1024
A_COLS = QKV + UP
MIX = 256
B_COLS = MIX + UP
A_HALF = A_COLS // 2
B_HALF = B_COLS // 2
ALL = 4 * SLOT
VMEM_LIMIT = 62 * 2**20


def dot(a, b):
    return lax.dot_general(a, b, (((1,), (0,)), ((), ())), preferred_element_type=F32)


def dot_nt(a, b):
    return lax.dot_general(a, b, (((1,), (1,)), ((), ())), preferred_element_type=F32)


def dot_tn(a, b):
    return lax.dot_general(a, b, (((0,), (0,)), ((), ())), preferred_element_type=F32)


def remote(src, dst, send, recv, device):
    return pltpu.make_async_remote_copy(
        src_ref=src, dst_ref=dst, send_sem=send, recv_sem=recv, device_id=device, device_id_type=MESH
    )


def greet(peers):
    barrier = pltpu.get_barrier_semaphore()
    for peer in peers:
        pl.semaphore_signal(barrier, inc=1, device_id=peer, device_id_type=MESH)
    pl.semaphore_wait(barrier, len(peers))


class Place:
    def __init__(self):
        self.dp = lax.axis_index("dp")
        self.core = lax.rem(self.dp, 2)
        self.x = lax.rem(self.dp // 2, 2)
        self.y = self.dp // 4
        self.z = lax.axis_index("tensor")
        self.sibling = {"dp": self.dp + 1 - 2 * self.core}
        self.across = {"dp": self.at(self.y, 1 - self.x, self.core)}

    def at(self, y, x, core):
        return (y * 2 + x) * 2 + core

    def turn(self, by):
        return lax.rem(self.y + 4 + by, 4)

    def beside(self, by):
        return {"dp": self.at(self.turn(by), self.x, self.core)}

    def z_peer(self, by):
        return {"tensor": lax.rem(self.z + by, 4)}


STAGES = (
    ((0, 512), (512, 512), (1024, 384), (1408, 384)),
    ((0, 384), (384, 384), (768, 256), (1024, 256)),
)


def layers_kernel(
    x_hbm, cot_hbm, qkv_hbm, up_hbm, ow_hbm, dw_hbm,
    qb_ref, ub_ref, ob_ref, db_ref, gain_ref, shift_ref, mine_ref, cos_ref, sin_ref,
    lo_out, ig_out, gq_out, gu_out, go_out, gd_out, sums_ref, gqb_ref, gub_ref,
    wa, wb, normed, grads, qkv, hcat, slope, probs, gproj, part, got, zgot, xrow, grow, ctab, stab, split, ours, theirs, bias,
    far_a, half_a, half_b, got_a, got_b, xa_in, sum_a, tally, came,
    own_sem, x_send, x_recv, y_send, y_recv, sib_send, sib_recv,
    agz_s, agz_r, ags_s, ags_r, par_s, par_r, rsz_s, rsz_r, sec_s, sec_r,
    xs, xr, fs, fr, ns, nr, ts, tr, end_s, end_r, end_k, keep_s, free_sem, pair_free,
):
    me = Place()
    section = lax.axis_index("section")
    core, z = me.core, me.z
    greet(
        [me.sibling, me.across, me.beside(1), me.beside(-1), me.beside(2)]
        + [me.z_peer(1), me.z_peer(2), me.z_peer(3), {"section": 1 - section}]
    )

    def device_span(dp):
        return pl.ds(pl.multiple_of(dp * 128, 128), 128)

    def chip_span(y_at, x_at):
        return pl.ds(pl.multiple_of((y_at * 2 + x_at) * 256, 256), 256)

    def place(at, size):
        return pl.ds(pl.multiple_of(at * size, size), size)

    def blocks(dp, half):
        span = device_span(dp)
        pairs = [
            (qkv_hbm.at[k, :, place(half, MIX)], wa.at[span, pl.ds(k * MIX, MIX)]) for k in range(3)
        ]
        pairs.append((up_hbm.at[:, place(half, UP)], wa.at[span, pl.ds(QKV, UP)]))
        pairs.append((ow_hbm.at[place(half, MIX), :], wb.at[pl.ds(0, MIX), span]))
        pairs.append((dw_hbm.at[place(half, UP), :], wb.at[pl.ds(MIX, UP), span]))
        return pairs

    other = me.dp + 1 - 2 * core
    holds = [
        pltpu.make_async_copy(source, target, own_sem.at[at])
        for at, (source, target) in enumerate(blocks(me.dp, core))
    ]
    gives = [
        remote(source, target, sib_send.at[at], sib_recv.at[at], me.sibling)
        for at, (source, target) in enumerate(blocks(me.dp, 1 - core))
    ]
    takes = [
        remote(source, target, sib_send.at[at], sib_recv.at[at], me.sibling)
        for at, (source, target) in enumerate(blocks(other, 1 - core))
    ]
    tell = remote(ours, theirs, sib_send.at[6], sib_recv.at[6], me.sibling)
    rows_in = [
        pltpu.make_async_copy(x_hbm, xrow, own_sem.at[6]),
        pltpu.make_async_copy(cot_hbm, grow, own_sem.at[6]),
    ]
    y, x = me.y, me.x
    far = me.turn(2)

    def piece_of(stage, y_at, x_at, which):
        span = pl.ds(*STAGES[stage][which])
        if stage == 0:
            return wa.at[chip_span(y_at, x_at), span]
        return wb.at[span, chip_span(y_at, x_at)]

    def over_x(stage, y_at, x_at, which, slot):
        piece = piece_of(stage, y_at, x_at, which)
        return remote(piece, piece, x_send.at[stage, slot], x_recv.at[stage, slot], me.across)

    def over_y(stage, by, y_at, x_at, which, slot):
        piece = piece_of(stage, y_at, x_at, which)
        way = 0 if by > 0 else 1
        return remote(piece, piece, y_send.at[stage, way, slot], y_recv.at[stage, way, slot], me.beside(by))

    sent = []

    def start(copy):
        copy.start()
        sent.append(copy)

    def own_first(stage):
        for which in (0, 1):
            start(over_x(stage, y, x, which, which))
        for which in (2, 3):
            for by in (1, -1):
                start(over_y(stage, by, y, x, which, which))

    def own_second(stage):
        for which in (2, 3):
            start(over_x(stage, y, x, which, which))
        for which in (0, 1):
            for by in (1, -1):
                start(over_y(stage, by, y, x, which, which))

    def pass_near(stage):
        for which in (2, 3):
            for by in (1, -1):
                source = me.turn(-by)
                over_y(stage, by, source, x, which, which).wait_recv()
                if (which == 2) == (by > 0):
                    start(over_y(stage, by, source, x, which, 6))
                start(over_x(stage, source, x, which, 2 * which + (0 if by > 0 else 1)))

    def pass_crossed(stage):
        for which in (0, 1):
            over_x(stage, y, 1 - x, which, which).wait_recv()
            for by in (1, -1):
                start(over_y(stage, by, y, 1 - x, which, 4 + which))

    def pass_far(stage):
        for which, by in ((2, 1), (3, -1)):
            over_y(stage, by, far, x, which, 6).wait_recv()
            start(over_x(stage, far, x, which, 6 + which))

    def pass_on(stage):
        for which, by in ((0, 1), (1, -1)):
            source = me.turn(-by)
            over_y(stage, by, source, x, which, which).wait_recv()
            start(over_y(stage, by, source, x, which, 7))

    def pass_on_crossed(stage):
        for which, by in ((0, 1), (1, -1)):
            source = me.turn(-by)
            over_y(stage, by, source, 1 - x, which, 4 + which).wait_recv()
            start(over_y(stage, by, source, 1 - x, which, 8))

    def settle(stage):
        for which, by in ((0, -1), (1, 1)):
            source = me.turn(-by)
            over_y(stage, by, source, x, which, which).wait_recv()
            over_y(stage, by, source, 1 - x, which, 4 + which).wait_recv()
        for which in (2, 3):
            over_x(stage, y, 1 - x, which, which).wait_recv()
            for by in (1, -1):
                over_x(stage, me.turn(-by), 1 - x, which, 2 * which + (0 if by > 0 else 1)).wait_recv()
            over_x(stage, far, 1 - x, which, 6 + which).wait_recv()
        for which, by in ((0, 1), (1, -1)):
            over_y(stage, by, far, x, which, 7).wait_recv()
            over_y(stage, by, far, 1 - x, which, 8).wait_recv()

    def band(at, h):
        return pl.ds(pl.multiple_of(at * ROWS + h * PART, PART), PART)

    def slot(i):
        return pl.ds(pl.multiple_of(i * SLOT, SLOT), SLOT)

    def slot_band(i, at, h):
        return pl.ds(pl.multiple_of(i * SLOT + at * ROWS + h * PART, PART), PART)

    parts = [slice(h * PART, (h + 1) * PART) for h in range(PARTS)]

    def standard(rows):
        average = jnp.mean(rows, axis=-1, keepdims=True)
        centred = rows - average
        variance = jnp.mean(centred * centred, axis=-1, keepdims=True)
        scale = lax.rsqrt(variance + EPSILON)
        return centred * scale, scale

    def spread_buffer(back):
        return grads if back else normed

    def to_z(back, m, i, k, h):
        piece = spread_buffer(back).at[slot_band(i, z, h)]
        at = PARTS * k + h
        return remote(piece, piece, agz_s.at[back, m, at], agz_r.at[back, m, at], me.z_peer(1 + k))

    def from_z(back, m, i, k, h):
        piece = spread_buffer(back).at[slot_band(i, lax.rem(z + 3 - k, 4), h)]
        at = PARTS * k + h
        return remote(piece, piece, agz_s.at[back, m, at], agz_r.at[back, m, at], me.z_peer(3 - k))

    def to_sibling(back, m, i, k, h):
        piece = spread_buffer(back).at[slot_band(i, lax.rem(z + 3 - k, 4), h)]
        at = PARTS * k + h
        return remote(piece, piece, ags_s.at[back, m, at], ags_r.at[back, m, at], me.sibling)

    def spread_own(back, m, wait):
        i = 2 * m + core
        for h in range(PARTS):
            if wait:
                onward(1 if back else 0, m, h).wait_recv()
            if back:
                grads[slot_band(i, z, h)] = grow[m, parts[h]]
            else:
                xhat, _ = standard(xrow[m, parts[h]].astype(F32))
                normed[slot_band(i, z, h)] = (xhat * gain_ref[...] + shift_ref[...]).astype(BF)
            for k in range(3):
                to_z(back, m, i, k, h).start()
            to_sibling(back, m, i, 3, h).start()

    def relay(back, i):
        m = i // 2
        for h in range(PARTS):
            for k in range(3):
                from_z(back, m, i, k, h).wait_recv()
                to_sibling(back, m, i, k, h).start()

    def await_rows(back, i):
        m = i // 2

        @pl.when(lax.rem(i, 2) != core)
        def _():
            for h in range(PARTS):
                for k in range(4):
                    to_sibling(back, m, i, k, h).wait_recv()

    def part_at(i):
        return (1 - lax.rem(i + core, 2)) * (i // 2) + lax.rem(i + core, 2) * (2 + i // 2)

    def to_pair(back, i, q):
        m = i // 2
        span = pl.ds(q * (D // 2), D // 2)
        return remote(
            part.at[2 + m, :, span], got.at[m, :, span], par_s.at[back, m, q], par_r.at[back, m, q], me.sibling
        )

    def sum_to_z(back, m, k, h):
        peer = me.z_peer(1 + k)
        at = PARTS * k + h
        return remote(
            part.at[m, band(peer["tensor"], h)],
            zgot.at[back * 2 + m, k, pl.ds(h * PART, PART)],
            rsz_s.at[back, m, at],
            rsz_r.at[back, m, at],
            peer,
        )

    def pair_add(back, m):
        for q in range(2):
            span = slice(q * (D // 2), (q + 1) * (D // 2))
            to_pair(back, 2 * m + core, q).wait_recv()
            part[m, :, span] = (part[m, :, span].astype(F32) + got[m, :, span].astype(F32)).astype(BF)

        @pl.when(section == back)
        def _():
            pl.semaphore_signal(pair_free.at[m], inc=1, device_id=me.sibling, device_id_type=MESH)

    def pair_spread(back, m):
        for h in range(PARTS):
            for k in range(3):
                sum_to_z(back, m, k, h).start()

    def pair_sum(back, m):
        pair_add(back, m)
        pair_spread(back, m)

    def pair_sent(back, m):
        for h in range(PARTS):
            for k in range(3):
                sum_to_z(back, m, k, h).wait_send()

    def row_sum(back, m, h):
        total = part[m, band(z, h)].astype(F32)
        for k in range(3):
            sum_to_z(back, m, k, h).wait_recv()
            total = total + zgot[back * 2 + m, k, parts[h]].astype(F32)
        return total

    def onward(back, m, h):
        target = grow if back else xrow
        span = pl.ds(h * PART, PART)
        return remote(
            zgot.at[back * 2 + m, 0, span],
            target.at[m, span],
            sec_s.at[back, m, h],
            sec_r.at[back, m, h],
            {"section": 1 - back},
        )

    def keep(back, m):
        target = ig_out if back else lo_out
        return pltpu.make_async_copy(zgot.at[back * 2 + m, 0], target.at[m], keep_s.at[back, m])

    def finish_forward(m):
        for h in range(PARTS):
            total = row_sum(0, m, h) + (ob_ref[...] + db_ref[...])
            zgot[m, 0, parts[h]] = (xrow[m, parts[h]].astype(F32) + total).astype(BF)

            @pl.when(section == 0)
            def _():
                onward(0, m, h).start()

        keep(0, m).start()

    def finish_backward(m):
        for h in range(PARTS):
            grad = row_sum(1, m, h)
            xhat, scale = standard(xrow[m, parts[h]].astype(F32))
            above = grow[m, parts[h]].astype(F32)
            a = grad * gain_ref[...]
            inner = a - jnp.mean(a, axis=-1, keepdims=True) - xhat * jnp.mean(a * xhat, axis=-1, keepdims=True)
            zgot[2 + m, 0, parts[h]] = (above + inner * scale).astype(BF)

            @pl.when(section == 1)
            def _():
                onward(1, m, h).start()

            tally[0, 0:1, :] += jnp.sum(grad * xhat, axis=0, keepdims=True)
            tally[0, 1:2, :] += jnp.sum(grad, axis=0, keepdims=True)
            tally[0, 2:3, :] += jnp.sum(above, axis=0, keepdims=True)

        keep(1, m).start()

    lanes = lax.broadcasted_iota(jnp.int32, (SLOT, 128), 1) % HD
    early = lanes < ROT // 2

    places = lax.broadcasted_iota(jnp.int32, (SLOT, 128), 0)

    def tables(i):
        first = places < split[pl.ds(i, 1), :]
        cosine, sine = cos_ref[...], sin_ref[...]
        cos_at, sin_at = ctab[pl.ds(i, 1), :], stab[pl.ds(i, 1), :]
        return (
            jnp.where(first, cosine, cosine * cos_at + sine * sin_at),
            jnp.where(first, sine, sine * cos_at - cosine * sin_at) * jnp.where(early, -1.0, 1.0),
        )

    def turned(values, table, sign):
        halves = []
        for at in (0, 128):
            piece = values[:, at : at + 128]
            swapped = jnp.where(early, pltpu.roll(piece, 128 - ROT // 2, 1), pltpu.roll(piece, ROT // 2, 1))
            halves.append(piece * table[0] + swapped * (table[1] * sign))
        return jnp.concatenate(halves, axis=1)

    def head_mask(head):
        lane = lax.broadcasted_iota(jnp.int32, (1, MIX), 1)
        return jnp.where(lane // HD == head, 1.0, 0.0).astype(BF)

    def forward_first(i):
        rows = normed[slot(i)]
        projected = dot(rows, wa[:, 0:QKV]) + bias[0:1, 0:QKV]
        table = tables(i)
        queries = turned(projected[:, 0:MIX], table, 1.0).astype(BF)
        keys = turned(projected[:, MIX : 2 * MIX], table, 1.0).astype(BF)
        values = projected[:, 2 * MIX : 3 * MIX].astype(BF)
        qkv[slot(i), 0:MIX] = queries
        qkv[slot(i), MIX : 2 * MIX] = keys
        qkv[slot(i), 2 * MIX : 3 * MIX] = values
        at = split[pl.ds(i, 1), :]
        at = jnp.concatenate([at, at], axis=1)
        row_at = lax.broadcasted_iota(jnp.int32, (SLOT, SLOT), 0)
        key_at = lax.broadcasted_iota(jnp.int32, (SLOT, SLOT), 1)
        same = jnp.where(row_at < at, 1, 0) == jnp.where(key_at < at, 1, 0)
        allowed = (key_at <= row_at) & same
        mixed = jnp.zeros((SLOT, MIX), F32)
        for head in range(4):
            mask = head_mask(head)
            scores = jnp.where(allowed, dot_nt(queries * mask, keys) * HD**-0.5, -1e30)
            weights = jnp.exp(scores - jnp.max(scores, axis=-1, keepdims=True))
            chances = (weights / jnp.sum(weights, axis=-1, keepdims=True)).astype(BF)
            probs[i, head] = chances
            mixed = mixed + dot(chances, values * mask)
        hcat[slot(i), 0:MIX] = mixed.astype(BF)
        v = dot(rows, wa[:, QKV:A_COLS]) + bias[0:1, QKV:A_COLS]
        root = np.sqrt(2 / np.pi).astype(np.float32)
        square = v * v
        bent = jnp.tanh(root * (v + 0.044715 * (square * v)))
        half = 0.5 * (1.0 + bent)
        hcat[slot(i), MIX:B_COLS] = (v * half).astype(BF)
        slope[slot(i)] = (half + 0.5 * v * (1.0 - bent * bent) * (root * (1.0 + 3 * 0.044715 * square))).astype(BF)

    def second_turn(back, i):
        @pl.when((lax.rem(i, 2) != core) & (section != back))
        def _():
            pl.semaphore_wait(pair_free.at[i // 2], 1)
            for q in range(2):
                to_pair(1 - back, i, q).wait_send()

    def forward_second(i):
        second_turn(0, i)
        for q in range(2):
            span = slice(q * (D // 2), (q + 1) * (D // 2))
            part[part_at(i), :, span] = dot(hcat[slot(i)], wb[:, span]).astype(BF)

            @pl.when(lax.rem(i, 2) != core)
            def _():
                to_pair(0, i, q).start()

    def backward_first(i):
        grad_hidden = dot_nt(grads[slot(i)], wb[...])
        grad_pre = (grad_hidden[:, MIX:B_COLS] * slope[slot(i)].astype(F32)).astype(BF)
        gproj[slot(i), QKV:A_COLS] = grad_pre
        sum_a[0:1, QKV:A_COLS] += jnp.sum(grad_pre.astype(F32), axis=0, keepdims=True)
        grad_mixed = grad_hidden[:, 0:MIX].astype(BF)
        queries = qkv[slot(i), 0:MIX]
        keys = qkv[slot(i), MIX : 2 * MIX]
        values = qkv[slot(i), 2 * MIX : 3 * MIX]
        zero = jnp.zeros((SLOT, MIX), F32)
        grad_queries, grad_keys, grad_values = zero, zero, zero
        for head in range(4):
            mask = head_mask(head)
            chances = probs[i, head]
            masked = grad_mixed * mask
            grad_values = grad_values + dot_tn(chances, masked)
            grad_probs = dot_nt(masked, values)
            wide = chances.astype(F32)
            centre = jnp.sum(wide * grad_probs, axis=-1, keepdims=True)
            grad_scores = (wide * (grad_probs - centre)).astype(BF)
            grad_queries = grad_queries + dot(grad_scores, keys * mask)
            grad_keys = grad_keys + dot_tn(grad_scores, queries * mask)
        table = tables(i)
        pieces = (
            turned(grad_queries * HD**-0.5, table, -1.0).astype(BF),
            turned(grad_keys * HD**-0.5, table, -1.0).astype(BF),
            grad_values.astype(BF),
        )
        for at, piece in enumerate(pieces):
            span = slice(at * MIX, (at + 1) * MIX)
            gproj[slot(i), span] = piece
            sum_a[0:1, span] += jnp.sum(piece.astype(F32), axis=0, keepdims=True)

    def backward_second(i):
        second_turn(1, i)
        for q in range(2):
            span = slice(q * (D // 2), (q + 1) * (D // 2))
            part[part_at(i), :, span] = dot_nt(gproj[slot(i)], wa[span, :]).astype(BF)

            @pl.when(lax.rem(i, 2) != core)
            def _():
                to_pair(1, i, q).start()

    for copy in holds + gives:
        copy.start()
    ours[...] = jnp.zeros_like(ours)
    for m in range(2):
        ours[m : m + 1, :] = jnp.broadcast_to(mine_ref[0:1, m : m + 1], (1, 128))
    tell.start()

    @pl.when(section == 0)
    def _():
        rows_in[0].start()

    @pl.when(section == 1)
    def _():
        rows_in[1].start()

    sum_a[...] = jnp.zeros_like(sum_a)
    tally[0] = jnp.zeros((8, D), F32)
    for at in range(4):
        holds[at].wait()
        takes[at].wait_recv()
    own_first(0)
    own_second(0)

    @pl.when(section == 0)
    def _():
        rows_in[0].wait()
        for m in range(2):
            spread_own(0, m, False)

    @pl.when(section == 1)
    def _():
        rows_in[1].wait()
        for m in range(2):
            spread_own(1, m, False)

    for at in (4, 5):
        holds[at].wait()
        takes[at].wait_recv()
    for at in range(3):
        bias[0:1, at * MIX : (at + 1) * MIX] = jnp.where(
            core == 0, qb_ref[at, 0:1, 0:MIX], qb_ref[at, 0:1, MIX : 2 * MIX]
        )
    bias[0:1, QKV:A_COLS] = jnp.where(core == 0, ub_ref[0:1, 0:UP], ub_ref[0:1, UP : 2 * UP])
    tell.wait_recv()
    for i in range(4):
        at = jnp.where(core == i % 2, ours[i // 2 : i // 2 + 1, :], theirs[i // 2 : i // 2 + 1, :])
        split[i : i + 1, :] = at
        here = places == at
        ctab[i : i + 1, :] = jnp.sum(jnp.where(here, cos_ref[...], 0.0), axis=0, keepdims=True)
        stab[i : i + 1, :] = jnp.sum(jnp.where(here, sin_ref[...], 0.0), axis=0, keepdims=True)

    pass_near(0)
    pass_crossed(0)

    def relay_early(m):
        @pl.when(section == 0)
        def _():
            relay(0, 2 * m + core)

        @pl.when(section == 1)
        def _():
            relay(1, 2 * m + core)

    relay_early(0)
    pass_on(0)
    own_first(1)
    pass_far(0)
    relay_early(1)
    pass_on_crossed(0)
    own_second(1)
    settle(0)
    pass_near(1)

    def forward_early(i):
        @pl.when(section == 0)
        def _():
            await_rows(0, i)
            forward_first(i)

    forward_early(0)
    pass_crossed(1)
    forward_early(1)
    pass_on(1)
    pass_far(1)
    forward_early(2)
    forward_early(3)
    pass_on_crossed(1)
    settle(1)

    def finish_forward_all():
        for m in range(2):
            finish_forward(m)

    @pl.when(section == 0)
    def _():
        def step(i, _):
            forward_second(i)

            @pl.when(i == 1 + core)
            def _():
                pair_sum(0, 0)

            return 0

        lax.fori_loop(0, 4, step, 0)
        pair_sum(0, 1)
        finish_forward_all()

        @pl.when(core == 0)
        def _():
            spread_own(1, 0, True)
            relay(1, 0)

    @pl.when(section == 1)
    def _():
        spread_own(0, 0, True)

        @pl.when(core == 0)
        def _():
            relay(0, 0)

    def turn_of(k):
        return lax.rem(y + 2 + 3 * k + 3 * (k // 2) + 2 * (k // 3), 4)

    a_cuts = ((0, A_HALF), (A_HALF, A_COLS))
    b_cuts = ((0, B_HALF), (B_HALF, B_COLS))

    def term_a(y_at, x_at, half):
        lo, hi = a_cuts[half]
        return dot_tn(normed[:, chip_span(y_at, x_at)], gproj[:, lo:hi])

    def term_b(y_at, x_at, half):
        lo, hi = b_cuts[half]
        return dot_tn(hcat[:, lo:hi], grads[:, chip_span(y_at, x_at)])

    def cross(k):
        span = pl.ds(pl.multiple_of(k * MIX, MIX), MIX)
        there = pl.ds(pl.multiple_of((4 + k) * 256, 256), 256)
        return (
            remote(probs.at[k, 0], wb.at[pl.ds(0, MIX), there], xs.at[k, 0], xr.at[k, 0], me.across),
            remote(slope.at[:, span], wb.at[pl.ds(MIX, UP), there], xs.at[k, 1], xr.at[k, 1], me.across),
        )

    def cross_all():
        pl.semaphore_wait(free_sem, 1)

        def step(k, _):
            span = pl.ds(pl.multiple_of(k * MIX, MIX), MIX)
            total = term_b(turn_of(k), 1 - x, 0).astype(BF)
            probs[k, 0] = total[0:MIX]
            slope[0 : B_HALF - MIX, span] = total[MIX:B_HALF]
            slope[B_HALF - MIX : UP, span] = term_b(turn_of(k), 1 - x, 1).astype(BF)
            for copy in cross(k):
                copy.start()
            return 0

        lax.fori_loop(0, 4, step, 0)

    def crossed(k):
        for copy in cross(k):
            copy.wait_recv()

    def from_across(k, half):
        lo, hi = b_cuts[half]
        return wb[lo:hi, (4 + k) * 256 : (5 + k) * 256].astype(F32)

    def a_place(at):
        return wa.at[pl.ds(pl.multiple_of(at * 256, 256), 256)]

    def b_place(at):
        return wb.at[:, pl.ds(at * 256, 256)]

    a_spans = (pl.ds(0, A_HALF), pl.ds(A_HALF, A_HALF))
    b_spans = (pl.ds(0, B_HALF), pl.ds(B_HALF, B_HALF))

    def far_piece(way, x_at):
        source = far_a.at[x_at, :, a_spans[way]]
        return remote(source, half_a.at[way, x_at], fs.at[way, x_at], fr.at[way, x_at], me.beside(1 - 2 * way))

    def far_piece_b(way):
        source = wb.at[b_spans[way], pl.ds(0, 256)]
        return remote(source, half_b.at[way], fs.at[way, 2], fr.at[way, 2], me.beside(1 - 2 * way))

    def near_piece(way, x_at):
        source = a_place(2 + 2 * way + x_at)
        return remote(source, got_a.at[way, x_at], ns.at[way, x_at], nr.at[way, x_at], me.beside(1 - 2 * way))

    def near_piece_b(way):
        return remote(b_place(1 + way), got_b.at[way], ns.at[way, 2], nr.at[way, 2], me.beside(1 - 2 * way))

    def cross_last():
        return remote(a_place(6), xa_in, xs.at[4, 0], xr.at[4, 0], me.across)

    def send_far_all():
        def step(k, _):
            x_at = (1 - k) * (1 - x) + k * x
            for way, (lo, hi) in enumerate(a_cuts):
                far_a[x_at, :, lo:hi] = term_a(far, x_at, way).astype(BF)
                far_piece(way, x_at).start()
            return 0

        lax.fori_loop(0, 2, step, 0)

    def send_near(way, x_at):
        target = pl.ds(pl.multiple_of((2 + 2 * way + x_at) * 256, 256), 256)
        for half in (1 - way, way):
            lo, hi = a_cuts[half]
            total = term_a(me.turn(1 - 2 * way), x_at, half)
            if half == way:
                far_piece(way, x_at).wait_recv()
                total = total + half_a[way, x_at].astype(F32)
            wa[target, lo:hi] = total.astype(BF)
        start(near_piece(way, x_at))

    def send_far_b():
        for way, (lo, hi) in enumerate(b_cuts):
            total = term_b(far, x, way)
            if way == 0:
                crossed(0)
            wb[lo:hi, 0:256] = (total + from_across(0, way)).astype(BF)
            start(far_piece_b(way))

    def send_near_b(way):
        span = slice((1 + way) * 256, (2 + way) * 256)
        for half in (1 - way, way):
            lo, hi = b_cuts[half]
            total = term_b(me.turn(1 - 2 * way), x, half)
            if half != way:
                crossed(1 + way)
            total = total + from_across(1 + way, half)
            if half == way:
                far_piece_b(way).wait_recv()
                total = total + half_b[way].astype(F32)
            wb[lo:hi, span] = total.astype(BF)
        start(near_piece_b(way))

    def arrived_a(x_at, at):
        for half, (lo, hi) in enumerate(a_cuts):
            total = term_a(y, x_at, half)
            for way in (0, 1):
                if half == 0:
                    near_piece(way, x_at).wait_recv()
                total = total + got_a[way, x_at, :, lo:hi].astype(F32)
            wa[at * 256 : (at + 1) * 256, lo:hi] = total.astype(BF)

    def begun_b(at):
        crossed(3)
        for half, (lo, hi) in enumerate(b_cuts):
            wb[lo:hi, at * 256 : (at + 1) * 256] = (term_b(y, x, half) + from_across(3, half)).astype(BF)

    def arrived_b(at):
        span = slice(at * 256, (at + 1) * 256)
        total = wb[:, span].astype(F32)
        for way in (0, 1):
            near_piece_b(way).wait_recv()
            total = total + got_b[way].astype(F32)
        wb[:, span] = total.astype(BF)

    near_z = {"tensor": z + 1 - 2 * lax.rem(z, 2)}
    near_y = {"dp": me.at(y + 1 - 2 * lax.rem(y, 2), x, core)}
    partners = (near_z, me.z_peer(2), me.sibling, me.across, near_y, me.beside(2))

    def exchange(step):
        return remote(tally.at[step], came.at[step], ts.at[step], tr.at[step], partners[step])

    def fold(step):
        exchange(step).wait_recv()
        total = tally[step] + came[step]
        if step < 3:
            tally[step + 1, 0:3] = total[0:3]
            tally[step + 1, 3:8] = tally[step, 3:8]
            if step == 2:
                tally[step + 1, 4:5] = came[step, 3:4]
        else:
            tally[step + 1] = total
        if step < 5:
            start(exchange(step + 1))

    for copy in sent:
        copy.wait_send()
    sent.clear()

    def forward_step(i):
        away = lax.rem(i, 2) != core

        @pl.when((i == 1) & (core == 1))
        def _():
            spread_own(0, 1, True)

        await_rows(0, i)
        forward_first(i)

        @pl.when((i < 3) & away)
        def _():
            relay(0, i + 1)

    def backward_step(i):
        own = lax.rem(i, 2) == core

        @pl.when((section == 0) & (i < 3) & jnp.logical_not(own))
        def _():
            spread_own(1, (i + 1) // 2, True)

        await_rows(1, i)
        backward_first(i)

        @pl.when((section == 1) & (i == 0) & (core == 0))
        def _():
            spread_own(0, 1, True)

        @pl.when((section == 0) & (i == 3))
        def _():
            pl.semaphore_signal(free_sem, inc=1, device_id=me.across, device_id_type=MESH)
            send_far_all()
            cross_all()

        @pl.when((section == 1) & (i >= 1) & jnp.logical_not(own))
        def _():
            pair_sum(1, (i - 1) // 2)

        @pl.when((section == 1) & (i >= 2) & own)
        def _():
            finish_backward(0)

        @pl.when((section == 0) & own)
        def _():
            pair_sent(0, i // 2)

        backward_second(i)

        @pl.when((section == 0) & (i < 3) & jnp.logical_not(own))
        def _():
            relay(1, i + 1)

    def joint_step(j, _):
        @pl.when((section == 1) & (j < 4))
        def _():
            forward_step(j)

        @pl.when(j != 2)
        def _():
            backward_step(j - j // 3)

        return 0

    lax.fori_loop(0, 5, joint_step, 0)

    @pl.when(section == 1)
    def _():
        @pl.when(core == 1)
        def _():
            pair_sum(1, 1)

        finish_backward(1)
        for m in range(2):
            pair_sent(1, m)

        def late_step(i, _):
            forward_second(i)
            return 0

        lax.fori_loop(0, 4, late_step, 0)
        pl.semaphore_signal(free_sem, inc=1, device_id=me.across, device_id_type=MESH)
        send_far_all()
        cross_all()

    for back in range(2):

        @pl.when(section != back)
        def _():
            for m in range(2):
                pair_sum(back, m)

    send_far_b()
    for x_at in (1 - x, x):
        for way in (0, 1):
            send_near(way, x_at)

    @pl.when(section == 0)
    def _():
        for m in range(2):
            finish_backward(m)

    @pl.when(section == 1)
    def _():
        finish_forward_all()

    tally[0, 3:4, 0:A_COLS] = sum_a[0:1]
    start(exchange(0))
    send_near_b(0)
    fold(0)
    fold(1)
    send_near_b(1)
    fold(2)
    arrived_a(1 - x, 6)
    start(cross_last())
    arrived_a(x, 7)
    begun_b(3)
    fold(3)

    def result(half, peer, at):
        rows = pl.ds(pl.multiple_of(7 * 256 + half * 128, 128), 128)
        cols = pl.ds(pl.multiple_of(3 * 256 + half * 128, 128), 128)
        sources = [wa.at[rows, pl.ds(k * MIX, MIX)] for k in range(3)]
        sources += [wa.at[rows, pl.ds(QKV, UP)], wb.at[pl.ds(0, MIX), cols], wb.at[pl.ds(MIX, UP), cols]]
        targets = [gq_out.at[k, :, place(at, MIX)] for k in range(3)]
        targets += [gu_out.at[:, place(at, UP)], go_out.at[place(at, MIX), :], gd_out.at[place(at, UP), :]]
        if peer:
            return [
                remote(source, target, end_s.at[k], end_r.at[k], me.sibling)
                for k, (source, target) in enumerate(zip(sources, targets))
            ]
        return [
            pltpu.make_async_copy(source, target, end_k.at[k])
            for k, (source, target) in enumerate(zip(sources, targets))
        ]

    outgoing, staying = result(1 - core, True, core), result(core, False, core)
    incoming = result(1 - core, True, 1 - core)
    cross_last().wait_recv()
    wa[7 * 256 : 8 * 256] = (wa[7 * 256 : 8 * 256].astype(F32) + xa_in[...].astype(F32)).astype(BF)
    for at in range(4):
        outgoing[at].start()
        staying[at].start()
    fold(4)
    arrived_b(3)
    for at in (4, 5):
        outgoing[at].start()
        staying[at].start()
    fold(5)
    sums_ref[...] = tally[6]
    for at in range(3):
        span = slice(at * MIX, (at + 1) * MIX)
        ours_a, others_a = tally[6, 3:4, span], tally[6, 4:5, span]
        gqb_ref[at : at + 1, 0:MIX] = jnp.where(core == 0, ours_a, others_a)
        gqb_ref[at : at + 1, MIX : 2 * MIX] = jnp.where(core == 0, others_a, ours_a)
    ours_a, others_a = tally[6, 3:4, QKV:A_COLS], tally[6, 4:5, QKV:A_COLS]
    gub_ref[0:1, 0:UP] = jnp.where(core == 0, ours_a, others_a)
    gub_ref[0:1, UP : 2 * UP] = jnp.where(core == 0, others_a, ours_a)

    for copy in sent + gives + [tell]:
        copy.wait_send()
    for k in range(4):
        for copy in cross(k):
            copy.wait_send()
    for way in range(2):
        for x_at in range(2):
            far_piece(way, x_at).wait_send()
    for back in range(2):
        for m in range(2):
            mine = 2 * m + core
            for h in range(PARTS):
                for k in range(3):
                    to_z(back, m, mine, k, h).wait_send()
                for k in range(4):
                    to_sibling(back, m, mine, k, h).wait_send()
            keep(back, m).wait()

        @pl.when(section == back)
        def _():
            for m in range(2):
                for h in range(PARTS):
                    onward(back, m, h).wait_send()

        @pl.when(section != back)
        def _():
            for m in range(2):
                pair_sent(back, m)
                for q in range(2):
                    to_pair(back, 2 * m + 1 - core, q).wait_send()

    for at in range(6):
        staying[at].wait()
        outgoing[at].wait_send()
        incoming[at].wait_recv()


def both_layers(rows_in, cotangent, qkv_w, up_w, out_w, down_w, bias_qkv, bias_up, bias_out, bias_down, gain, shift, mine):
    places = np.arange(SLOT, dtype=np.float32)
    frequency = (10000.0 ** (-(np.arange(ROT // 2, dtype=np.float32) * np.float32(2.0 / ROT)))).astype(np.float32)
    angles = (places[:, None] * frequency[None, :]).astype(np.float32).astype(np.float64)
    cosine = np.ones((SLOT, HD), np.float32)
    sine = np.zeros((SLOT, HD), np.float32)
    cosine[:, 0:ROT] = np.tile(np.cos(angles), (1, 2))
    sine[:, 0:ROT] = np.tile(np.sin(angles), (1, 2))
    cosine, sine = (jnp.asarray(np.tile(table, (1, 2))) for table in (cosine, sine))
    any_ = pl.BlockSpec(memory_space=pl.ANY)
    vmem = pl.BlockSpec(memory_space=pltpu.VMEM)
    dma = pltpu.SemaphoreType.DMA
    shape = jax.ShapeDtypeStruct
    return pl.pallas_call(
        layers_kernel,
        out_shape=(
            shape((2, ROWS, D), BF),
            shape((2, ROWS, D), BF),
            shape((3, 128, 2 * MIX), BF),
            shape((128, 2 * UP), BF),
            shape((2 * MIX, 128), BF),
            shape((2 * UP, 128), BF),
            shape((8, D), F32),
            shape((3, 2 * MIX), F32),
            shape((1, 2 * UP), F32),
        ),
        in_specs=[any_] * 6 + [vmem] * 9,
        out_specs=[any_] * 6 + [vmem] * 3,
        scratch_shapes=[
            pltpu.VMEM((D, A_COLS), BF),
            pltpu.VMEM((B_COLS, D), BF),
            pltpu.VMEM((ALL, D), BF),
            pltpu.VMEM((ALL, D), BF),
            pltpu.VMEM((ALL, QKV), BF),
            pltpu.VMEM((ALL, B_COLS), BF),
            pltpu.VMEM((ALL, UP), BF),
            pltpu.VMEM((4, 4, SLOT, SLOT), BF),
            pltpu.VMEM((ALL, A_COLS), BF),
            pltpu.VMEM((4, SLOT, D), BF),
            pltpu.VMEM((2, SLOT, D), BF),
            pltpu.VMEM((4, 3, ROWS, D), BF),
            pltpu.VMEM((2, ROWS, D), BF),
            pltpu.VMEM((2, ROWS, D), BF),
            pltpu.VMEM((8, 128), F32),
            pltpu.VMEM((8, 128), F32),
            pltpu.VMEM((8, 128), jnp.int32),
            pltpu.VMEM((8, 128), jnp.int32),
            pltpu.VMEM((8, 128), jnp.int32),
            pltpu.VMEM((8, A_COLS), F32),
            pltpu.VMEM((2, 256, A_COLS), BF),
            pltpu.VMEM((2, 2, 256, A_HALF), BF),
            pltpu.VMEM((2, B_HALF, 256), BF),
            pltpu.VMEM((2, 2, 256, A_COLS), BF),
            pltpu.VMEM((2, B_COLS, 256), BF),
            pltpu.VMEM((256, A_COLS), BF),
            pltpu.VMEM((8, A_COLS), F32),
            pltpu.VMEM((7, 8, D), F32),
            pltpu.VMEM((6, 8, D), F32),
            dma((7,)),
            dma((2, 10)),
            dma((2, 10)),
            dma((2, 2, 9)),
            dma((2, 2, 9)),
            dma((7,)),
            dma((7,)),
            dma((2, 2, 3 * PARTS)),
            dma((2, 2, 3 * PARTS)),
            dma((2, 2, 4 * PARTS)),
            dma((2, 2, 4 * PARTS)),
            dma((2, 2, 2)),
            dma((2, 2, 2)),
            dma((2, 2, 3 * PARTS)),
            dma((2, 2, 3 * PARTS)),
            dma((2, 2, PARTS)),
            dma((2, 2, PARTS)),
            dma((5, 2)),
            dma((5, 2)),
            dma((2, 3)),
            dma((2, 3)),
            dma((2, 3)),
            dma((2, 3)),
            dma((6,)),
            dma((6,)),
            dma((6,)),
            dma((6,)),
            dma((6,)),
            dma((2, 2)),
            pltpu.SemaphoreType.REGULAR,
            pltpu.SemaphoreType.REGULAR((2,)),
        ],
        compiler_params=pltpu.CompilerParams(
            collective_id=1, has_side_effects=True, vmem_limit_bytes=VMEM_LIMIT
        ),
        name="both_layers",
    )(
        rows_in, cotangent, qkv_w, up_w, out_w, down_w,
        bias_qkv, bias_up, bias_out, bias_down, gain, shift, mine, cosine, sine,
    )


def widen_kernel(lo, ig, gq, gu, go, gd, sums, gqb, gub, *outs):
    lo_out, ig_out, gq_out, gu_out, go_out, gd_out, gain, shift, out_b, down_b, qkv_b, up_b = outs
    lo_out[...] = lo[...]
    ig_out[...] = ig[...]
    gq_out[...] = gq[...].astype(F32)
    gu_out[...] = gu[...].astype(F32)
    go_out[...] = go[...].astype(F32)
    gd_out[...] = gd[...].astype(F32)
    gain[...] = sums[0:1]
    shift[...] = sums[1:2]
    out_b[...] = sums[2:3]
    down_b[...] = sums[2:3]
    for k in range(3):
        qkv_b[k] = gqb[k : k + 1]
    up_b[...] = gub[...]


def widened(lo, ig, gq, gu, go, gd, sums, gqb, gub):
    steps = 4
    shape = jax.ShapeDtypeStruct

    def cut(whole, dim):
        block = tuple(size // steps if at == dim else size for at, size in enumerate(whole))
        return pl.BlockSpec(block, lambda i: tuple(i if at == dim else 0 for at in range(len(whole))))

    def same(whole):
        return pl.BlockSpec(whole, lambda i: (0,) * len(whole))

    large = [cut(lo.shape, 1), cut(ig.shape, 1), cut(gq.shape, 1), cut(gu.shape, 0), cut(go.shape, 0), cut(gd.shape, 0)]
    small = [(1, D)] * 4 + [(3, 1, 2 * MIX), (1, 2 * UP)]
    return pl.pallas_call(
        widen_kernel,
        grid=(steps,),
        out_shape=(
            [shape(lo.shape, BF), shape(ig.shape, BF)]
            + [shape(each.shape, F32) for each in (gq, gu, go, gd)]
            + [shape(each, F32) for each in small]
        ),
        in_specs=large + [same(sums.shape), same(gqb.shape), same(gub.shape)],
        out_specs=large + [same(each) for each in small],
        compiler_params=pltpu.CompilerParams(vmem_limit_bytes=VMEM_LIMIT),
        name="widened",
    )(lo, ig, gq, gu, go, gd, sums, gqb, gub)


def shards(
    inputs,
    cotangent,
    doc_split,
    qkv_weight,
    qkv_bias,
    out_weight,
    out_bias,
    fc1_weight,
    fc1_bias,
    fc2_weight,
    fc2_bias,
    ln_gain,
    ln_bias,
):
    results = both_layers(
        inputs[:, 0],
        cotangent[:, 0],
        qkv_weight[0].transpose(1, 0, 2),
        fc1_weight[0],
        out_weight[0],
        fc2_weight[0],
        qkv_bias[0][:, None, :],
        fc1_bias,
        out_bias,
        fc2_bias,
        ln_gain,
        ln_bias,
        doc_split.reshape(1, 2),
    )
    layer_out, input_grad, grad_qkv, grad_up, grad_out, grad_down, gain, shift, out_b, down_b, qkv_b, up_b = widened(
        *results
    )
    return (
        layer_out[None, :, None],
        input_grad[None, :, None],
        grad_qkv.transpose(1, 0, 2)[None],
        qkv_b.transpose(1, 0, 2),
        grad_out[None],
        out_b,
        grad_up[None],
        up_b,
        grad_down[None],
        down_b,
        gain,
        shift,
    )


def solution(mesh):
    rows = P(None, "dp", "tensor", None)
    placed_weights = (
        P("section", "dp", None, "tensor"),
        P("section", None, "tensor"),
        P("section", "tensor", "dp"),
        P("section", None),
        P("section", "dp", "tensor"),
        P("section", "tensor"),
        P("section", "tensor", "dp"),
        P("section", None),
        P("section", None),
        P("section", None),
    )
    out_rows = P("section", None, "dp", "tensor", None)
    return jax.shard_map(
        shards,
        mesh=mesh,
        in_specs=(rows, rows, P(None, "dp")) + placed_weights,
        out_specs=(out_rows, out_rows) + placed_weights,
        check_vma=False,
    )
```

```python
from functools import partial

import jax
import jax.numpy as jnp
import numpy as np
from jax import lax
from jax.experimental import pallas as pl
from jax.experimental.pallas import tpu as pltpu
from jax.sharding import PartitionSpec as P

HD = 64
ROT = 32
EPSILON = 1e-05
MESH = pl.DeviceIdType.MESH
BF = jnp.bfloat16
F32 = jnp.float32

D = 2048
SLOT = 256
ROWS = 64
PARTS = 4
PART = ROWS // PARTS
QKV = 768
UP = 1024
A_COLS = QKV + UP
MIX = 256
B_COLS = MIX + UP
A_HALF = A_COLS // 2
B_HALF = B_COLS // 2
ALL = 4 * SLOT
VMEM_LIMIT = 62 * 2**20


def dot(a, b):
    return lax.dot_general(a, b, (((1,), (0,)), ((), ())), preferred_element_type=F32)


def dot_nt(a, b):
    return lax.dot_general(a, b, (((1,), (1,)), ((), ())), preferred_element_type=F32)


def dot_tn(a, b):
    return lax.dot_general(a, b, (((0,), (0,)), ((), ())), preferred_element_type=F32)


def remote(src, dst, send, recv, device):
    return pltpu.make_async_remote_copy(
        src_ref=src, dst_ref=dst, send_sem=send, recv_sem=recv, device_id=device, device_id_type=MESH
    )


def greet(peers):
    barrier = pltpu.get_barrier_semaphore()
    for peer in peers:
        pl.semaphore_signal(barrier, inc=1, device_id=peer, device_id_type=MESH)
    pl.semaphore_wait(barrier, len(peers))


class Place:
    def __init__(self):
        self.dp = lax.axis_index("dp")
        self.core = lax.rem(self.dp, 2)
        self.x = lax.rem(self.dp // 2, 2)
        self.y = self.dp // 4
        self.z = lax.axis_index("tensor")
        self.sibling = {"dp": self.dp + 1 - 2 * self.core}
        self.across = {"dp": self.at(self.y, 1 - self.x, self.core)}

    def at(self, y, x, core):
        return (y * 2 + x) * 2 + core

    def turn(self, by):
        return lax.rem(self.y + 4 + by, 4)

    def beside(self, by):
        return {"dp": self.at(self.turn(by), self.x, self.core)}

    def z_peer(self, by):
        return {"tensor": lax.rem(self.z + by, 4)}


STAGES = (
    ((0, 512), (512, 512), (1024, 384), (1408, 384)),
    ((0, 384), (384, 384), (768, 256), (1024, 256)),
)


def layers_kernel(
    x_hbm, cot_hbm, qkv_hbm, up_hbm, ow_hbm, dw_hbm,
    qb_ref, ub_ref, ob_ref, db_ref, gain_ref, shift_ref, mine_ref, cos_ref, sin_ref,
    lo_out, ig_out, gq_out, gu_out, go_out, gd_out, sums_ref, gqb_ref, gub_ref,
    wa, wb, normed, grads, qkv, hcat, slope, probs, gproj, part, got, zgot, xrow, grow, ctab, stab, split, ours, theirs, bias,
    far_a, half_a, half_b, got_a, got_b, xa_in, sum_a, tally, came,
    own_sem, x_send, x_recv, y_send, y_recv, sib_send, sib_recv,
    agz_s, agz_r, ags_s, ags_r, par_s, par_r, rsz_s, rsz_r, sec_s, sec_r,
    xs, xr, fs, fr, ns, nr, ts, tr, end_s, end_r, end_k, keep_s, free_sem, pair_free,
):
    me = Place()
    section = lax.axis_index("section")
    core, z = me.core, me.z
    greet(
        [me.sibling, me.across, me.beside(1), me.beside(-1), me.beside(2)]
        + [me.z_peer(1), me.z_peer(2), me.z_peer(3), {"section": 1 - section}]
    )

    def device_span(dp):
        return pl.ds(pl.multiple_of(dp * 128, 128), 128)

    def chip_span(y_at, x_at):
        return pl.ds(pl.multiple_of((y_at * 2 + x_at) * 256, 256), 256)

    def place(at, size):
        return pl.ds(pl.multiple_of(at * size, size), size)

    def blocks(dp, half):
        span = device_span(dp)
        pairs = [
            (qkv_hbm.at[k, :, place(half, MIX)], wa.at[span, pl.ds(k * MIX, MIX)]) for k in range(3)
        ]
        pairs.append((up_hbm.at[:, place(half, UP)], wa.at[span, pl.ds(QKV, UP)]))
        pairs.append((ow_hbm.at[place(half, MIX), :], wb.at[pl.ds(0, MIX), span]))
        pairs.append((dw_hbm.at[place(half, UP), :], wb.at[pl.ds(MIX, UP), span]))
        return pairs

    other = me.dp + 1 - 2 * core
    holds = [
        pltpu.make_async_copy(source, target, own_sem.at[at])
        for at, (source, target) in enumerate(blocks(me.dp, core))
    ]
    gives = [
        remote(source, target, sib_send.at[at], sib_recv.at[at], me.sibling)
        for at, (source, target) in enumerate(blocks(me.dp, 1 - core))
    ]
    takes = [
        remote(source, target, sib_send.at[at], sib_recv.at[at], me.sibling)
        for at, (source, target) in enumerate(blocks(other, 1 - core))
    ]
    tell = remote(ours, theirs, sib_send.at[6], sib_recv.at[6], me.sibling)
    rows_in = [
        pltpu.make_async_copy(x_hbm, xrow, own_sem.at[6]),
        pltpu.make_async_copy(cot_hbm, grow, own_sem.at[6]),
    ]
    y, x = me.y, me.x
    far = me.turn(2)

    def piece_of(stage, y_at, x_at, which):
        span = pl.ds(*STAGES[stage][which])
        if stage == 0:
            return wa.at[chip_span(y_at, x_at), span]
        return wb.at[span, chip_span(y_at, x_at)]

    def over_x(stage, y_at, x_at, which, slot):
        piece = piece_of(stage, y_at, x_at, which)
        return remote(piece, piece, x_send.at[stage, slot], x_recv.at[stage, slot], me.across)

    def over_y(stage, by, y_at, x_at, which, slot):
        piece = piece_of(stage, y_at, x_at, which)
        way = 0 if by > 0 else 1
        return remote(piece, piece, y_send.at[stage, way, slot], y_recv.at[stage, way, slot], me.beside(by))

    sent = []

    def start(copy):
        copy.start()
        sent.append(copy)

    def own_first(stage):
        for which in (0, 1):
            start(over_x(stage, y, x, which, which))
        for which in (2, 3):
            for by in (1, -1):
                start(over_y(stage, by, y, x, which, which))

    def own_second(stage):
        for which in (2, 3):
            start(over_x(stage, y, x, which, which))
        for which in (0, 1):
            for by in (1, -1):
                start(over_y(stage, by, y, x, which, which))

    def pass_near(stage):
        for which in (2, 3):
            for by in (1, -1):
                source = me.turn(-by)
                over_y(stage, by, source, x, which, which).wait_recv()
                if (which == 2) == (by > 0):
                    start(over_y(stage, by, source, x, which, 6))
                start(over_x(stage, source, x, which, 2 * which + (0 if by > 0 else 1)))

    def pass_crossed(stage):
        for which in (0, 1):
            over_x(stage, y, 1 - x, which, which).wait_recv()
            for by in (1, -1):
                start(over_y(stage, by, y, 1 - x, which, 4 + which))

    def pass_far(stage):
        for which, by in ((2, 1), (3, -1)):
            over_y(stage, by, far, x, which, 6).wait_recv()
            start(over_x(stage, far, x, which, 6 + which))

    def pass_on(stage):
        for which, by in ((0, 1), (1, -1)):
            source = me.turn(-by)
            over_y(stage, by, source, x, which, which).wait_recv()
            start(over_y(stage, by, source, x, which, 7))

    def pass_on_crossed(stage):
        for which, by in ((0, 1), (1, -1)):
            source = me.turn(-by)
            over_y(stage, by, source, 1 - x, which, 4 + which).wait_recv()
            start(over_y(stage, by, source, 1 - x, which, 8))

    def settle(stage):
        for which, by in ((0, -1), (1, 1)):
            source = me.turn(-by)
            over_y(stage, by, source, x, which, which).wait_recv()
            over_y(stage, by, source, 1 - x, which, 4 + which).wait_recv()
        for which in (2, 3):
            over_x(stage, y, 1 - x, which, which).wait_recv()
            for by in (1, -1):
                over_x(stage, me.turn(-by), 1 - x, which, 2 * which + (0 if by > 0 else 1)).wait_recv()
            over_x(stage, far, 1 - x, which, 6 + which).wait_recv()
        for which, by in ((0, 1), (1, -1)):
            over_y(stage, by, far, x, which, 7).wait_recv()
            over_y(stage, by, far, 1 - x, which, 8).wait_recv()

    def band(at, h):
        return pl.ds(pl.multiple_of(at * ROWS + h * PART, PART), PART)

    def slot(i):
        return pl.ds(pl.multiple_of(i * SLOT, SLOT), SLOT)

    def slot_band(i, at, h):
        return pl.ds(pl.multiple_of(i * SLOT + at * ROWS + h * PART, PART), PART)

    parts = [slice(h * PART, (h + 1) * PART) for h in range(PARTS)]

    def standard(rows):
        average = jnp.mean(rows, axis=-1, keepdims=True)
        centred = rows - average
        variance = jnp.mean(centred * centred, axis=-1, keepdims=True)
        scale = lax.rsqrt(variance + EPSILON)
        return centred * scale, scale

    def spread_buffer(back):
        return grads if back else normed

    def to_z(back, m, i, k, h):
        piece = spread_buffer(back).at[slot_band(i, z, h)]
        at = PARTS * k + h
        return remote(piece, piece, agz_s.at[back, m, at], agz_r.at[back, m, at], me.z_peer(1 + k))

    def from_z(back, m, i, k, h):
        piece = spread_buffer(back).at[slot_band(i, lax.rem(z + 3 - k, 4), h)]
        at = PARTS * k + h
        return remote(piece, piece, agz_s.at[back, m, at], agz_r.at[back, m, at], me.z_peer(3 - k))

    def to_sibling(back, m, i, k, h):
        piece = spread_buffer(back).at[slot_band(i, lax.rem(z + 3 - k, 4), h)]
        at = PARTS * k + h
        return remote(piece, piece, ags_s.at[back, m, at], ags_r.at[back, m, at], me.sibling)

    def spread_own(back, m, wait):
        i = 2 * m + core
        for h in range(PARTS):
            if wait:
                onward(1 if back else 0, m, h).wait_recv()
            if back:
                grads[slot_band(i, z, h)] = grow[m, parts[h]]
            else:
                xhat, _ = standard(xrow[m, parts[h]].astype(F32))
                normed[slot_band(i, z, h)] = (xhat * gain_ref[...] + shift_ref[...]).astype(BF)
            for k in range(3):
                to_z(back, m, i, k, h).start()
            to_sibling(back, m, i, 3, h).start()

    def relay(back, i):
        m = i // 2
        for h in range(PARTS):
            for k in range(3):
                from_z(back, m, i, k, h).wait_recv()
                to_sibling(back, m, i, k, h).start()

    def await_rows(back, i):
        m = i // 2

        @pl.when(lax.rem(i, 2) != core)
        def _():
            for h in range(PARTS):
                for k in range(4):
                    to_sibling(back, m, i, k, h).wait_recv()

    def part_at(i):
        return (1 - lax.rem(i + core, 2)) * (i // 2) + lax.rem(i + core, 2) * (2 + i // 2)

    def to_pair(back, i, q):
        m = i // 2
        span = pl.ds(q * (D // 2), D // 2)
        return remote(
            part.at[2 + m, :, span], got.at[m, :, span], par_s.at[back, m, q], par_r.at[back, m, q], me.sibling
        )

    def sum_to_z(back, m, k, h):
        peer = me.z_peer(1 + k)
        at = PARTS * k + h
        return remote(
            part.at[m, band(peer["tensor"], h)],
            zgot.at[back * 2 + m, k, pl.ds(h * PART, PART)],
            rsz_s.at[back, m, at],
            rsz_r.at[back, m, at],
            peer,
        )

    def pair_add(back, m):
        for q in range(2):
            span = slice(q * (D // 2), (q + 1) * (D // 2))
            to_pair(back, 2 * m + core, q).wait_recv()
            part[m, :, span] = (part[m, :, span].astype(F32) + got[m, :, span].astype(F32)).astype(BF)

        @pl.when(section == back)
        def _():
            pl.semaphore_signal(pair_free.at[m], inc=1, device_id=me.sibling, device_id_type=MESH)

    def pair_spread(back, m):
        for h in range(PARTS):
            for k in range(3):
                sum_to_z(back, m, k, h).start()

    def pair_sum(back, m):
        pair_add(back, m)
        pair_spread(back, m)

    def pair_sent(back, m):
        for h in range(PARTS):
            for k in range(3):
                sum_to_z(back, m, k, h).wait_send()

    def row_sum(back, m, h):
        total = part[m, band(z, h)].astype(F32)
        for k in range(3):
            sum_to_z(back, m, k, h).wait_recv()
            total = total + zgot[back * 2 + m, k, parts[h]].astype(F32)
        return total

    def onward(back, m, h):
        target = grow if back else xrow
        span = pl.ds(h * PART, PART)
        return remote(
            zgot.at[back * 2 + m, 0, span],
            target.at[m, span],
            sec_s.at[back, m, h],
            sec_r.at[back, m, h],
            {"section": 1 - back},
        )

    def keep(back, m):
        target = ig_out if back else lo_out
        return pltpu.make_async_copy(zgot.at[back * 2 + m, 0], target.at[m], keep_s.at[back, m])

    def finish_forward(m):
        for h in range(PARTS):
            total = row_sum(0, m, h) + (ob_ref[...] + db_ref[...])
            zgot[m, 0, parts[h]] = (xrow[m, parts[h]].astype(F32) + total).astype(BF)

            @pl.when(section == 0)
            def _():
                onward(0, m, h).start()

        keep(0, m).start()

    def finish_backward(m):
        for h in range(PARTS):
            grad = row_sum(1, m, h)
            xhat, scale = standard(xrow[m, parts[h]].astype(F32))
            above = grow[m, parts[h]].astype(F32)
            a = grad * gain_ref[...]
            inner = a - jnp.mean(a, axis=-1, keepdims=True) - xhat * jnp.mean(a * xhat, axis=-1, keepdims=True)
            zgot[2 + m, 0, parts[h]] = (above + inner * scale).astype(BF)

            @pl.when(section == 1)
            def _():
                onward(1, m, h).start()

            tally[0, 0:1, :] += jnp.sum(grad * xhat, axis=0, keepdims=True)
            tally[0, 1:2, :] += jnp.sum(grad, axis=0, keepdims=True)
            tally[0, 2:3, :] += jnp.sum(above, axis=0, keepdims=True)

        keep(1, m).start()

    lanes = lax.broadcasted_iota(jnp.int32, (SLOT, 128), 1) % HD
    early = lanes < ROT // 2

    places = lax.broadcasted_iota(jnp.int32, (SLOT, 128), 0)

    def tables(i):
        first = places < split[pl.ds(i, 1), :]
        cosine, sine = cos_ref[...], sin_ref[...]
        cos_at, sin_at = ctab[pl.ds(i, 1), :], stab[pl.ds(i, 1), :]
        return (
            jnp.where(first, cosine, cosine * cos_at + sine * sin_at),
            jnp.where(first, sine, sine * cos_at - cosine * sin_at) * jnp.where(early, -1.0, 1.0),
        )

    def turned(values, table, sign):
        halves = []
        for at in (0, 128):
            piece = values[:, at : at + 128]
            swapped = jnp.where(early, pltpu.roll(piece, 128 - ROT // 2, 1), pltpu.roll(piece, ROT // 2, 1))
            halves.append(piece * table[0] + swapped * (table[1] * sign))
        return jnp.concatenate(halves, axis=1)

    def head_mask(head):
        lane = lax.broadcasted_iota(jnp.int32, (1, MIX), 1)
        return jnp.where(lane // HD == head, 1.0, 0.0).astype(BF)

    def forward_first(i):
        rows = normed[slot(i)]
        projected = dot(rows, wa[:, 0:QKV]) + bias[0:1, 0:QKV]
        table = tables(i)
        queries = turned(projected[:, 0:MIX], table, 1.0).astype(BF)
        keys = turned(projected[:, MIX : 2 * MIX], table, 1.0).astype(BF)
        values = projected[:, 2 * MIX : 3 * MIX].astype(BF)
        qkv[slot(i), 0:MIX] = queries
        qkv[slot(i), MIX : 2 * MIX] = keys
        qkv[slot(i), 2 * MIX : 3 * MIX] = values
        v = dot(rows, wa[:, QKV:A_COLS]) + bias[0:1, QKV:A_COLS]
        at = split[pl.ds(i, 1), :]
        at = jnp.concatenate([at, at], axis=1)
        row_at = lax.broadcasted_iota(jnp.int32, (SLOT, SLOT), 0)
        key_at = lax.broadcasted_iota(jnp.int32, (SLOT, SLOT), 1)
        same = jnp.where(row_at < at, 1, 0) == jnp.where(key_at < at, 1, 0)
        allowed = (key_at <= row_at) & same
        mixed = jnp.zeros((SLOT, MIX), F32)
        for head in range(4):
            mask = head_mask(head)
            scores = jnp.where(allowed, dot_nt(queries * mask, keys) * HD**-0.5, -1e30)
            weights = jnp.exp(scores - jnp.max(scores, axis=-1, keepdims=True))
            chances = (weights / jnp.sum(weights, axis=-1, keepdims=True)).astype(BF)
            probs[i, head] = chances
            mixed = mixed + dot(chances, values * mask)
        hcat[slot(i), 0:MIX] = mixed.astype(BF)
        root = np.sqrt(2 / np.pi).astype(np.float32)
        square = v * v
        bent = jnp.tanh(root * (v + 0.044715 * (square * v)))
        half = 0.5 * (1.0 + bent)
        hcat[slot(i), MIX:B_COLS] = (v * half).astype(BF)
        slope[slot(i)] = (half + 0.5 * v * (1.0 - bent * bent) * (root * (1.0 + 3 * 0.044715 * square))).astype(BF)

    def second_turn(back, i):
        @pl.when((lax.rem(i, 2) != core) & (section != back))
        def _():
            pl.semaphore_wait(pair_free.at[i // 2], 1)
            for q in range(2):
                to_pair(1 - back, i, q).wait_send()

    def forward_second(i):
        second_turn(0, i)
        for q in range(2):
            span = slice(q * (D // 2), (q + 1) * (D // 2))
            part[part_at(i), :, span] = dot(hcat[slot(i)], wb[:, span]).astype(BF)

            @pl.when(lax.rem(i, 2) != core)
            def _():
                to_pair(0, i, q).start()

    def backward_first(i):
        grad_hidden = dot_nt(grads[slot(i)], wb[...])
        grad_pre = (grad_hidden[:, MIX:B_COLS] * slope[slot(i)].astype(F32)).astype(BF)
        gproj[slot(i), QKV:A_COLS] = grad_pre
        sum_a[0:1, QKV:A_COLS] += jnp.sum(grad_pre.astype(F32), axis=0, keepdims=True)
        grad_mixed = grad_hidden[:, 0:MIX].astype(BF)
        queries = qkv[slot(i), 0:MIX]
        keys = qkv[slot(i), MIX : 2 * MIX]
        values = qkv[slot(i), 2 * MIX : 3 * MIX]
        zero = jnp.zeros((SLOT, MIX), F32)
        grad_queries, grad_keys, grad_values = zero, zero, zero
        for head in range(4):
            mask = head_mask(head)
            chances = probs[i, head]
            masked = grad_mixed * mask
            grad_values = grad_values + dot_tn(chances, masked)
            grad_probs = dot_nt(masked, values)
            wide = chances.astype(F32)
            centre = jnp.sum(wide * grad_probs, axis=-1, keepdims=True)
            grad_scores = (wide * (grad_probs - centre)).astype(BF)
            grad_queries = grad_queries + dot(grad_scores, keys * mask)
            grad_keys = grad_keys + dot_tn(grad_scores, queries * mask)
        table = tables(i)
        pieces = (
            turned(grad_queries * HD**-0.5, table, -1.0).astype(BF),
            turned(grad_keys * HD**-0.5, table, -1.0).astype(BF),
            grad_values.astype(BF),
        )
        for at, piece in enumerate(pieces):
            span = slice(at * MIX, (at + 1) * MIX)
            gproj[slot(i), span] = piece
            sum_a[0:1, span] += jnp.sum(piece.astype(F32), axis=0, keepdims=True)

    def backward_second(i):
        second_turn(1, i)
        for q in range(2):
            span = slice(q * (D // 2), (q + 1) * (D // 2))
            part[part_at(i), :, span] = dot_nt(gproj[slot(i)], wa[span, :]).astype(BF)

            @pl.when(lax.rem(i, 2) != core)
            def _():
                to_pair(1, i, q).start()

    for copy in holds + gives:
        copy.start()
    ours[...] = jnp.zeros_like(ours)
    for m in range(2):
        ours[m : m + 1, :] = jnp.broadcast_to(mine_ref[0:1, m : m + 1], (1, 128))
    tell.start()

    @pl.when(section == 0)
    def _():
        rows_in[0].start()

    @pl.when(section == 1)
    def _():
        rows_in[1].start()

    sum_a[...] = jnp.zeros_like(sum_a)
    tally[0] = jnp.zeros((8, D), F32)
    for at in range(4):
        holds[at].wait()
        takes[at].wait_recv()
    own_first(0)
    own_second(0)

    @pl.when(section == 0)
    def _():
        rows_in[0].wait()
        for m in range(2):
            spread_own(0, m, False)

    @pl.when(section == 1)
    def _():
        rows_in[1].wait()
        for m in range(2):
            spread_own(1, m, False)

    for at in (4, 5):
        holds[at].wait()
        takes[at].wait_recv()
    for at in range(3):
        bias[0:1, at * MIX : (at + 1) * MIX] = jnp.where(
            core == 0, qb_ref[at, 0:1, 0:MIX], qb_ref[at, 0:1, MIX : 2 * MIX]
        )
    bias[0:1, QKV:A_COLS] = jnp.where(core == 0, ub_ref[0:1, 0:UP], ub_ref[0:1, UP : 2 * UP])
    tell.wait_recv()
    for i in range(4):
        at = jnp.where(core == i % 2, ours[i // 2 : i // 2 + 1, :], theirs[i // 2 : i // 2 + 1, :])
        split[i : i + 1, :] = at
        here = places == at
        ctab[i : i + 1, :] = jnp.sum(jnp.where(here, cos_ref[...], 0.0), axis=0, keepdims=True)
        stab[i : i + 1, :] = jnp.sum(jnp.where(here, sin_ref[...], 0.0), axis=0, keepdims=True)

    pass_near(0)
    pass_crossed(0)

    def relay_early(m):
        @pl.when(section == 0)
        def _():
            relay(0, 2 * m + core)

        @pl.when(section == 1)
        def _():
            relay(1, 2 * m + core)

    relay_early(0)
    pass_on(0)
    own_first(1)
    pass_far(0)
    relay_early(1)
    pass_on_crossed(0)
    own_second(1)
    settle(0)
    pass_near(1)

    def forward_early(i):
        @pl.when(section == 0)
        def _():
            await_rows(0, i)
            forward_first(i)

    forward_early(0)
    pass_crossed(1)
    forward_early(1)
    pass_on(1)
    pass_far(1)
    forward_early(2)
    forward_early(3)
    pass_on_crossed(1)
    settle(1)

    def finish_forward_all():
        for m in range(2):
            finish_forward(m)

    @pl.when(section == 0)
    def _():
        def step(i, _):
            forward_second(i)

            @pl.when(i == 1 + core)
            def _():
                pair_sum(0, 0)

            return 0

        lax.fori_loop(0, 4, step, 0)
        pair_sum(0, 1)
        finish_forward_all()

        @pl.when(core == 0)
        def _():
            spread_own(1, 0, True)
            relay(1, 0)

    @pl.when(section == 1)
    def _():
        spread_own(0, 0, True)

        @pl.when(core == 0)
        def _():
            relay(0, 0)

    def turn_of(k):
        return lax.rem(y + 2 + 3 * k + 3 * (k // 2) + 2 * (k // 3), 4)

    a_cuts = ((0, A_HALF), (A_HALF, A_COLS))
    b_cuts = ((0, B_HALF), (B_HALF, B_COLS))

    def term_a(y_at, x_at, half):
        lo, hi = a_cuts[half]
        return dot_tn(normed[:, chip_span(y_at, x_at)], gproj[:, lo:hi])

    def term_b(y_at, x_at, half):
        lo, hi = b_cuts[half]
        return dot_tn(hcat[:, lo:hi], grads[:, chip_span(y_at, x_at)])

    def cross(k):
        span = pl.ds(pl.multiple_of(k * MIX, MIX), MIX)
        there = pl.ds(pl.multiple_of((4 + k) * 256, 256), 256)
        return (
            remote(probs.at[k, 0], wb.at[pl.ds(0, MIX), there], xs.at[k, 0], xr.at[k, 0], me.across),
            remote(slope.at[:, span], wb.at[pl.ds(MIX, UP), there], xs.at[k, 1], xr.at[k, 1], me.across),
        )

    def cross_all():
        pl.semaphore_wait(free_sem, 1)

        def step(k, _):
            span = pl.ds(pl.multiple_of(k * MIX, MIX), MIX)
            total = term_b(turn_of(k), 1 - x, 0).astype(BF)
            probs[k, 0] = total[0:MIX]
            slope[0 : B_HALF - MIX, span] = total[MIX:B_HALF]
            slope[B_HALF - MIX : UP, span] = term_b(turn_of(k), 1 - x, 1).astype(BF)
            for copy in cross(k):
                copy.start()
            return 0

        lax.fori_loop(0, 4, step, 0)

    def crossed(k):
        for copy in cross(k):
            copy.wait_recv()

    def from_across(k, half):
        lo, hi = b_cuts[half]
        return wb[lo:hi, (4 + k) * 256 : (5 + k) * 256].astype(F32)

    def a_place(at):
        return wa.at[pl.ds(pl.multiple_of(at * 256, 256), 256)]

    def b_place(at):
        return wb.at[:, pl.ds(at * 256, 256)]

    a_spans = (pl.ds(0, A_HALF), pl.ds(A_HALF, A_HALF))
    b_spans = (pl.ds(0, B_HALF), pl.ds(B_HALF, B_HALF))

    def far_piece(way, x_at):
        source = far_a.at[x_at, :, a_spans[way]]
        return remote(source, half_a.at[way, x_at], fs.at[way, x_at], fr.at[way, x_at], me.beside(1 - 2 * way))

    def far_piece_b(way):
        source = wb.at[b_spans[way], pl.ds(0, 256)]
        return remote(source, half_b.at[way], fs.at[way, 2], fr.at[way, 2], me.beside(1 - 2 * way))

    def near_piece(way, x_at):
        source = a_place(2 + 2 * way + x_at)
        return remote(source, got_a.at[way, x_at], ns.at[way, x_at], nr.at[way, x_at], me.beside(1 - 2 * way))

    def near_piece_b(way, half):
        lo, hi = b_cuts[half]
        source = wb.at[pl.ds(lo, hi - lo), pl.ds((1 + way) * 256, 256)]
        target = got_b.at[way, pl.ds(lo, hi - lo)]
        return remote(source, target, ns.at[way, 2 + half], nr.at[way, 2 + half], me.beside(1 - 2 * way))

    def cross_last():
        return remote(a_place(6), xa_in, xs.at[4, 0], xr.at[4, 0], me.across)

    def send_far_all():
        def step(k, _):
            x_at = (1 - k) * (1 - x) + k * x
            for way, (lo, hi) in enumerate(a_cuts):
                far_a[x_at, :, lo:hi] = term_a(far, x_at, way).astype(BF)
                far_piece(way, x_at).start()
            return 0

        lax.fori_loop(0, 2, step, 0)

    def send_near(way, x_at):
        target = pl.ds(pl.multiple_of((2 + 2 * way + x_at) * 256, 256), 256)
        for half in (1 - way, way):
            lo, hi = a_cuts[half]
            total = term_a(me.turn(1 - 2 * way), x_at, half)
            if half == way:
                far_piece(way, x_at).wait_recv()
                total = total + half_a[way, x_at].astype(F32)
            wa[target, lo:hi] = total.astype(BF)
        start(near_piece(way, x_at))

    def send_far_b():
        for way, (lo, hi) in enumerate(b_cuts):
            total = term_b(far, x, way)
            if way == 0:
                crossed(0)
            wb[lo:hi, 0:256] = (total + from_across(0, way)).astype(BF)
            start(far_piece_b(way))

    def send_near_b(way):
        span = slice((1 + way) * 256, (2 + way) * 256)
        for half, (lo, hi) in enumerate(b_cuts):
            total = term_b(me.turn(1 - 2 * way), x, half)
            if half == 0:
                crossed(1 + way)
            total = total + from_across(1 + way, half)
            if half == way:
                far_piece_b(way).wait_recv()
                total = total + half_b[way].astype(F32)
            wb[lo:hi, span] = total.astype(BF)
            start(near_piece_b(way, half))

    def arrived_a(x_at, at):
        for half, (lo, hi) in enumerate(a_cuts):
            total = term_a(y, x_at, half)
            for way in (0, 1):
                if half == 0:
                    near_piece(way, x_at).wait_recv()
                total = total + got_a[way, x_at, :, lo:hi].astype(F32)
            wa[at * 256 : (at + 1) * 256, lo:hi] = total.astype(BF)

    def begun_b(at):
        crossed(3)
        for half, (lo, hi) in enumerate(b_cuts):
            wb[lo:hi, at * 256 : (at + 1) * 256] = (term_b(y, x, half) + from_across(3, half)).astype(BF)

    def arrived_b(at, half):
        lo, hi = b_cuts[half]
        span = slice(at * 256, (at + 1) * 256)
        total = wb[lo:hi, span].astype(F32)
        for way in (0, 1):
            near_piece_b(way, half).wait_recv()
            total = total + got_b[way, lo:hi].astype(F32)
        wb[lo:hi, span] = total.astype(BF)

    near_z = {"tensor": z + 1 - 2 * lax.rem(z, 2)}
    near_y = {"dp": me.at(y + 1 - 2 * lax.rem(y, 2), x, core)}
    partners = (near_z, me.z_peer(2), me.sibling, me.across, near_y, me.beside(2))

    def exchange(step):
        return remote(tally.at[step], came.at[step], ts.at[step], tr.at[step], partners[step])

    def fold(step):
        exchange(step).wait_recv()
        total = tally[step] + came[step]
        if step < 3:
            tally[step + 1, 0:3] = total[0:3]
            tally[step + 1, 3:8] = tally[step, 3:8]
            if step == 2:
                tally[step + 1, 4:5] = came[step, 3:4]
        else:
            tally[step + 1] = total
        if step < 5:
            start(exchange(step + 1))

    for copy in sent:
        copy.wait_send()
    sent.clear()

    def forward_step(i):
        away = lax.rem(i, 2) != core

        @pl.when((i == 1) & (core == 1))
        def _():
            spread_own(0, 1, True)

        await_rows(0, i)
        forward_first(i)

        @pl.when((i < 3) & away)
        def _():
            relay(0, i + 1)

    def backward_step(i):
        own = lax.rem(i, 2) == core

        @pl.when((section == 0) & (i < 3) & jnp.logical_not(own))
        def _():
            spread_own(1, (i + 1) // 2, True)

        await_rows(1, i)
        backward_first(i)

        @pl.when((section == 1) & (i == 0) & (core == 0))
        def _():
            spread_own(0, 1, True)

        @pl.when((section == 0) & (i == 3))
        def _():
            pl.semaphore_signal(free_sem, inc=1, device_id=me.across, device_id_type=MESH)
            send_far_all()
            cross_all()

        @pl.when((section == 1) & (i >= 1) & jnp.logical_not(own))
        def _():
            pair_sum(1, (i - 1) // 2)

        @pl.when((section == 1) & (i >= 2) & own)
        def _():
            finish_backward(0)

        @pl.when((section == 0) & own)
        def _():
            pair_sent(0, i // 2)

        backward_second(i)

        @pl.when((section == 0) & (i < 3) & jnp.logical_not(own))
        def _():
            relay(1, i + 1)

    def joint_step(j, _):
        @pl.when((section == 1) & (j < 4))
        def _():
            forward_step(j)

        @pl.when(j != 2)
        def _():
            backward_step(j - j // 3)

        return 0

    lax.fori_loop(0, 5, joint_step, 0)

    @pl.when(section == 1)
    def _():
        @pl.when(core == 1)
        def _():
            pair_sum(1, 1)

        finish_backward(1)
        for m in range(2):
            pair_sent(1, m)

        def late_step(i, _):
            forward_second(i)
            return 0

        lax.fori_loop(0, 4, late_step, 0)
        pl.semaphore_signal(free_sem, inc=1, device_id=me.across, device_id_type=MESH)
        send_far_all()
        cross_all()

    for back in range(2):

        @pl.when(section != back)
        def _():
            for m in range(2):
                pair_sum(back, m)

    send_far_b()
    for x_at in (1 - x, x):
        for way in (0, 1):
            send_near(way, x_at)

    @pl.when(section == 0)
    def _():
        for m in range(2):
            finish_backward(m)

    @pl.when(section == 1)
    def _():
        finish_forward_all()

    tally[0, 3:4, 0:A_COLS] = sum_a[0:1]
    start(exchange(0))
    send_near_b(0)
    fold(0)
    fold(1)
    send_near_b(1)
    fold(2)
    arrived_a(1 - x, 6)
    start(cross_last())
    arrived_a(x, 7)
    begun_b(3)
    fold(3)

    def result(half, peer, at):
        rows = pl.ds(pl.multiple_of(7 * 256 + half * 128, 128), 128)
        cols = pl.ds(pl.multiple_of(3 * 256 + half * 128, 128), 128)
        sources = [wa.at[rows, pl.ds(k * MIX, MIX)] for k in range(3)]
        low = B_HALF - MIX
        sources += [wa.at[rows, pl.ds(QKV, UP)], wb.at[pl.ds(0, MIX), cols]]
        sources += [wb.at[pl.ds(MIX, low), cols], wb.at[pl.ds(B_HALF, UP - low), cols]]
        targets = [gq_out.at[k, :, place(at, MIX)] for k in range(3)]
        first, second = pl.multiple_of(at * UP, 128), pl.multiple_of(at * UP + low, 128)
        targets += [gu_out.at[:, place(at, UP)], go_out.at[place(at, MIX), :]]
        targets += [gd_out.at[pl.ds(first, low), :], gd_out.at[pl.ds(second, UP - low), :]]
        if peer:
            return [
                remote(source, target, end_s.at[k], end_r.at[k], me.sibling)
                for k, (source, target) in enumerate(zip(sources, targets))
            ]
        return [
            pltpu.make_async_copy(source, target, end_k.at[k])
            for k, (source, target) in enumerate(zip(sources, targets))
        ]

    outgoing, staying = result(1 - core, True, core), result(core, False, core)
    incoming = result(1 - core, True, 1 - core)
    cross_last().wait_recv()
    wa[7 * 256 : 8 * 256] = (wa[7 * 256 : 8 * 256].astype(F32) + xa_in[...].astype(F32)).astype(BF)
    for at in range(4):
        outgoing[at].start()
        staying[at].start()
    fold(4)
    for half, pieces in enumerate(((4, 5), (6,))):
        arrived_b(3, half)
        for at in pieces:
            outgoing[at].start()
            staying[at].start()
    fold(5)
    sums_ref[...] = tally[6]
    for at in range(3):
        span = slice(at * MIX, (at + 1) * MIX)
        ours_a, others_a = tally[6, 3:4, span], tally[6, 4:5, span]
        gqb_ref[at : at + 1, 0:MIX] = jnp.where(core == 0, ours_a, others_a)
        gqb_ref[at : at + 1, MIX : 2 * MIX] = jnp.where(core == 0, others_a, ours_a)
    ours_a, others_a = tally[6, 3:4, QKV:A_COLS], tally[6, 4:5, QKV:A_COLS]
    gub_ref[0:1, 0:UP] = jnp.where(core == 0, ours_a, others_a)
    gub_ref[0:1, UP : 2 * UP] = jnp.where(core == 0, others_a, ours_a)

    for copy in sent + gives + [tell]:
        copy.wait_send()
    for k in range(4):
        for copy in cross(k):
            copy.wait_send()
    for way in range(2):
        for x_at in range(2):
            far_piece(way, x_at).wait_send()
    for back in range(2):
        for m in range(2):
            mine = 2 * m + core
            for h in range(PARTS):
                for k in range(3):
                    to_z(back, m, mine, k, h).wait_send()
                for k in range(4):
                    to_sibling(back, m, mine, k, h).wait_send()
            keep(back, m).wait()

        @pl.when(section == back)
        def _():
            for m in range(2):
                for h in range(PARTS):
                    onward(back, m, h).wait_send()

        @pl.when(section != back)
        def _():
            for m in range(2):
                pair_sent(back, m)
                for q in range(2):
                    to_pair(back, 2 * m + 1 - core, q).wait_send()

    for at in range(7):
        staying[at].wait()
        outgoing[at].wait_send()
        incoming[at].wait_recv()


def both_layers(rows_in, cotangent, qkv_w, up_w, out_w, down_w, bias_qkv, bias_up, bias_out, bias_down, gain, shift, mine):
    places = np.arange(SLOT, dtype=np.float32)
    frequency = (10000.0 ** (-(np.arange(ROT // 2, dtype=np.float32) * np.float32(2.0 / ROT)))).astype(np.float32)
    angles = (places[:, None] * frequency[None, :]).astype(np.float32).astype(np.float64)
    cosine = np.ones((SLOT, HD), np.float32)
    sine = np.zeros((SLOT, HD), np.float32)
    cosine[:, 0:ROT] = np.tile(np.cos(angles), (1, 2))
    sine[:, 0:ROT] = np.tile(np.sin(angles), (1, 2))
    cosine, sine = (jnp.asarray(np.tile(table, (1, 2))) for table in (cosine, sine))
    any_ = pl.BlockSpec(memory_space=pl.ANY)
    vmem = pl.BlockSpec(memory_space=pltpu.VMEM)
    dma = pltpu.SemaphoreType.DMA
    shape = jax.ShapeDtypeStruct
    return pl.pallas_call(
        layers_kernel,
        out_shape=(
            shape((2, ROWS, D), BF),
            shape((2, ROWS, D), BF),
            shape((3, 128, 2 * MIX), BF),
            shape((128, 2 * UP), BF),
            shape((2 * MIX, 128), BF),
            shape((2 * UP, 128), BF),
            shape((8, D), F32),
            shape((3, 2 * MIX), F32),
            shape((1, 2 * UP), F32),
        ),
        in_specs=[any_] * 6 + [vmem] * 9,
        out_specs=[any_] * 6 + [vmem] * 3,
        scratch_shapes=[
            pltpu.VMEM((D, A_COLS), BF),
            pltpu.VMEM((B_COLS, D), BF),
            pltpu.VMEM((ALL, D), BF),
            pltpu.VMEM((ALL, D), BF),
            pltpu.VMEM((ALL, QKV), BF),
            pltpu.VMEM((ALL, B_COLS), BF),
            pltpu.VMEM((ALL, UP), BF),
            pltpu.VMEM((4, 4, SLOT, SLOT), BF),
            pltpu.VMEM((ALL, A_COLS), BF),
            pltpu.VMEM((4, SLOT, D), BF),
            pltpu.VMEM((2, SLOT, D), BF),
            pltpu.VMEM((4, 3, ROWS, D), BF),
            pltpu.VMEM((2, ROWS, D), BF),
            pltpu.VMEM((2, ROWS, D), BF),
            pltpu.VMEM((8, 128), F32),
            pltpu.VMEM((8, 128), F32),
            pltpu.VMEM((8, 128), jnp.int32),
            pltpu.VMEM((8, 128), jnp.int32),
            pltpu.VMEM((8, 128), jnp.int32),
            pltpu.VMEM((8, A_COLS), F32),
            pltpu.VMEM((2, 256, A_COLS), BF),
            pltpu.VMEM((2, 2, 256, A_HALF), BF),
            pltpu.VMEM((2, B_HALF, 256), BF),
            pltpu.VMEM((2, 2, 256, A_COLS), BF),
            pltpu.VMEM((2, B_COLS, 256), BF),
            pltpu.VMEM((256, A_COLS), BF),
            pltpu.VMEM((8, A_COLS), F32),
            pltpu.VMEM((7, 8, D), F32),
            pltpu.VMEM((6, 8, D), F32),
            dma((7,)),
            dma((2, 10)),
            dma((2, 10)),
            dma((2, 2, 9)),
            dma((2, 2, 9)),
            dma((7,)),
            dma((7,)),
            dma((2, 2, 3 * PARTS)),
            dma((2, 2, 3 * PARTS)),
            dma((2, 2, 4 * PARTS)),
            dma((2, 2, 4 * PARTS)),
            dma((2, 2, 2)),
            dma((2, 2, 2)),
            dma((2, 2, 3 * PARTS)),
            dma((2, 2, 3 * PARTS)),
            dma((2, 2, PARTS)),
            dma((2, 2, PARTS)),
            dma((5, 2)),
            dma((5, 2)),
            dma((2, 3)),
            dma((2, 3)),
            dma((2, 4)),
            dma((2, 4)),
            dma((6,)),
            dma((6,)),
            dma((7,)),
            dma((7,)),
            dma((7,)),
            dma((2, 2)),
            pltpu.SemaphoreType.REGULAR,
            pltpu.SemaphoreType.REGULAR((2,)),
        ],
        compiler_params=pltpu.CompilerParams(
            collective_id=1, has_side_effects=True, vmem_limit_bytes=VMEM_LIMIT
        ),
        name="both_layers",
    )(
        rows_in, cotangent, qkv_w, up_w, out_w, down_w,
        bias_qkv, bias_up, bias_out, bias_down, gain, shift, mine, cosine, sine,
    )


def widen_kernel(lo, ig, gq, gu, go, gd, sums, gqb, gub, *outs):
    lo_out, ig_out, gq_out, gu_out, go_out, gd_out, gain, shift, out_b, down_b, qkv_b, up_b = outs
    lo_out[...] = lo[...]
    ig_out[...] = ig[...]
    gq_out[...] = gq[...].astype(F32)
    gu_out[...] = gu[...].astype(F32)
    go_out[...] = go[...].astype(F32)
    gd_out[...] = gd[...].astype(F32)
    gain[...] = sums[0:1]
    shift[...] = sums[1:2]
    out_b[...] = sums[2:3]
    down_b[...] = sums[2:3]
    for k in range(3):
        qkv_b[k] = gqb[k : k + 1]
    up_b[...] = gub[...]


def widened(lo, ig, gq, gu, go, gd, sums, gqb, gub):
    steps = 2
    shape = jax.ShapeDtypeStruct

    def cut(whole, dim):
        block = tuple(size // steps if at == dim else size for at, size in enumerate(whole))
        return pl.BlockSpec(block, lambda i: tuple(i if at == dim else 0 for at in range(len(whole))))

    def same(whole):
        return pl.BlockSpec(whole, lambda i: (0,) * len(whole))

    large = [cut(lo.shape, 1), cut(ig.shape, 1), cut(gq.shape, 1), cut(gu.shape, 0), cut(go.shape, 0), cut(gd.shape, 0)]
    small = [(1, D)] * 4 + [(3, 1, 2 * MIX), (1, 2 * UP)]
    return pl.pallas_call(
        widen_kernel,
        grid=(steps,),
        out_shape=(
            [shape(lo.shape, BF), shape(ig.shape, BF)]
            + [shape(each.shape, F32) for each in (gq, gu, go, gd)]
            + [shape(each, F32) for each in small]
        ),
        in_specs=large + [same(sums.shape), same(gqb.shape), same(gub.shape)],
        out_specs=large + [same(each) for each in small],
        compiler_params=pltpu.CompilerParams(vmem_limit_bytes=VMEM_LIMIT),
        name="widened",
    )(lo, ig, gq, gu, go, gd, sums, gqb, gub)


def shards(
    inputs,
    cotangent,
    doc_split,
    qkv_weight,
    qkv_bias,
    out_weight,
    out_bias,
    fc1_weight,
    fc1_bias,
    fc2_weight,
    fc2_bias,
    ln_gain,
    ln_bias,
):
    results = both_layers(
        inputs[:, 0],
        cotangent[:, 0],
        qkv_weight[0].transpose(1, 0, 2),
        fc1_weight[0],
        out_weight[0],
        fc2_weight[0],
        qkv_bias[0][:, None, :],
        fc1_bias,
        out_bias,
        fc2_bias,
        ln_gain,
        ln_bias,
        doc_split.reshape(1, 2),
    )
    layer_out, input_grad, grad_qkv, grad_up, grad_out, grad_down, gain, shift, out_b, down_b, qkv_b, up_b = widened(
        *results
    )
    return (
        layer_out[None, :, None],
        input_grad[None, :, None],
        grad_qkv.transpose(1, 0, 2)[None],
        qkv_b.transpose(1, 0, 2),
        grad_out[None],
        out_b,
        grad_up[None],
        up_b,
        grad_down[None],
        down_b,
        gain,
        shift,
    )


def solution(mesh):
    rows = P(None, "dp", "tensor", None)
    placed_weights = (
        P("section", "dp", None, "tensor"),
        P("section", None, "tensor"),
        P("section", "tensor", "dp"),
        P("section", None),
        P("section", "dp", "tensor"),
        P("section", "tensor"),
        P("section", "tensor", "dp"),
        P("section", None),
        P("section", None),
        P("section", None),
    )
    out_rows = P("section", None, "dp", "tensor", None)
    return jax.shard_map(
        shards,
        mesh=mesh,
        in_specs=(rows, rows, P(None, "dp")) + placed_weights,
        out_specs=(out_rows, out_rows) + placed_weights,
        check_vma=False,
    )
```

```python
from functools import partial

import jax
import jax.numpy as jnp
import numpy as np
from jax import lax
from jax.experimental import pallas as pl
from jax.experimental.pallas import tpu as pltpu
from jax.sharding import PartitionSpec as P

HD = 64
ROT = 32
EPSILON = 1e-05
MESH = pl.DeviceIdType.MESH
BF = jnp.bfloat16
F32 = jnp.float32

D = 2048
SLOT = 256
ROWS = 64
PARTS = 4
PART = ROWS // PARTS
QKV = 768
UP = 1024
A_COLS = QKV + UP
MIX = 256
B_COLS = MIX + UP
A_HALF = A_COLS // 2
B_HALF = B_COLS // 2
ALL = 4 * SLOT
VMEM_LIMIT = 62 * 2**20


def dot(a, b):
    return lax.dot_general(a, b, (((1,), (0,)), ((), ())), preferred_element_type=F32)


def dot_nt(a, b):
    return lax.dot_general(a, b, (((1,), (1,)), ((), ())), preferred_element_type=F32)


def dot_tn(a, b):
    return lax.dot_general(a, b, (((0,), (0,)), ((), ())), preferred_element_type=F32)


def remote(src, dst, send, recv, device):
    return pltpu.make_async_remote_copy(
        src_ref=src, dst_ref=dst, send_sem=send, recv_sem=recv, device_id=device, device_id_type=MESH
    )


def greet(peers):
    barrier = pltpu.get_barrier_semaphore()
    for peer in peers:
        pl.semaphore_signal(barrier, inc=1, device_id=peer, device_id_type=MESH)
    pl.semaphore_wait(barrier, len(peers))


class Place:
    def __init__(self):
        self.dp = lax.axis_index("dp")
        self.core = lax.rem(self.dp, 2)
        self.x = lax.rem(self.dp // 2, 2)
        self.y = self.dp // 4
        self.z = lax.axis_index("tensor")
        self.sibling = {"dp": self.dp + 1 - 2 * self.core}
        self.across = {"dp": self.at(self.y, 1 - self.x, self.core)}

    def at(self, y, x, core):
        return (y * 2 + x) * 2 + core

    def turn(self, by):
        return lax.rem(self.y + 4 + by, 4)

    def beside(self, by):
        return {"dp": self.at(self.turn(by), self.x, self.core)}

    def z_peer(self, by):
        return {"tensor": lax.rem(self.z + by, 4)}


STAGES = (
    ((0, 512), (512, 512), (1024, 384), (1408, 384)),
    ((0, 384), (384, 384), (768, 256), (1024, 256)),
)


def layers_kernel(
    x_hbm, cot_hbm, qkv_hbm, up_hbm, ow_hbm, dw_hbm,
    qb_ref, ub_ref, ob_ref, db_ref, gain_ref, shift_ref, mine_ref, cos_ref, sin_ref,
    lo_out, ig_out, gq_out, gu_out, go_out, gd_out, sums_ref, gqb_ref, gub_ref,
    wa, wb, normed, grads, qkv, hcat, slope, probs, gproj, part, got, zgot, xrow, grow, ctab, stab, split, ours, theirs, bias,
    far_a, half_a, half_b, got_a, got_b, xa_in, sum_a, tally, came,
    own_sem, x_send, x_recv, y_send, y_recv, sib_send, sib_recv,
    agz_s, agz_r, ags_s, ags_r, par_s, par_r, rsz_s, rsz_r, sec_s, sec_r,
    xs, xr, fs, fr, ns, nr, ts, tr, end_s, end_r, end_k, keep_s, free_sem, pair_free,
):
    me = Place()
    section = lax.axis_index("section")
    core, z = me.core, me.z
    greet(
        [me.sibling, me.across, me.beside(1), me.beside(-1), me.beside(2)]
        + [me.z_peer(1), me.z_peer(2), me.z_peer(3), {"section": 1 - section}]
    )

    def device_span(dp):
        return pl.ds(pl.multiple_of(dp * 128, 128), 128)

    def chip_span(y_at, x_at):
        return pl.ds(pl.multiple_of((y_at * 2 + x_at) * 256, 256), 256)

    def place(at, size):
        return pl.ds(pl.multiple_of(at * size, size), size)

    def blocks(dp, half):
        span = device_span(dp)
        pairs = [
            (qkv_hbm.at[k, :, place(half, MIX)], wa.at[span, pl.ds(k * MIX, MIX)]) for k in range(3)
        ]
        pairs.append((up_hbm.at[:, place(half, UP)], wa.at[span, pl.ds(QKV, UP)]))
        pairs.append((ow_hbm.at[place(half, MIX), :], wb.at[pl.ds(0, MIX), span]))
        pairs.append((dw_hbm.at[place(half, UP), :], wb.at[pl.ds(MIX, UP), span]))
        return pairs

    other = me.dp + 1 - 2 * core
    holds = [
        pltpu.make_async_copy(source, target, own_sem.at[at])
        for at, (source, target) in enumerate(blocks(me.dp, core))
    ]
    gives = [
        remote(source, target, sib_send.at[at], sib_recv.at[at], me.sibling)
        for at, (source, target) in enumerate(blocks(me.dp, 1 - core))
    ]
    takes = [
        remote(source, target, sib_send.at[at], sib_recv.at[at], me.sibling)
        for at, (source, target) in enumerate(blocks(other, 1 - core))
    ]
    tell = remote(ours, theirs, sib_send.at[6], sib_recv.at[6], me.sibling)
    rows_in = [
        pltpu.make_async_copy(x_hbm, xrow, own_sem.at[6]),
        pltpu.make_async_copy(cot_hbm, grow, own_sem.at[6]),
    ]
    y, x = me.y, me.x
    far = me.turn(2)

    def piece_of(stage, y_at, x_at, which):
        span = pl.ds(*STAGES[stage][which])
        if stage == 0:
            return wa.at[chip_span(y_at, x_at), span]
        return wb.at[span, chip_span(y_at, x_at)]

    def over_x(stage, y_at, x_at, which, slot):
        piece = piece_of(stage, y_at, x_at, which)
        return remote(piece, piece, x_send.at[stage, slot], x_recv.at[stage, slot], me.across)

    def over_y(stage, by, y_at, x_at, which, slot):
        piece = piece_of(stage, y_at, x_at, which)
        way = 0 if by > 0 else 1
        return remote(piece, piece, y_send.at[stage, way, slot], y_recv.at[stage, way, slot], me.beside(by))

    sent = []

    def start(copy):
        copy.start()
        sent.append(copy)

    def own_first(stage):
        for which in (0, 1):
            start(over_x(stage, y, x, which, which))
        for which in (2, 3):
            for by in (1, -1):
                start(over_y(stage, by, y, x, which, which))

    def own_second(stage):
        for which in (2, 3):
            start(over_x(stage, y, x, which, which))
        for which in (0, 1):
            for by in (1, -1):
                start(over_y(stage, by, y, x, which, which))

    def pass_near(stage):
        for which in (2, 3):
            for by in (1, -1):
                source = me.turn(-by)
                over_y(stage, by, source, x, which, which).wait_recv()
                if (which == 2) == (by > 0):
                    start(over_y(stage, by, source, x, which, 6))
                start(over_x(stage, source, x, which, 2 * which + (0 if by > 0 else 1)))

    def pass_crossed(stage):
        for which in (0, 1):
            over_x(stage, y, 1 - x, which, which).wait_recv()
            for by in (1, -1):
                start(over_y(stage, by, y, 1 - x, which, 4 + which))

    def pass_far(stage):
        for which, by in ((2, 1), (3, -1)):
            over_y(stage, by, far, x, which, 6).wait_recv()
            start(over_x(stage, far, x, which, 6 + which))

    def pass_on(stage):
        for which, by in ((0, 1), (1, -1)):
            source = me.turn(-by)
            over_y(stage, by, source, x, which, which).wait_recv()
            start(over_y(stage, by, source, x, which, 7))

    def pass_on_crossed(stage):
        for which, by in ((0, 1), (1, -1)):
            source = me.turn(-by)
            over_y(stage, by, source, 1 - x, which, 4 + which).wait_recv()
            start(over_y(stage, by, source, 1 - x, which, 8))

    def settle(stage):
        for which, by in ((0, -1), (1, 1)):
            source = me.turn(-by)
            over_y(stage, by, source, x, which, which).wait_recv()
            over_y(stage, by, source, 1 - x, which, 4 + which).wait_recv()
        for which in (2, 3):
            over_x(stage, y, 1 - x, which, which).wait_recv()
            for by in (1, -1):
                over_x(stage, me.turn(-by), 1 - x, which, 2 * which + (0 if by > 0 else 1)).wait_recv()
            over_x(stage, far, 1 - x, which, 6 + which).wait_recv()
        for which, by in ((0, 1), (1, -1)):
            over_y(stage, by, far, x, which, 7).wait_recv()
            over_y(stage, by, far, 1 - x, which, 8).wait_recv()

    def band(at, h):
        return pl.ds(pl.multiple_of(at * ROWS + h * PART, PART), PART)

    def slot(i):
        return pl.ds(pl.multiple_of(i * SLOT, SLOT), SLOT)

    def slot_band(i, at, h):
        return pl.ds(pl.multiple_of(i * SLOT + at * ROWS + h * PART, PART), PART)

    parts = [slice(h * PART, (h + 1) * PART) for h in range(PARTS)]

    def standard(rows):
        average = jnp.mean(rows, axis=-1, keepdims=True)
        centred = rows - average
        variance = jnp.mean(centred * centred, axis=-1, keepdims=True)
        scale = lax.rsqrt(variance + EPSILON)
        return centred * scale, scale

    def spread_buffer(back):
        return grads if back else normed

    def to_z(back, m, i, k, h):
        piece = spread_buffer(back).at[slot_band(i, z, h)]
        at = PARTS * k + h
        return remote(piece, piece, agz_s.at[back, m, at], agz_r.at[back, m, at], me.z_peer(1 + k))

    def from_z(back, m, i, k, h):
        piece = spread_buffer(back).at[slot_band(i, lax.rem(z + 3 - k, 4), h)]
        at = PARTS * k + h
        return remote(piece, piece, agz_s.at[back, m, at], agz_r.at[back, m, at], me.z_peer(3 - k))

    def to_sibling(back, m, i, k, h):
        piece = spread_buffer(back).at[slot_band(i, lax.rem(z + 3 - k, 4), h)]
        at = PARTS * k + h
        return remote(piece, piece, ags_s.at[back, m, at], ags_r.at[back, m, at], me.sibling)

    def spread_own(back, m, wait):
        i = 2 * m + core
        for h in range(PARTS):
            if wait:
                onward(1 if back else 0, m, h).wait_recv()
            if back:
                grads[slot_band(i, z, h)] = grow[m, parts[h]]
            else:
                xhat, _ = standard(xrow[m, parts[h]].astype(F32))
                normed[slot_band(i, z, h)] = (xhat * gain_ref[...] + shift_ref[...]).astype(BF)
            for k in range(3):
                to_z(back, m, i, k, h).start()
            to_sibling(back, m, i, 3, h).start()

    def relay(back, i):
        m = i // 2
        for h in range(PARTS):
            for k in range(3):
                from_z(back, m, i, k, h).wait_recv()
                to_sibling(back, m, i, k, h).start()

    def await_rows(back, i):
        m = i // 2

        @pl.when(lax.rem(i, 2) != core)
        def _():
            for h in range(PARTS):
                for k in range(4):
                    to_sibling(back, m, i, k, h).wait_recv()

    def part_at(i):
        return (1 - lax.rem(i + core, 2)) * (i // 2) + lax.rem(i + core, 2) * (2 + i // 2)

    def to_pair(back, i, q):
        m = i // 2
        span = pl.ds(q * (D // 2), D // 2)
        return remote(
            part.at[2 + m, :, span], got.at[m, :, span], par_s.at[back, m, q], par_r.at[back, m, q], me.sibling
        )

    def sum_to_z(back, m, k, h):
        peer = me.z_peer(1 + k)
        at = PARTS * k + h
        return remote(
            part.at[m, band(peer["tensor"], h)],
            zgot.at[back * 2 + m, k, pl.ds(h * PART, PART)],
            rsz_s.at[back, m, at],
            rsz_r.at[back, m, at],
            peer,
        )

    def pair_add(back, m):
        for q in range(2):
            span = slice(q * (D // 2), (q + 1) * (D // 2))
            to_pair(back, 2 * m + core, q).wait_recv()
            part[m, :, span] = (part[m, :, span].astype(F32) + got[m, :, span].astype(F32)).astype(BF)

        @pl.when(section == back)
        def _():
            pl.semaphore_signal(pair_free.at[m], inc=1, device_id=me.sibling, device_id_type=MESH)

    def pair_spread(back, m):
        for h in range(PARTS):
            for k in range(3):
                sum_to_z(back, m, k, h).start()

    def pair_sum(back, m):
        pair_add(back, m)
        pair_spread(back, m)

    def pair_sent(back, m):
        for h in range(PARTS):
            for k in range(3):
                sum_to_z(back, m, k, h).wait_send()

    def row_sum(back, m, h):
        total = part[m, band(z, h)].astype(F32)
        for k in range(3):
            sum_to_z(back, m, k, h).wait_recv()
            total = total + zgot[back * 2 + m, k, parts[h]].astype(F32)
        return total

    def onward(back, m, h):
        target = grow if back else xrow
        span = pl.ds(h * PART, PART)
        return remote(
            zgot.at[back * 2 + m, 0, span],
            target.at[m, span],
            sec_s.at[back, m, h],
            sec_r.at[back, m, h],
            {"section": 1 - back},
        )

    def keep(back, m):
        target = ig_out if back else lo_out
        return pltpu.make_async_copy(zgot.at[back * 2 + m, 0], target.at[m], keep_s.at[back, m])

    def finish_forward(m):
        for h in range(PARTS):
            total = row_sum(0, m, h) + (ob_ref[...] + db_ref[...])
            zgot[m, 0, parts[h]] = (xrow[m, parts[h]].astype(F32) + total).astype(BF)

            @pl.when(section == 0)
            def _():
                onward(0, m, h).start()

        keep(0, m).start()

    def finish_backward(m):
        for h in range(PARTS):
            grad = row_sum(1, m, h)
            xhat, scale = standard(xrow[m, parts[h]].astype(F32))
            above = grow[m, parts[h]].astype(F32)
            a = grad * gain_ref[...]
            inner = a - jnp.mean(a, axis=-1, keepdims=True) - xhat * jnp.mean(a * xhat, axis=-1, keepdims=True)
            zgot[2 + m, 0, parts[h]] = (above + inner * scale).astype(BF)

            @pl.when(section == 1)
            def _():
                onward(1, m, h).start()

            tally[0, 0:1, :] += jnp.sum(grad * xhat, axis=0, keepdims=True)
            tally[0, 1:2, :] += jnp.sum(grad, axis=0, keepdims=True)
            tally[0, 2:3, :] += jnp.sum(above, axis=0, keepdims=True)

        keep(1, m).start()

    lanes = lax.broadcasted_iota(jnp.int32, (SLOT, 128), 1) % HD
    early = lanes < ROT // 2

    places = lax.broadcasted_iota(jnp.int32, (SLOT, 128), 0)

    def tables(i):
        first = places < split[pl.ds(i, 1), :]
        cosine, sine = cos_ref[...], sin_ref[...]
        cos_at, sin_at = ctab[pl.ds(i, 1), :], stab[pl.ds(i, 1), :]
        return (
            jnp.where(first, cosine, cosine * cos_at + sine * sin_at),
            jnp.where(first, sine, sine * cos_at - cosine * sin_at) * jnp.where(early, -1.0, 1.0),
        )

    def turned(values, table, sign):
        halves = []
        for at in (0, 128):
            piece = values[:, at : at + 128]
            swapped = jnp.where(early, pltpu.roll(piece, 128 - ROT // 2, 1), pltpu.roll(piece, ROT // 2, 1))
            halves.append(piece * table[0] + swapped * (table[1] * sign))
        return jnp.concatenate(halves, axis=1)

    def head_mask(head):
        lane = lax.broadcasted_iota(jnp.int32, (1, MIX), 1)
        return jnp.where(lane // HD == head, 1.0, 0.0).astype(BF)

    def forward_first(i):
        rows = normed[slot(i)]
        projected = dot(rows, wa[:, 0:QKV]) + bias[0:1, 0:QKV]
        table = tables(i)
        queries = turned(projected[:, 0:MIX], table, 1.0).astype(BF)
        keys = turned(projected[:, MIX : 2 * MIX], table, 1.0).astype(BF)
        values = projected[:, 2 * MIX : 3 * MIX].astype(BF)
        qkv[slot(i), 0:MIX] = queries
        qkv[slot(i), MIX : 2 * MIX] = keys
        qkv[slot(i), 2 * MIX : 3 * MIX] = values
        v = dot(rows, wa[:, QKV:A_COLS]) + bias[0:1, QKV:A_COLS]
        at = split[pl.ds(i, 1), :]
        at = jnp.concatenate([at, at], axis=1)
        row_at = lax.broadcasted_iota(jnp.int32, (SLOT, SLOT), 0)
        key_at = lax.broadcasted_iota(jnp.int32, (SLOT, SLOT), 1)
        same = jnp.where(row_at < at, 1, 0) == jnp.where(key_at < at, 1, 0)
        allowed = (key_at <= row_at) & same
        mixed = jnp.zeros((SLOT, MIX), F32)
        for head in range(4):
            mask = head_mask(head)
            scores = jnp.where(allowed, dot_nt(queries * mask, keys) * HD**-0.5, -1e30)
            weights = jnp.exp(scores - jnp.max(scores, axis=-1, keepdims=True))
            chances = (weights / jnp.sum(weights, axis=-1, keepdims=True)).astype(BF)
            probs[i, head] = chances
            mixed = mixed + dot(chances, values * mask)
        hcat[slot(i), 0:MIX] = mixed.astype(BF)
        root = np.sqrt(2 / np.pi).astype(np.float32)
        square = v * v
        bent = jnp.tanh(root * (v + 0.044715 * (square * v)))
        half = 0.5 * (1.0 + bent)
        hcat[slot(i), MIX:B_COLS] = (v * half).astype(BF)
        slope[slot(i)] = (half + 0.5 * v * (1.0 - bent * bent) * (root * (1.0 + 3 * 0.044715 * square))).astype(BF)

    def second_turn(back, i):
        @pl.when((lax.rem(i, 2) != core) & (section != back))
        def _():
            pl.semaphore_wait(pair_free.at[i // 2], 1)
            for q in range(2):
                to_pair(1 - back, i, q).wait_send()

    def forward_second(i):
        second_turn(0, i)
        for q in range(2):
            span = slice(q * (D // 2), (q + 1) * (D // 2))
            part[part_at(i), :, span] = dot(hcat[slot(i)], wb[:, span]).astype(BF)

            @pl.when(lax.rem(i, 2) != core)
            def _():
                to_pair(0, i, q).start()

    def backward_first(i):
        grad_hidden = dot_nt(grads[slot(i)], wb[...])
        grad_pre = (grad_hidden[:, MIX:B_COLS] * slope[slot(i)].astype(F32)).astype(BF)
        gproj[slot(i), QKV:A_COLS] = grad_pre
        sum_a[0:1, QKV:A_COLS] += jnp.sum(grad_pre.astype(F32), axis=0, keepdims=True)
        grad_mixed = grad_hidden[:, 0:MIX].astype(BF)
        queries = qkv[slot(i), 0:MIX]
        keys = qkv[slot(i), MIX : 2 * MIX]
        values = qkv[slot(i), 2 * MIX : 3 * MIX]
        zero = jnp.zeros((SLOT, MIX), F32)
        grad_queries, grad_keys, grad_values = zero, zero, zero
        for head in range(4):
            mask = head_mask(head)
            chances = probs[i, head]
            masked = grad_mixed * mask
            grad_values = grad_values + dot_tn(chances, masked)
            grad_probs = dot_nt(masked, values)
            wide = chances.astype(F32)
            centre = jnp.sum(wide * grad_probs, axis=-1, keepdims=True)
            grad_scores = (wide * (grad_probs - centre)).astype(BF)
            grad_queries = grad_queries + dot(grad_scores, keys * mask)
            grad_keys = grad_keys + dot_tn(grad_scores, queries * mask)
        table = tables(i)
        pieces = (
            turned(grad_queries * HD**-0.5, table, -1.0).astype(BF),
            turned(grad_keys * HD**-0.5, table, -1.0).astype(BF),
            grad_values.astype(BF),
        )
        for at, piece in enumerate(pieces):
            span = slice(at * MIX, (at + 1) * MIX)
            gproj[slot(i), span] = piece
            sum_a[0:1, span] += jnp.sum(piece.astype(F32), axis=0, keepdims=True)

    def backward_second(i):
        second_turn(1, i)
        for q in range(2):
            span = slice(q * (D // 2), (q + 1) * (D // 2))
            part[part_at(i), :, span] = dot_nt(gproj[slot(i)], wa[span, :]).astype(BF)

            @pl.when(lax.rem(i, 2) != core)
            def _():
                to_pair(1, i, q).start()

    for copy in holds + gives:
        copy.start()
    ours[...] = jnp.zeros_like(ours)
    for m in range(2):
        ours[m : m + 1, :] = jnp.broadcast_to(mine_ref[0:1, m : m + 1], (1, 128))
    tell.start()

    @pl.when(section == 0)
    def _():
        rows_in[0].start()

    @pl.when(section == 1)
    def _():
        rows_in[1].start()

    sum_a[...] = jnp.zeros_like(sum_a)
    tally[0] = jnp.zeros((8, D), F32)
    for at in range(4):
        holds[at].wait()
        takes[at].wait_recv()
    own_first(0)
    own_second(0)

    @pl.when(section == 0)
    def _():
        rows_in[0].wait()
        for m in range(2):
            spread_own(0, m, False)

    @pl.when(section == 1)
    def _():
        rows_in[1].wait()
        for m in range(2):
            spread_own(1, m, False)

    for at in (4, 5):
        holds[at].wait()
        takes[at].wait_recv()
    for at in range(3):
        bias[0:1, at * MIX : (at + 1) * MIX] = jnp.where(
            core == 0, qb_ref[at, 0:1, 0:MIX], qb_ref[at, 0:1, MIX : 2 * MIX]
        )
    bias[0:1, QKV:A_COLS] = jnp.where(core == 0, ub_ref[0:1, 0:UP], ub_ref[0:1, UP : 2 * UP])
    tell.wait_recv()
    for i in range(4):
        at = jnp.where(core == i % 2, ours[i // 2 : i // 2 + 1, :], theirs[i // 2 : i // 2 + 1, :])
        split[i : i + 1, :] = at
        here = places == at
        ctab[i : i + 1, :] = jnp.sum(jnp.where(here, cos_ref[...], 0.0), axis=0, keepdims=True)
        stab[i : i + 1, :] = jnp.sum(jnp.where(here, sin_ref[...], 0.0), axis=0, keepdims=True)

    pass_near(0)
    pass_crossed(0)

    def relay_early(m):
        @pl.when(section == 0)
        def _():
            relay(0, 2 * m + core)

        @pl.when(section == 1)
        def _():
            relay(1, 2 * m + core)

    relay_early(0)
    pass_on(0)
    own_first(1)
    pass_far(0)
    relay_early(1)
    pass_on_crossed(0)
    own_second(1)
    settle(0)
    pass_near(1)

    def forward_early(i):
        @pl.when(section == 0)
        def _():
            await_rows(0, i)
            forward_first(i)

    forward_early(0)
    pass_crossed(1)
    forward_early(1)
    pass_on(1)
    pass_far(1)
    forward_early(2)
    forward_early(3)
    pass_on_crossed(1)
    settle(1)

    def finish_forward_all():
        for m in range(2):
            finish_forward(m)

    @pl.when(section == 0)
    def _():
        def step(i, _):
            forward_second(i)

            @pl.when(i == 1 + core)
            def _():
                pair_sum(0, 0)

            return 0

        lax.fori_loop(0, 4, step, 0)
        pair_sum(0, 1)
        finish_forward_all()

        @pl.when(core == 0)
        def _():
            spread_own(1, 0, True)
            relay(1, 0)

    @pl.when(section == 1)
    def _():
        spread_own(0, 0, True)

        @pl.when(core == 0)
        def _():
            relay(0, 0)

    def turn_of(k):
        return lax.rem(y + 2 + 3 * k + 3 * (k // 2) + 2 * (k // 3), 4)

    a_cuts = ((0, A_HALF), (A_HALF, A_COLS))
    b_cuts = ((0, B_HALF), (B_HALF, B_COLS))

    def term_a(y_at, x_at, half):
        lo, hi = a_cuts[half]
        return dot_tn(normed[:, chip_span(y_at, x_at)], gproj[:, lo:hi])

    def term_b(y_at, x_at, half):
        lo, hi = b_cuts[half]
        return dot_tn(hcat[:, lo:hi], grads[:, chip_span(y_at, x_at)])

    def cross(k):
        span = pl.ds(pl.multiple_of(k * MIX, MIX), MIX)
        there = pl.ds(pl.multiple_of((4 + k) * 256, 256), 256)
        return (
            remote(probs.at[k, 0], wb.at[pl.ds(0, MIX), there], xs.at[k, 0], xr.at[k, 0], me.across),
            remote(slope.at[:, span], wb.at[pl.ds(MIX, UP), there], xs.at[k, 1], xr.at[k, 1], me.across),
        )

    def cross_all():
        pl.semaphore_wait(free_sem, 1)

        def step(k, _):
            span = pl.ds(pl.multiple_of(k * MIX, MIX), MIX)
            total = term_b(turn_of(k), 1 - x, 0).astype(BF)
            probs[k, 0] = total[0:MIX]
            slope[0 : B_HALF - MIX, span] = total[MIX:B_HALF]
            slope[B_HALF - MIX : UP, span] = term_b(turn_of(k), 1 - x, 1).astype(BF)
            for copy in cross(k):
                copy.start()
            return 0

        lax.fori_loop(0, 4, step, 0)

    def crossed(k):
        for copy in cross(k):
            copy.wait_recv()

    def from_across(k, half):
        lo, hi = b_cuts[half]
        return wb[lo:hi, (4 + k) * 256 : (5 + k) * 256].astype(F32)

    def a_place(at):
        return wa.at[pl.ds(pl.multiple_of(at * 256, 256), 256)]

    def b_place(at):
        return wb.at[:, pl.ds(at * 256, 256)]

    a_spans = (pl.ds(0, A_HALF), pl.ds(A_HALF, A_HALF))
    b_spans = (pl.ds(0, B_HALF), pl.ds(B_HALF, B_HALF))

    def far_piece(way, x_at):
        source = far_a.at[x_at, :, a_spans[way]]
        return remote(source, half_a.at[way, x_at], fs.at[way, x_at], fr.at[way, x_at], me.beside(1 - 2 * way))

    def far_piece_b(way):
        source = wb.at[b_spans[way], pl.ds(0, 256)]
        return remote(source, half_b.at[way], fs.at[way, 2], fr.at[way, 2], me.beside(1 - 2 * way))

    def near_piece(way, x_at):
        source = a_place(2 + 2 * way + x_at)
        return remote(source, got_a.at[way, x_at], ns.at[way, x_at], nr.at[way, x_at], me.beside(1 - 2 * way))

    def near_piece_b(way, half):
        lo, hi = b_cuts[half]
        source = wb.at[pl.ds(lo, hi - lo), pl.ds((1 + way) * 256, 256)]
        target = got_b.at[way, pl.ds(lo, hi - lo)]
        return remote(source, target, ns.at[way, 2 + half], nr.at[way, 2 + half], me.beside(1 - 2 * way))

    def cross_last():
        return remote(a_place(6), xa_in, xs.at[4, 0], xr.at[4, 0], me.across)

    def send_far_all():
        def step(k, _):
            x_at = (1 - k) * (1 - x) + k * x
            for way, (lo, hi) in enumerate(a_cuts):
                far_a[x_at, :, lo:hi] = term_a(far, x_at, way).astype(BF)
                far_piece(way, x_at).start()
            return 0

        lax.fori_loop(0, 2, step, 0)

    def send_near(way, x_at):
        target = pl.ds(pl.multiple_of((2 + 2 * way + x_at) * 256, 256), 256)
        for half in (1 - way, way):
            lo, hi = a_cuts[half]
            total = term_a(me.turn(1 - 2 * way), x_at, half)
            if half == way:
                far_piece(way, x_at).wait_recv()
                total = total + half_a[way, x_at].astype(F32)
            wa[target, lo:hi] = total.astype(BF)
        start(near_piece(way, x_at))

    def send_far_b():
        for way, (lo, hi) in enumerate(b_cuts):
            total = term_b(far, x, way)
            if way == 0:
                crossed(0)
            wb[lo:hi, 0:256] = (total + from_across(0, way)).astype(BF)
            start(far_piece_b(way))

    def send_near_b(way):
        span = slice((1 + way) * 256, (2 + way) * 256)
        for half, (lo, hi) in enumerate(b_cuts):
            total = term_b(me.turn(1 - 2 * way), x, half)
            if half == 0:
                crossed(1 + way)
            total = total + from_across(1 + way, half)
            if half == way:
                far_piece_b(way).wait_recv()
                total = total + half_b[way].astype(F32)
            wb[lo:hi, span] = total.astype(BF)
            start(near_piece_b(way, half))

    def arrived_a(x_at, at):
        for half, (lo, hi) in enumerate(a_cuts):
            total = term_a(y, x_at, half)
            for way in (0, 1):
                if half == 0:
                    near_piece(way, x_at).wait_recv()
                total = total + got_a[way, x_at, :, lo:hi].astype(F32)
            wa[at * 256 : (at + 1) * 256, lo:hi] = total.astype(BF)

    def begun_b(at):
        crossed(3)
        for half, (lo, hi) in enumerate(b_cuts):
            wb[lo:hi, at * 256 : (at + 1) * 256] = (term_b(y, x, half) + from_across(3, half)).astype(BF)

    def arrived_b(at, half):
        lo, hi = b_cuts[half]
        span = slice(at * 256, (at + 1) * 256)
        total = wb[lo:hi, span].astype(F32)
        for way in (0, 1):
            near_piece_b(way, half).wait_recv()
            total = total + got_b[way, lo:hi].astype(F32)
        wb[lo:hi, span] = total.astype(BF)

    near_z = {"tensor": z + 1 - 2 * lax.rem(z, 2)}
    near_y = {"dp": me.at(y + 1 - 2 * lax.rem(y, 2), x, core)}
    partners = (near_z, me.z_peer(2), me.sibling, me.across, near_y, me.beside(2))

    def exchange(step):
        return remote(tally.at[step], came.at[step], ts.at[step], tr.at[step], partners[step])

    def fold(step):
        exchange(step).wait_recv()
        total = tally[step] + came[step]
        if step < 3:
            tally[step + 1, 0:3] = total[0:3]
            tally[step + 1, 3:8] = tally[step, 3:8]
            if step == 2:
                tally[step + 1, 4:5] = came[step, 3:4]
        else:
            tally[step + 1] = total
        if step < 5:
            start(exchange(step + 1))

    for copy in sent:
        copy.wait_send()
    sent.clear()

    def forward_step(i):
        away = lax.rem(i, 2) != core

        @pl.when((i == 1) & (core == 1))
        def _():
            spread_own(0, 1, True)

        await_rows(0, i)
        forward_first(i)

        @pl.when((i < 3) & away)
        def _():
            relay(0, i + 1)

    def backward_step(i):
        own = lax.rem(i, 2) == core

        @pl.when((section == 0) & (i < 3) & jnp.logical_not(own))
        def _():
            spread_own(1, (i + 1) // 2, True)

        await_rows(1, i)
        backward_first(i)

        @pl.when((section == 1) & (i == 0) & (core == 0))
        def _():
            spread_own(0, 1, True)

        @pl.when((section == 0) & (i == 3))
        def _():
            pl.semaphore_signal(free_sem, inc=1, device_id=me.across, device_id_type=MESH)
            send_far_all()
            cross_all()

        @pl.when((section == 1) & (i >= 1) & jnp.logical_not(own))
        def _():
            pair_sum(1, (i - 1) // 2)

        @pl.when((section == 1) & (i >= 2) & own)
        def _():
            finish_backward(0)

        @pl.when((section == 0) & own)
        def _():
            pair_sent(0, i // 2)

        backward_second(i)

        @pl.when((section == 0) & (i < 3) & jnp.logical_not(own))
        def _():
            relay(1, i + 1)

    def joint_step(j, _):
        @pl.when((section == 1) & (j < 4))
        def _():
            forward_step(j)

        @pl.when(j != 1)
        def _():
            backward_step(j - (j + 3) // 4)

        return 0

    lax.fori_loop(0, 5, joint_step, 0)

    @pl.when(section == 1)
    def _():
        @pl.when(core == 1)
        def _():
            pair_sum(1, 1)

        finish_backward(1)
        for m in range(2):
            pair_sent(1, m)

        def late_step(i, _):
            forward_second(i)
            return 0

        lax.fori_loop(0, 4, late_step, 0)
        pl.semaphore_signal(free_sem, inc=1, device_id=me.across, device_id_type=MESH)
        send_far_all()
        cross_all()

    for back in range(2):

        @pl.when(section != back)
        def _():
            for m in range(2):
                pair_sum(back, m)

    send_far_b()
    for x_at in (1 - x, x):
        for way in (0, 1):
            send_near(way, x_at)

    @pl.when(section == 0)
    def _():
        for m in range(2):
            finish_backward(m)

    @pl.when(section == 1)
    def _():
        finish_forward_all()

    tally[0, 3:4, 0:A_COLS] = sum_a[0:1]
    start(exchange(0))
    send_near_b(0)
    fold(0)
    fold(1)
    send_near_b(1)
    fold(2)
    arrived_a(1 - x, 6)
    start(cross_last())
    arrived_a(x, 7)
    begun_b(3)
    fold(3)

    def result(half, peer, at):
        rows = pl.ds(pl.multiple_of(7 * 256 + half * 128, 128), 128)
        cols = pl.ds(pl.multiple_of(3 * 256 + half * 128, 128), 128)
        sources = [wa.at[rows, pl.ds(k * MIX, MIX)] for k in range(3)]
        low = B_HALF - MIX
        sources += [wa.at[rows, pl.ds(QKV, UP)], wb.at[pl.ds(0, MIX), cols]]
        sources += [wb.at[pl.ds(MIX, low), cols], wb.at[pl.ds(B_HALF, UP - low), cols]]
        targets = [gq_out.at[k, :, place(at, MIX)] for k in range(3)]
        first, second = pl.multiple_of(at * UP, 128), pl.multiple_of(at * UP + low, 128)
        targets += [gu_out.at[:, place(at, UP)], go_out.at[place(at, MIX), :]]
        targets += [gd_out.at[pl.ds(first, low), :], gd_out.at[pl.ds(second, UP - low), :]]
        if peer:
            return [
                remote(source, target, end_s.at[k], end_r.at[k], me.sibling)
                for k, (source, target) in enumerate(zip(sources, targets))
            ]
        return [
            pltpu.make_async_copy(source, target, end_k.at[k])
            for k, (source, target) in enumerate(zip(sources, targets))
        ]

    outgoing, staying = result(1 - core, True, core), result(core, False, core)
    incoming = result(1 - core, True, 1 - core)
    cross_last().wait_recv()
    wa[7 * 256 : 8 * 256] = (wa[7 * 256 : 8 * 256].astype(F32) + xa_in[...].astype(F32)).astype(BF)
    for at in range(4):
        outgoing[at].start()
        staying[at].start()
    fold(4)
    for half, pieces in enumerate(((4, 5), (6,))):
        arrived_b(3, half)
        for at in pieces:
            outgoing[at].start()
            staying[at].start()
    fold(5)
    sums_ref[...] = tally[6]
    for at in range(3):
        span = slice(at * MIX, (at + 1) * MIX)
        ours_a, others_a = tally[6, 3:4, span], tally[6, 4:5, span]
        gqb_ref[at : at + 1, 0:MIX] = jnp.where(core == 0, ours_a, others_a)
        gqb_ref[at : at + 1, MIX : 2 * MIX] = jnp.where(core == 0, others_a, ours_a)
    ours_a, others_a = tally[6, 3:4, QKV:A_COLS], tally[6, 4:5, QKV:A_COLS]
    gub_ref[0:1, 0:UP] = jnp.where(core == 0, ours_a, others_a)
    gub_ref[0:1, UP : 2 * UP] = jnp.where(core == 0, others_a, ours_a)

    for copy in sent + gives + [tell]:
        copy.wait_send()
    for k in range(4):
        for copy in cross(k):
            copy.wait_send()
    for way in range(2):
        for x_at in range(2):
            far_piece(way, x_at).wait_send()
    for back in range(2):
        for m in range(2):
            mine = 2 * m + core
            for h in range(PARTS):
                for k in range(3):
                    to_z(back, m, mine, k, h).wait_send()
                for k in range(4):
                    to_sibling(back, m, mine, k, h).wait_send()
            keep(back, m).wait()

        @pl.when(section == back)
        def _():
            for m in range(2):
                for h in range(PARTS):
                    onward(back, m, h).wait_send()

        @pl.when(section != back)
        def _():
            for m in range(2):
                pair_sent(back, m)
                for q in range(2):
                    to_pair(back, 2 * m + 1 - core, q).wait_send()

    for at in range(7):
        staying[at].wait()
        outgoing[at].wait_send()
        incoming[at].wait_recv()


def both_layers(rows_in, cotangent, qkv_w, up_w, out_w, down_w, bias_qkv, bias_up, bias_out, bias_down, gain, shift, mine):
    places = np.arange(SLOT, dtype=np.float32)
    frequency = (10000.0 ** (-(np.arange(ROT // 2, dtype=np.float32) * np.float32(2.0 / ROT)))).astype(np.float32)
    angles = (places[:, None] * frequency[None, :]).astype(np.float32).astype(np.float64)
    cosine = np.ones((SLOT, HD), np.float32)
    sine = np.zeros((SLOT, HD), np.float32)
    cosine[:, 0:ROT] = np.tile(np.cos(angles), (1, 2))
    sine[:, 0:ROT] = np.tile(np.sin(angles), (1, 2))
    cosine, sine = (jnp.asarray(np.tile(table, (1, 2))) for table in (cosine, sine))
    any_ = pl.BlockSpec(memory_space=pl.ANY)
    vmem = pl.BlockSpec(memory_space=pltpu.VMEM)
    dma = pltpu.SemaphoreType.DMA
    shape = jax.ShapeDtypeStruct
    return pl.pallas_call(
        layers_kernel,
        out_shape=(
            shape((2, ROWS, D), BF),
            shape((2, ROWS, D), BF),
            shape((3, 128, 2 * MIX), BF),
            shape((128, 2 * UP), BF),
            shape((2 * MIX, 128), BF),
            shape((2 * UP, 128), BF),
            shape((8, D), F32),
            shape((3, 2 * MIX), F32),
            shape((1, 2 * UP), F32),
        ),
        in_specs=[any_] * 6 + [vmem] * 9,
        out_specs=[any_] * 6 + [vmem] * 3,
        scratch_shapes=[
            pltpu.VMEM((D, A_COLS), BF),
            pltpu.VMEM((B_COLS, D), BF),
            pltpu.VMEM((ALL, D), BF),
            pltpu.VMEM((ALL, D), BF),
            pltpu.VMEM((ALL, QKV), BF),
            pltpu.VMEM((ALL, B_COLS), BF),
            pltpu.VMEM((ALL, UP), BF),
            pltpu.VMEM((4, 4, SLOT, SLOT), BF),
            pltpu.VMEM((ALL, A_COLS), BF),
            pltpu.VMEM((4, SLOT, D), BF),
            pltpu.VMEM((2, SLOT, D), BF),
            pltpu.VMEM((4, 3, ROWS, D), BF),
            pltpu.VMEM((2, ROWS, D), BF),
            pltpu.VMEM((2, ROWS, D), BF),
            pltpu.VMEM((8, 128), F32),
            pltpu.VMEM((8, 128), F32),
            pltpu.VMEM((8, 128), jnp.int32),
            pltpu.VMEM((8, 128), jnp.int32),
            pltpu.VMEM((8, 128), jnp.int32),
            pltpu.VMEM((8, A_COLS), F32),
            pltpu.VMEM((2, 256, A_COLS), BF),
            pltpu.VMEM((2, 2, 256, A_HALF), BF),
            pltpu.VMEM((2, B_HALF, 256), BF),
            pltpu.VMEM((2, 2, 256, A_COLS), BF),
            pltpu.VMEM((2, B_COLS, 256), BF),
            pltpu.VMEM((256, A_COLS), BF),
            pltpu.VMEM((8, A_COLS), F32),
            pltpu.VMEM((7, 8, D), F32),
            pltpu.VMEM((6, 8, D), F32),
            dma((7,)),
            dma((2, 10)),
            dma((2, 10)),
            dma((2, 2, 9)),
            dma((2, 2, 9)),
            dma((7,)),
            dma((7,)),
            dma((2, 2, 3 * PARTS)),
            dma((2, 2, 3 * PARTS)),
            dma((2, 2, 4 * PARTS)),
            dma((2, 2, 4 * PARTS)),
            dma((2, 2, 2)),
            dma((2, 2, 2)),
            dma((2, 2, 3 * PARTS)),
            dma((2, 2, 3 * PARTS)),
            dma((2, 2, PARTS)),
            dma((2, 2, PARTS)),
            dma((5, 2)),
            dma((5, 2)),
            dma((2, 3)),
            dma((2, 3)),
            dma((2, 4)),
            dma((2, 4)),
            dma((6,)),
            dma((6,)),
            dma((7,)),
            dma((7,)),
            dma((7,)),
            dma((2, 2)),
            pltpu.SemaphoreType.REGULAR,
            pltpu.SemaphoreType.REGULAR((2,)),
        ],
        compiler_params=pltpu.CompilerParams(
            collective_id=1, has_side_effects=True, vmem_limit_bytes=VMEM_LIMIT
        ),
        name="both_layers",
    )(
        rows_in, cotangent, qkv_w, up_w, out_w, down_w,
        bias_qkv, bias_up, bias_out, bias_down, gain, shift, mine, cosine, sine,
    )


def widen_kernel(lo, ig, gq, gu, go, gd, sums, gqb, gub, *outs):
    lo_out, ig_out, gq_out, gu_out, go_out, gd_out, gain, shift, out_b, down_b, qkv_b, up_b = outs
    lo_out[...] = lo[...]
    ig_out[...] = ig[...]
    gq_out[...] = gq[...].astype(F32)
    gu_out[...] = gu[...].astype(F32)
    go_out[...] = go[...].astype(F32)
    gd_out[...] = gd[...].astype(F32)
    gain[...] = sums[0:1]
    shift[...] = sums[1:2]
    out_b[...] = sums[2:3]
    down_b[...] = sums[2:3]
    for k in range(3):
        qkv_b[k] = gqb[k : k + 1]
    up_b[...] = gub[...]


def widened(lo, ig, gq, gu, go, gd, sums, gqb, gub):
    steps = 2
    shape = jax.ShapeDtypeStruct

    def cut(whole, dim):
        block = tuple(size // steps if at == dim else size for at, size in enumerate(whole))
        return pl.BlockSpec(block, lambda i: tuple(i if at == dim else 0 for at in range(len(whole))))

    def same(whole):
        return pl.BlockSpec(whole, lambda i: (0,) * len(whole))

    large = [cut(lo.shape, 1), cut(ig.shape, 1), cut(gq.shape, 1), cut(gu.shape, 0), cut(go.shape, 0), cut(gd.shape, 0)]
    small = [(1, D)] * 4 + [(3, 1, 2 * MIX), (1, 2 * UP)]
    return pl.pallas_call(
        widen_kernel,
        grid=(steps,),
        out_shape=(
            [shape(lo.shape, BF), shape(ig.shape, BF)]
            + [shape(each.shape, F32) for each in (gq, gu, go, gd)]
            + [shape(each, F32) for each in small]
        ),
        in_specs=large + [same(sums.shape), same(gqb.shape), same(gub.shape)],
        out_specs=large + [same(each) for each in small],
        compiler_params=pltpu.CompilerParams(vmem_limit_bytes=VMEM_LIMIT),
        name="widened",
    )(lo, ig, gq, gu, go, gd, sums, gqb, gub)


def shards(
    inputs,
    cotangent,
    doc_split,
    qkv_weight,
    qkv_bias,
    out_weight,
    out_bias,
    fc1_weight,
    fc1_bias,
    fc2_weight,
    fc2_bias,
    ln_gain,
    ln_bias,
):
    results = both_layers(
        inputs[:, 0],
        cotangent[:, 0],
        qkv_weight[0].transpose(1, 0, 2),
        fc1_weight[0],
        out_weight[0],
        fc2_weight[0],
        qkv_bias[0][:, None, :],
        fc1_bias,
        out_bias,
        fc2_bias,
        ln_gain,
        ln_bias,
        doc_split.reshape(1, 2),
    )
    layer_out, input_grad, grad_qkv, grad_up, grad_out, grad_down, gain, shift, out_b, down_b, qkv_b, up_b = widened(
        *results
    )
    return (
        layer_out[None, :, None],
        input_grad[None, :, None],
        grad_qkv.transpose(1, 0, 2)[None],
        qkv_b.transpose(1, 0, 2),
        grad_out[None],
        out_b,
        grad_up[None],
        up_b,
        grad_down[None],
        down_b,
        gain,
        shift,
    )


def solution(mesh):
    rows = P(None, "dp", "tensor", None)
    placed_weights = (
        P("section", "dp", None, "tensor"),
        P("section", None, "tensor"),
        P("section", "tensor", "dp"),
        P("section", None),
        P("section", "dp", "tensor"),
        P("section", "tensor"),
        P("section", "tensor", "dp"),
        P("section", None),
        P("section", None),
        P("section", None),
    )
    out_rows = P("section", None, "dp", "tensor", None)
    return jax.shard_map(
        shards,
        mesh=mesh,
        in_specs=(rows, rows, P(None, "dp")) + placed_weights,
        out_specs=(out_rows, out_rows) + placed_weights,
        check_vma=False,
    )
```

```python
from functools import partial

import jax
import jax.numpy as jnp
import numpy as np
from jax import lax
from jax.experimental import pallas as pl
from jax.experimental.pallas import tpu as pltpu
from jax.sharding import PartitionSpec as P

HD = 64
ROT = 32
EPSILON = 1e-05
MESH = pl.DeviceIdType.MESH
BF = jnp.bfloat16
F32 = jnp.float32

D = 2048
SLOT = 256
ROWS = 64
PARTS = 4
PART = ROWS // PARTS
QKV = 768
UP = 1024
A_COLS = QKV + UP
MIX = 256
B_COLS = MIX + UP
A_HALF = A_COLS // 2
B_HALF = B_COLS // 2
ALL = 4 * SLOT
VMEM_LIMIT = 62 * 2**20


def dot(a, b):
    return lax.dot_general(a, b, (((1,), (0,)), ((), ())), preferred_element_type=F32)


def dot_nt(a, b):
    return lax.dot_general(a, b, (((1,), (1,)), ((), ())), preferred_element_type=F32)


def dot_tn(a, b):
    return lax.dot_general(a, b, (((0,), (0,)), ((), ())), preferred_element_type=F32)


def remote(src, dst, send, recv, device):
    return pltpu.make_async_remote_copy(
        src_ref=src, dst_ref=dst, send_sem=send, recv_sem=recv, device_id=device, device_id_type=MESH
    )


def greet(peers):
    barrier = pltpu.get_barrier_semaphore()
    for peer in peers:
        pl.semaphore_signal(barrier, inc=1, device_id=peer, device_id_type=MESH)
    pl.semaphore_wait(barrier, len(peers))


class Place:
    def __init__(self):
        self.dp = lax.axis_index("dp")
        self.core = lax.rem(self.dp, 2)
        self.x = lax.rem(self.dp // 2, 2)
        self.y = self.dp // 4
        self.z = lax.axis_index("tensor")
        self.sibling = {"dp": self.dp + 1 - 2 * self.core}
        self.across = {"dp": self.at(self.y, 1 - self.x, self.core)}

    def at(self, y, x, core):
        return (y * 2 + x) * 2 + core

    def turn(self, by):
        return lax.rem(self.y + 4 + by, 4)

    def beside(self, by):
        return {"dp": self.at(self.turn(by), self.x, self.core)}

    def z_peer(self, by):
        return {"tensor": lax.rem(self.z + by, 4)}


STAGES = (
    ((0, 512), (512, 512), (1024, 384), (1408, 384)),
    ((0, 384), (384, 384), (768, 256), (1024, 256)),
)


def layers_kernel(
    x_hbm, cot_hbm, qkv_hbm, up_hbm, ow_hbm, dw_hbm,
    qb_ref, ub_ref, ob_ref, db_ref, gain_ref, shift_ref, mine_ref, cos_ref, sin_ref,
    lo_out, ig_out, gq_out, gu_out, go_out, gd_out, sums_ref, gqb_ref, gub_ref,
    wa, wb, normed, grads, qkv, hcat, slope, probs, gproj, part, got, zgot, xrow, grow, ctab, stab, split, ours, theirs, bias,
    far_a, half_a, half_b, got_a, got_b, xa_in, sum_a, tally, came,
    own_sem, x_send, x_recv, y_send, y_recv, sib_send, sib_recv,
    agz_s, agz_r, ags_s, ags_r, par_s, par_r, rsz_s, rsz_r, sec_s, sec_r,
    xs, xr, fs, fr, ns, nr, ts, tr, end_s, end_r, end_k, keep_s, free_sem, pair_free,
):
    me = Place()
    section = lax.axis_index("section")
    core, z = me.core, me.z
    greet(
        [me.sibling, me.across, me.beside(1), me.beside(-1), me.beside(2)]
        + [me.z_peer(1), me.z_peer(2), me.z_peer(3), {"section": 1 - section}]
    )

    def device_span(dp):
        return pl.ds(pl.multiple_of(dp * 128, 128), 128)

    def chip_span(y_at, x_at):
        return pl.ds(pl.multiple_of((y_at * 2 + x_at) * 256, 256), 256)

    def place(at, size):
        return pl.ds(pl.multiple_of(at * size, size), size)

    def blocks(dp, half):
        span = device_span(dp)
        pairs = [
            (qkv_hbm.at[k, :, place(half, MIX)], wa.at[span, pl.ds(k * MIX, MIX)]) for k in range(3)
        ]
        pairs.append((up_hbm.at[:, place(half, UP)], wa.at[span, pl.ds(QKV, UP)]))
        pairs.append((ow_hbm.at[place(half, MIX), :], wb.at[pl.ds(0, MIX), span]))
        pairs.append((dw_hbm.at[place(half, UP), :], wb.at[pl.ds(MIX, UP), span]))
        return pairs

    other = me.dp + 1 - 2 * core
    holds = [
        pltpu.make_async_copy(source, target, own_sem.at[at])
        for at, (source, target) in enumerate(blocks(me.dp, core))
    ]
    gives = [
        remote(source, target, sib_send.at[at], sib_recv.at[at], me.sibling)
        for at, (source, target) in enumerate(blocks(me.dp, 1 - core))
    ]
    takes = [
        remote(source, target, sib_send.at[at], sib_recv.at[at], me.sibling)
        for at, (source, target) in enumerate(blocks(other, 1 - core))
    ]
    tell = remote(ours, theirs, sib_send.at[6], sib_recv.at[6], me.sibling)
    rows_in = [
        pltpu.make_async_copy(x_hbm, xrow, own_sem.at[6]),
        pltpu.make_async_copy(cot_hbm, grow, own_sem.at[6]),
    ]
    y, x = me.y, me.x
    far = me.turn(2)

    def piece_of(stage, y_at, x_at, which):
        span = pl.ds(*STAGES[stage][which])
        if stage == 0:
            return wa.at[chip_span(y_at, x_at), span]
        return wb.at[span, chip_span(y_at, x_at)]

    def over_x(stage, y_at, x_at, which, slot):
        piece = piece_of(stage, y_at, x_at, which)
        return remote(piece, piece, x_send.at[stage, slot], x_recv.at[stage, slot], me.across)

    def over_y(stage, by, y_at, x_at, which, slot):
        piece = piece_of(stage, y_at, x_at, which)
        way = 0 if by > 0 else 1
        return remote(piece, piece, y_send.at[stage, way, slot], y_recv.at[stage, way, slot], me.beside(by))

    sent = []

    def start(copy):
        copy.start()
        sent.append(copy)

    def own_first(stage):
        for which in (0, 1):
            start(over_x(stage, y, x, which, which))
        for which in (2, 3):
            for by in (1, -1):
                start(over_y(stage, by, y, x, which, which))

    def own_second(stage):
        for which in (2, 3):
            start(over_x(stage, y, x, which, which))
        for which in (0, 1):
            for by in (1, -1):
                start(over_y(stage, by, y, x, which, which))

    def pass_near(stage):
        for which in (2, 3):
            for by in (1, -1):
                source = me.turn(-by)
                over_y(stage, by, source, x, which, which).wait_recv()
                if (which == 2) == (by > 0):
                    start(over_y(stage, by, source, x, which, 6))
                start(over_x(stage, source, x, which, 2 * which + (0 if by > 0 else 1)))

    def pass_crossed(stage):
        for which in (0, 1):
            over_x(stage, y, 1 - x, which, which).wait_recv()
            for by in (1, -1):
                start(over_y(stage, by, y, 1 - x, which, 4 + which))

    def pass_far(stage):
        for which, by in ((2, 1), (3, -1)):
            over_y(stage, by, far, x, which, 6).wait_recv()
            start(over_x(stage, far, x, which, 6 + which))

    def pass_on(stage):
        for which, by in ((0, 1), (1, -1)):
            source = me.turn(-by)
            over_y(stage, by, source, x, which, which).wait_recv()
            start(over_y(stage, by, source, x, which, 7))

    def pass_on_crossed(stage):
        for which, by in ((0, 1), (1, -1)):
            source = me.turn(-by)
            over_y(stage, by, source, 1 - x, which, 4 + which).wait_recv()
            start(over_y(stage, by, source, 1 - x, which, 8))

    def settle(stage):
        for which, by in ((0, -1), (1, 1)):
            source = me.turn(-by)
            over_y(stage, by, source, x, which, which).wait_recv()
            over_y(stage, by, source, 1 - x, which, 4 + which).wait_recv()
        for which in (2, 3):
            over_x(stage, y, 1 - x, which, which).wait_recv()
            for by in (1, -1):
                over_x(stage, me.turn(-by), 1 - x, which, 2 * which + (0 if by > 0 else 1)).wait_recv()
            over_x(stage, far, 1 - x, which, 6 + which).wait_recv()
        for which, by in ((0, 1), (1, -1)):
            over_y(stage, by, far, x, which, 7).wait_recv()
            over_y(stage, by, far, 1 - x, which, 8).wait_recv()

    def band(at, h):
        return pl.ds(pl.multiple_of(at * ROWS + h * PART, PART), PART)

    def slot(i):
        return pl.ds(pl.multiple_of(i * SLOT, SLOT), SLOT)

    def slot_band(i, at, h):
        return pl.ds(pl.multiple_of(i * SLOT + at * ROWS + h * PART, PART), PART)

    parts = [slice(h * PART, (h + 1) * PART) for h in range(PARTS)]

    def standard(rows):
        average = jnp.mean(rows, axis=-1, keepdims=True)
        centred = rows - average
        variance = jnp.mean(centred * centred, axis=-1, keepdims=True)
        scale = lax.rsqrt(variance + EPSILON)
        return centred * scale, scale

    def spread_buffer(back):
        return grads if back else normed

    def to_z(back, m, i, k, h):
        piece = spread_buffer(back).at[slot_band(i, z, h)]
        at = PARTS * k + h
        return remote(piece, piece, agz_s.at[back, m, at], agz_r.at[back, m, at], me.z_peer(1 + k))

    def from_z(back, m, i, k, h):
        piece = spread_buffer(back).at[slot_band(i, lax.rem(z + 3 - k, 4), h)]
        at = PARTS * k + h
        return remote(piece, piece, agz_s.at[back, m, at], agz_r.at[back, m, at], me.z_peer(3 - k))

    def to_sibling(back, m, i, k, h):
        piece = spread_buffer(back).at[slot_band(i, lax.rem(z + 3 - k, 4), h)]
        at = PARTS * k + h
        return remote(piece, piece, ags_s.at[back, m, at], ags_r.at[back, m, at], me.sibling)

    def spread_own(back, m, wait):
        i = 2 * m + core
        for h in range(PARTS):
            if wait:
                onward(1 if back else 0, m, h).wait_recv()
            if back:
                grads[slot_band(i, z, h)] = grow[m, parts[h]]
            else:
                xhat, _ = standard(xrow[m, parts[h]].astype(F32))
                normed[slot_band(i, z, h)] = (xhat * gain_ref[...] + shift_ref[...]).astype(BF)
            for k in range(3):
                to_z(back, m, i, k, h).start()
            to_sibling(back, m, i, 3, h).start()

    def relay(back, i):
        m = i // 2
        for h in range(PARTS):
            for k in range(3):
                from_z(back, m, i, k, h).wait_recv()
                to_sibling(back, m, i, k, h).start()

    def await_rows(back, i):
        m = i // 2

        @pl.when(lax.rem(i, 2) != core)
        def _():
            for h in range(PARTS):
                for k in range(4):
                    to_sibling(back, m, i, k, h).wait_recv()

    def part_at(i):
        return (1 - lax.rem(i + core, 2)) * (i // 2) + lax.rem(i + core, 2) * (2 + i // 2)

    def to_pair(back, i, q):
        m = i // 2
        span = pl.ds(q * (D // 2), D // 2)
        return remote(
            part.at[2 + m, :, span], got.at[m, :, span], par_s.at[back, m, q], par_r.at[back, m, q], me.sibling
        )

    def sum_to_z(back, m, k, h):
        peer = me.z_peer(1 + k)
        at = PARTS * k + h
        return remote(
            part.at[m, band(peer["tensor"], h)],
            zgot.at[back * 2 + m, k, pl.ds(h * PART, PART)],
            rsz_s.at[back, m, at],
            rsz_r.at[back, m, at],
            peer,
        )

    def pair_add(back, m):
        for q in range(2):
            span = slice(q * (D // 2), (q + 1) * (D // 2))
            to_pair(back, 2 * m + core, q).wait_recv()
            part[m, :, span] = (part[m, :, span].astype(F32) + got[m, :, span].astype(F32)).astype(BF)

        @pl.when(section == back)
        def _():
            pl.semaphore_signal(pair_free.at[m], inc=1, device_id=me.sibling, device_id_type=MESH)

    def pair_spread(back, m):
        for h in range(PARTS):
            for k in range(3):
                sum_to_z(back, m, k, h).start()

    def pair_sum(back, m):
        pair_add(back, m)
        pair_spread(back, m)

    def pair_sent(back, m):
        for h in range(PARTS):
            for k in range(3):
                sum_to_z(back, m, k, h).wait_send()

    def row_sum(back, m, h):
        total = part[m, band(z, h)].astype(F32)
        for k in range(3):
            sum_to_z(back, m, k, h).wait_recv()
            total = total + zgot[back * 2 + m, k, parts[h]].astype(F32)
        return total

    def onward(back, m, h):
        target = grow if back else xrow
        span = pl.ds(h * PART, PART)
        return remote(
            zgot.at[back * 2 + m, 0, span],
            target.at[m, span],
            sec_s.at[back, m, h],
            sec_r.at[back, m, h],
            {"section": 1 - back},
        )

    def keep(back, m):
        target = ig_out if back else lo_out
        return pltpu.make_async_copy(zgot.at[back * 2 + m, 0], target.at[m], keep_s.at[back, m])

    def finish_forward(m):
        for h in range(PARTS):
            total = row_sum(0, m, h) + (ob_ref[...] + db_ref[...])
            zgot[m, 0, parts[h]] = (xrow[m, parts[h]].astype(F32) + total).astype(BF)

            @pl.when(section == 0)
            def _():
                onward(0, m, h).start()

        keep(0, m).start()

    def finish_backward(m):
        for h in range(PARTS):
            grad = row_sum(1, m, h)
            xhat, scale = standard(xrow[m, parts[h]].astype(F32))
            above = grow[m, parts[h]].astype(F32)
            a = grad * gain_ref[...]
            inner = a - jnp.mean(a, axis=-1, keepdims=True) - xhat * jnp.mean(a * xhat, axis=-1, keepdims=True)
            zgot[2 + m, 0, parts[h]] = (above + inner * scale).astype(BF)

            @pl.when(section == 1)
            def _():
                onward(1, m, h).start()

            tally[0, 0:1, :] += jnp.sum(grad * xhat, axis=0, keepdims=True)
            tally[0, 1:2, :] += jnp.sum(grad, axis=0, keepdims=True)
            tally[0, 2:3, :] += jnp.sum(above, axis=0, keepdims=True)

        keep(1, m).start()

    lanes = lax.broadcasted_iota(jnp.int32, (SLOT, 128), 1) % HD
    early = lanes < ROT // 2

    places = lax.broadcasted_iota(jnp.int32, (SLOT, 128), 0)

    def tables(i):
        first = places < split[pl.ds(i, 1), :]
        cosine, sine = cos_ref[...], sin_ref[...]
        cos_at, sin_at = ctab[pl.ds(i, 1), :], stab[pl.ds(i, 1), :]
        return (
            jnp.where(first, cosine, cosine * cos_at + sine * sin_at),
            jnp.where(first, sine, sine * cos_at - cosine * sin_at) * jnp.where(early, -1.0, 1.0),
        )

    def turned(values, table, sign):
        halves = []
        for at in (0, 128):
            piece = values[:, at : at + 128]
            swapped = jnp.where(early, pltpu.roll(piece, 128 - ROT // 2, 1), pltpu.roll(piece, ROT // 2, 1))
            halves.append(piece * table[0] + swapped * (table[1] * sign))
        return jnp.concatenate(halves, axis=1)

    def head_mask(head):
        lane = lax.broadcasted_iota(jnp.int32, (1, MIX), 1)
        return jnp.where(lane // HD == head, 1.0, 0.0).astype(BF)

    def forward_first(i):
        rows = normed[slot(i)]
        projected = dot(rows, wa[:, 0:QKV]) + bias[0:1, 0:QKV]
        table = tables(i)
        queries = turned(projected[:, 0:MIX], table, 1.0).astype(BF)
        keys = turned(projected[:, MIX : 2 * MIX], table, 1.0).astype(BF)
        values = projected[:, 2 * MIX : 3 * MIX].astype(BF)
        qkv[slot(i), 0:MIX] = queries
        qkv[slot(i), MIX : 2 * MIX] = keys
        qkv[slot(i), 2 * MIX : 3 * MIX] = values
        v = dot(rows, wa[:, QKV:A_COLS]) + bias[0:1, QKV:A_COLS]
        at = split[pl.ds(i, 1), :]
        at = jnp.concatenate([at, at], axis=1)
        row_at = lax.broadcasted_iota(jnp.int32, (SLOT, SLOT), 0)
        key_at = lax.broadcasted_iota(jnp.int32, (SLOT, SLOT), 1)
        same = jnp.where(row_at < at, 1, 0) == jnp.where(key_at < at, 1, 0)
        allowed = (key_at <= row_at) & same
        mixed = jnp.zeros((SLOT, MIX), F32)
        for head in range(4):
            mask = head_mask(head)
            scores = jnp.where(allowed, dot_nt(queries * mask, keys) * HD**-0.5, -1e30)
            weights = jnp.exp(scores - jnp.max(scores, axis=-1, keepdims=True))
            chances = (weights * (1.0 / jnp.sum(weights, axis=-1, keepdims=True))).astype(BF)
            probs[i, head] = chances
            mixed = mixed + dot(chances, values * mask)
        hcat[slot(i), 0:MIX] = mixed.astype(BF)
        root = np.sqrt(2 / np.pi).astype(np.float32)
        square = v * v
        bent = jnp.tanh(root * (v + 0.044715 * (square * v)))
        half = 0.5 * (1.0 + bent)
        hcat[slot(i), MIX:B_COLS] = (v * half).astype(BF)
        slope[slot(i)] = (half + 0.5 * v * (1.0 - bent * bent) * (root * (1.0 + 3 * 0.044715 * square))).astype(BF)

    def second_turn(back, i):
        @pl.when((lax.rem(i, 2) != core) & (section != back))
        def _():
            pl.semaphore_wait(pair_free.at[i // 2], 1)
            for q in range(2):
                to_pair(1 - back, i, q).wait_send()

    def forward_second(i):
        second_turn(0, i)
        for q in range(2):
            span = slice(q * (D // 2), (q + 1) * (D // 2))
            part[part_at(i), :, span] = dot(hcat[slot(i)], wb[:, span]).astype(BF)

            @pl.when(lax.rem(i, 2) != core)
            def _():
                to_pair(0, i, q).start()

    def backward_first(i):
        grad_hidden = dot_nt(grads[slot(i)], wb[...])
        grad_pre = (grad_hidden[:, MIX:B_COLS] * slope[slot(i)].astype(F32)).astype(BF)
        gproj[slot(i), QKV:A_COLS] = grad_pre
        sum_a[0:1, QKV:A_COLS] += jnp.sum(grad_pre.astype(F32), axis=0, keepdims=True)
        grad_mixed = grad_hidden[:, 0:MIX].astype(BF)
        queries = qkv[slot(i), 0:MIX]
        keys = qkv[slot(i), MIX : 2 * MIX]
        values = qkv[slot(i), 2 * MIX : 3 * MIX]
        zero = jnp.zeros((SLOT, MIX), F32)
        grad_queries, grad_keys, grad_values = zero, zero, zero
        for head in range(4):
            mask = head_mask(head)
            chances = probs[i, head]
            masked = grad_mixed * mask
            grad_values = grad_values + dot_tn(chances, masked)
            grad_probs = dot_nt(masked, values)
            wide = chances.astype(F32)
            centre = jnp.sum(wide * grad_probs, axis=-1, keepdims=True)
            grad_scores = (wide * (grad_probs - centre)).astype(BF)
            grad_queries = grad_queries + dot(grad_scores, keys * mask)
            grad_keys = grad_keys + dot_tn(grad_scores, queries * mask)
        table = tables(i)
        pieces = (
            turned(grad_queries * HD**-0.5, table, -1.0).astype(BF),
            turned(grad_keys * HD**-0.5, table, -1.0).astype(BF),
            grad_values.astype(BF),
        )
        for at, piece in enumerate(pieces):
            span = slice(at * MIX, (at + 1) * MIX)
            gproj[slot(i), span] = piece
            sum_a[0:1, span] += jnp.sum(piece.astype(F32), axis=0, keepdims=True)

    def backward_second(i):
        second_turn(1, i)
        for q in range(2):
            span = slice(q * (D // 2), (q + 1) * (D // 2))
            part[part_at(i), :, span] = dot_nt(gproj[slot(i)], wa[span, :]).astype(BF)

            @pl.when(lax.rem(i, 2) != core)
            def _():
                to_pair(1, i, q).start()

    for copy in holds + gives:
        copy.start()
    ours[...] = jnp.zeros_like(ours)
    for m in range(2):
        ours[m : m + 1, :] = jnp.broadcast_to(mine_ref[0:1, m : m + 1], (1, 128))
    tell.start()

    @pl.when(section == 0)
    def _():
        rows_in[0].start()

    @pl.when(section == 1)
    def _():
        rows_in[1].start()

    sum_a[...] = jnp.zeros_like(sum_a)
    tally[0] = jnp.zeros((8, D), F32)
    for at in range(4):
        holds[at].wait()
        takes[at].wait_recv()
    own_first(0)
    own_second(0)

    @pl.when(section == 0)
    def _():
        rows_in[0].wait()
        for m in range(2):
            spread_own(0, m, False)

    @pl.when(section == 1)
    def _():
        rows_in[1].wait()
        for m in range(2):
            spread_own(1, m, False)

    for at in (4, 5):
        holds[at].wait()
        takes[at].wait_recv()
    for at in range(3):
        bias[0:1, at * MIX : (at + 1) * MIX] = jnp.where(
            core == 0, qb_ref[at, 0:1, 0:MIX], qb_ref[at, 0:1, MIX : 2 * MIX]
        )
    bias[0:1, QKV:A_COLS] = jnp.where(core == 0, ub_ref[0:1, 0:UP], ub_ref[0:1, UP : 2 * UP])
    tell.wait_recv()
    for i in range(4):
        at = jnp.where(core == i % 2, ours[i // 2 : i // 2 + 1, :], theirs[i // 2 : i // 2 + 1, :])
        split[i : i + 1, :] = at
        here = places == at
        ctab[i : i + 1, :] = jnp.sum(jnp.where(here, cos_ref[...], 0.0), axis=0, keepdims=True)
        stab[i : i + 1, :] = jnp.sum(jnp.where(here, sin_ref[...], 0.0), axis=0, keepdims=True)

    pass_near(0)
    pass_crossed(0)

    def relay_early(m):
        @pl.when(section == 0)
        def _():
            relay(0, 2 * m + core)

        @pl.when(section == 1)
        def _():
            relay(1, 2 * m + core)

    relay_early(0)
    pass_on(0)
    own_first(1)
    pass_far(0)
    relay_early(1)
    pass_on_crossed(0)
    own_second(1)
    settle(0)
    pass_near(1)

    def forward_early(i):
        @pl.when(section == 0)
        def _():
            await_rows(0, i)
            forward_first(i)

    forward_early(0)
    pass_crossed(1)
    forward_early(1)
    pass_on(1)
    pass_far(1)
    forward_early(2)
    forward_early(3)
    pass_on_crossed(1)
    settle(1)

    def finish_forward_all():
        for m in range(2):
            finish_forward(m)

    @pl.when(section == 0)
    def _():
        def step(i, _):
            forward_second(i)

            @pl.when(i == 1 + core)
            def _():
                pair_sum(0, 0)

            return 0

        lax.fori_loop(0, 4, step, 0)
        pair_sum(0, 1)
        finish_forward_all()

        @pl.when(core == 0)
        def _():
            spread_own(1, 0, True)
            relay(1, 0)

    @pl.when(section == 1)
    def _():
        spread_own(0, 0, True)

        @pl.when(core == 0)
        def _():
            relay(0, 0)

    def turn_of(k):
        return lax.rem(y + 2 + 3 * k + 3 * (k // 2) + 2 * (k // 3), 4)

    a_cuts = ((0, A_HALF), (A_HALF, A_COLS))
    b_cuts = ((0, B_HALF), (B_HALF, B_COLS))

    def term_a(y_at, x_at, half):
        lo, hi = a_cuts[half]
        return dot_tn(normed[:, chip_span(y_at, x_at)], gproj[:, lo:hi])

    def term_b(y_at, x_at, half):
        lo, hi = b_cuts[half]
        return dot_tn(hcat[:, lo:hi], grads[:, chip_span(y_at, x_at)])

    def cross(k):
        span = pl.ds(pl.multiple_of(k * MIX, MIX), MIX)
        there = pl.ds(pl.multiple_of((4 + k) * 256, 256), 256)
        return (
            remote(probs.at[k, 0], wb.at[pl.ds(0, MIX), there], xs.at[k, 0], xr.at[k, 0], me.across),
            remote(slope.at[:, span], wb.at[pl.ds(MIX, UP), there], xs.at[k, 1], xr.at[k, 1], me.across),
        )

    def cross_all():
        pl.semaphore_wait(free_sem, 1)

        def step(k, _):
            span = pl.ds(pl.multiple_of(k * MIX, MIX), MIX)
            total = term_b(turn_of(k), 1 - x, 0).astype(BF)
            probs[k, 0] = total[0:MIX]
            slope[0 : B_HALF - MIX, span] = total[MIX:B_HALF]
            slope[B_HALF - MIX : UP, span] = term_b(turn_of(k), 1 - x, 1).astype(BF)
            for copy in cross(k):
                copy.start()
            return 0

        lax.fori_loop(0, 4, step, 0)

    def crossed(k):
        for copy in cross(k):
            copy.wait_recv()

    def from_across(k, half):
        lo, hi = b_cuts[half]
        return wb[lo:hi, (4 + k) * 256 : (5 + k) * 256].astype(F32)

    def a_place(at):
        return wa.at[pl.ds(pl.multiple_of(at * 256, 256), 256)]

    def b_place(at):
        return wb.at[:, pl.ds(at * 256, 256)]

    a_spans = (pl.ds(0, A_HALF), pl.ds(A_HALF, A_HALF))
    b_spans = (pl.ds(0, B_HALF), pl.ds(B_HALF, B_HALF))

    def far_piece(way, x_at):
        source = far_a.at[x_at, :, a_spans[way]]
        return remote(source, half_a.at[way, x_at], fs.at[way, x_at], fr.at[way, x_at], me.beside(1 - 2 * way))

    def far_piece_b(way):
        source = wb.at[b_spans[way], pl.ds(0, 256)]
        return remote(source, half_b.at[way], fs.at[way, 2], fr.at[way, 2], me.beside(1 - 2 * way))

    def near_piece(way, x_at):
        source = a_place(2 + 2 * way + x_at)
        return remote(source, got_a.at[way, x_at], ns.at[way, x_at], nr.at[way, x_at], me.beside(1 - 2 * way))

    def near_piece_b(way, half):
        lo, hi = b_cuts[half]
        source = wb.at[pl.ds(lo, hi - lo), pl.ds((1 + way) * 256, 256)]
        target = got_b.at[way, pl.ds(lo, hi - lo)]
        return remote(source, target, ns.at[way, 2 + half], nr.at[way, 2 + half], me.beside(1 - 2 * way))

    def cross_last():
        return remote(a_place(6), xa_in, xs.at[4, 0], xr.at[4, 0], me.across)

    def send_far_all():
        def step(k, _):
            x_at = (1 - k) * (1 - x) + k * x
            for way, (lo, hi) in enumerate(a_cuts):
                far_a[x_at, :, lo:hi] = term_a(far, x_at, way).astype(BF)
                far_piece(way, x_at).start()
            return 0

        lax.fori_loop(0, 2, step, 0)

    def send_near(way, x_at):
        target = pl.ds(pl.multiple_of((2 + 2 * way + x_at) * 256, 256), 256)
        for half in (1 - way, way):
            lo, hi = a_cuts[half]
            total = term_a(me.turn(1 - 2 * way), x_at, half)
            if half == way:
                far_piece(way, x_at).wait_recv()
                total = total + half_a[way, x_at].astype(F32)
            wa[target, lo:hi] = total.astype(BF)
        start(near_piece(way, x_at))

    def send_far_b():
        for way, (lo, hi) in enumerate(b_cuts):
            total = term_b(far, x, way)
            if way == 0:
                crossed(0)
            wb[lo:hi, 0:256] = (total + from_across(0, way)).astype(BF)
            start(far_piece_b(way))

    def send_near_b(way):
        span = slice((1 + way) * 256, (2 + way) * 256)
        for half, (lo, hi) in enumerate(b_cuts):
            total = term_b(me.turn(1 - 2 * way), x, half)
            if half == 0:
                crossed(1 + way)
            total = total + from_across(1 + way, half)
            if half == way:
                far_piece_b(way).wait_recv()
                total = total + half_b[way].astype(F32)
            wb[lo:hi, span] = total.astype(BF)
            start(near_piece_b(way, half))

    def arrived_a(x_at, at):
        for half, (lo, hi) in enumerate(a_cuts):
            total = term_a(y, x_at, half)
            for way in (0, 1):
                if half == 0:
                    near_piece(way, x_at).wait_recv()
                total = total + got_a[way, x_at, :, lo:hi].astype(F32)
            wa[at * 256 : (at + 1) * 256, lo:hi] = total.astype(BF)

    def begun_b(at):
        crossed(3)
        for half, (lo, hi) in enumerate(b_cuts):
            wb[lo:hi, at * 256 : (at + 1) * 256] = (term_b(y, x, half) + from_across(3, half)).astype(BF)

    def arrived_b(at, half):
        lo, hi = b_cuts[half]
        span = slice(at * 256, (at + 1) * 256)
        total = wb[lo:hi, span].astype(F32)
        for way in (0, 1):
            near_piece_b(way, half).wait_recv()
            total = total + got_b[way, lo:hi].astype(F32)
        wb[lo:hi, span] = total.astype(BF)

    near_z = {"tensor": z + 1 - 2 * lax.rem(z, 2)}
    near_y = {"dp": me.at(y + 1 - 2 * lax.rem(y, 2), x, core)}
    partners = (near_z, me.z_peer(2), me.sibling, me.across, near_y, me.beside(2))

    def exchange(step):
        return remote(tally.at[step], came.at[step], ts.at[step], tr.at[step], partners[step])

    def fold(step):
        exchange(step).wait_recv()
        total = tally[step] + came[step]
        if step < 3:
            tally[step + 1, 0:3] = total[0:3]
            tally[step + 1, 3:8] = tally[step, 3:8]
            if step == 2:
                tally[step + 1, 4:5] = came[step, 3:4]
        else:
            tally[step + 1] = total
        if step < 5:
            start(exchange(step + 1))

    for copy in sent:
        copy.wait_send()
    sent.clear()

    def forward_step(i):
        away = lax.rem(i, 2) != core

        @pl.when((i == 1) & (core == 1))
        def _():
            spread_own(0, 1, True)

        await_rows(0, i)
        forward_first(i)

        @pl.when((i < 3) & away)
        def _():
            relay(0, i + 1)

    def backward_step(i):
        own = lax.rem(i, 2) == core

        @pl.when((section == 0) & (i < 3) & jnp.logical_not(own))
        def _():
            spread_own(1, (i + 1) // 2, True)

        await_rows(1, i)
        backward_first(i)

        @pl.when((section == 1) & (i == 0) & (core == 0))
        def _():
            spread_own(0, 1, True)

        @pl.when((section == 0) & (i == 3))
        def _():
            pl.semaphore_signal(free_sem, inc=1, device_id=me.across, device_id_type=MESH)
            send_far_all()
            cross_all()

        @pl.when((section == 1) & (i >= 1) & jnp.logical_not(own))
        def _():
            pair_sum(1, (i - 1) // 2)

        @pl.when((section == 1) & (i >= 2) & own)
        def _():
            finish_backward(0)

        @pl.when((section == 0) & own)
        def _():
            pair_sent(0, i // 2)

        backward_second(i)

        @pl.when((section == 0) & (i < 3) & jnp.logical_not(own))
        def _():
            relay(1, i + 1)

    def joint_step(j, _):
        @pl.when((section == 1) & (j < 4))
        def _():
            forward_step(j)

        @pl.when(j != 1)
        def _():
            backward_step(j - (j + 3) // 4)

        return 0

    lax.fori_loop(0, 5, joint_step, 0)

    @pl.when(section == 1)
    def _():
        @pl.when(core == 1)
        def _():
            pair_sum(1, 1)

        finish_backward(1)
        for m in range(2):
            pair_sent(1, m)

        def late_step(i, _):
            forward_second(i)
            return 0

        lax.fori_loop(0, 4, late_step, 0)
        pl.semaphore_signal(free_sem, inc=1, device_id=me.across, device_id_type=MESH)
        send_far_all()
        cross_all()

    for back in range(2):

        @pl.when(section != back)
        def _():
            for m in range(2):
                pair_sum(back, m)

    send_far_b()
    for x_at in (1 - x, x):
        for way in (0, 1):
            send_near(way, x_at)

    @pl.when(section == 0)
    def _():
        for m in range(2):
            finish_backward(m)

    @pl.when(section == 1)
    def _():
        finish_forward_all()

    tally[0, 3:4, 0:A_COLS] = sum_a[0:1]
    start(exchange(0))
    send_near_b(0)
    fold(0)
    fold(1)
    send_near_b(1)
    fold(2)
    arrived_a(1 - x, 6)
    start(cross_last())
    arrived_a(x, 7)
    begun_b(3)
    fold(3)

    def result(half, peer, at):
        rows = pl.ds(pl.multiple_of(7 * 256 + half * 128, 128), 128)
        cols = pl.ds(pl.multiple_of(3 * 256 + half * 128, 128), 128)
        sources = [wa.at[rows, pl.ds(k * MIX, MIX)] for k in range(3)]
        low = B_HALF - MIX
        sources += [wa.at[rows, pl.ds(QKV, UP)], wb.at[pl.ds(0, MIX), cols]]
        sources += [wb.at[pl.ds(MIX, low), cols], wb.at[pl.ds(B_HALF, UP - low), cols]]
        targets = [gq_out.at[k, :, place(at, MIX)] for k in range(3)]
        first, second = pl.multiple_of(at * UP, 128), pl.multiple_of(at * UP + low, 128)
        targets += [gu_out.at[:, place(at, UP)], go_out.at[place(at, MIX), :]]
        targets += [gd_out.at[pl.ds(first, low), :], gd_out.at[pl.ds(second, UP - low), :]]
        if peer:
            return [
                remote(source, target, end_s.at[k], end_r.at[k], me.sibling)
                for k, (source, target) in enumerate(zip(sources, targets))
            ]
        return [
            pltpu.make_async_copy(source, target, end_k.at[k])
            for k, (source, target) in enumerate(zip(sources, targets))
        ]

    outgoing, staying = result(1 - core, True, core), result(core, False, core)
    incoming = result(1 - core, True, 1 - core)
    cross_last().wait_recv()
    wa[7 * 256 : 8 * 256] = (wa[7 * 256 : 8 * 256].astype(F32) + xa_in[...].astype(F32)).astype(BF)
    for at in range(4):
        outgoing[at].start()
        staying[at].start()
    fold(4)
    for half, pieces in enumerate(((4, 5), (6,))):
        arrived_b(3, half)
        for at in pieces:
            outgoing[at].start()
            staying[at].start()
    fold(5)
    sums_ref[...] = tally[6]
    for at in range(3):
        span = slice(at * MIX, (at + 1) * MIX)
        ours_a, others_a = tally[6, 3:4, span], tally[6, 4:5, span]
        gqb_ref[at : at + 1, 0:MIX] = jnp.where(core == 0, ours_a, others_a)
        gqb_ref[at : at + 1, MIX : 2 * MIX] = jnp.where(core == 0, others_a, ours_a)
    ours_a, others_a = tally[6, 3:4, QKV:A_COLS], tally[6, 4:5, QKV:A_COLS]
    gub_ref[0:1, 0:UP] = jnp.where(core == 0, ours_a, others_a)
    gub_ref[0:1, UP : 2 * UP] = jnp.where(core == 0, others_a, ours_a)

    for copy in sent + gives + [tell]:
        copy.wait_send()
    for k in range(4):
        for copy in cross(k):
            copy.wait_send()
    for way in range(2):
        for x_at in range(2):
            far_piece(way, x_at).wait_send()
    for back in range(2):
        for m in range(2):
            mine = 2 * m + core
            for h in range(PARTS):
                for k in range(3):
                    to_z(back, m, mine, k, h).wait_send()
                for k in range(4):
                    to_sibling(back, m, mine, k, h).wait_send()
            keep(back, m).wait()

        @pl.when(section == back)
        def _():
            for m in range(2):
                for h in range(PARTS):
                    onward(back, m, h).wait_send()

        @pl.when(section != back)
        def _():
            for m in range(2):
                pair_sent(back, m)
                for q in range(2):
                    to_pair(back, 2 * m + 1 - core, q).wait_send()

    for at in range(7):
        staying[at].wait()
        outgoing[at].wait_send()
        incoming[at].wait_recv()


def both_layers(rows_in, cotangent, qkv_w, up_w, out_w, down_w, bias_qkv, bias_up, bias_out, bias_down, gain, shift, mine):
    places = np.arange(SLOT, dtype=np.float32)
    frequency = (10000.0 ** (-(np.arange(ROT // 2, dtype=np.float32) * np.float32(2.0 / ROT)))).astype(np.float32)
    angles = (places[:, None] * frequency[None, :]).astype(np.float32).astype(np.float64)
    cosine = np.ones((SLOT, HD), np.float32)
    sine = np.zeros((SLOT, HD), np.float32)
    cosine[:, 0:ROT] = np.tile(np.cos(angles), (1, 2))
    sine[:, 0:ROT] = np.tile(np.sin(angles), (1, 2))
    cosine, sine = (jnp.asarray(np.tile(table, (1, 2))) for table in (cosine, sine))
    any_ = pl.BlockSpec(memory_space=pl.ANY)
    vmem = pl.BlockSpec(memory_space=pltpu.VMEM)
    dma = pltpu.SemaphoreType.DMA
    shape = jax.ShapeDtypeStruct
    return pl.pallas_call(
        layers_kernel,
        out_shape=(
            shape((2, ROWS, D), BF),
            shape((2, ROWS, D), BF),
            shape((3, 128, 2 * MIX), BF),
            shape((128, 2 * UP), BF),
            shape((2 * MIX, 128), BF),
            shape((2 * UP, 128), BF),
            shape((8, D), F32),
            shape((3, 2 * MIX), F32),
            shape((1, 2 * UP), F32),
        ),
        in_specs=[any_] * 6 + [vmem] * 9,
        out_specs=[any_] * 6 + [vmem] * 3,
        scratch_shapes=[
            pltpu.VMEM((D, A_COLS), BF),
            pltpu.VMEM((B_COLS, D), BF),
            pltpu.VMEM((ALL, D), BF),
            pltpu.VMEM((ALL, D), BF),
            pltpu.VMEM((ALL, QKV), BF),
            pltpu.VMEM((ALL, B_COLS), BF),
            pltpu.VMEM((ALL, UP), BF),
            pltpu.VMEM((4, 4, SLOT, SLOT), BF),
            pltpu.VMEM((ALL, A_COLS), BF),
            pltpu.VMEM((4, SLOT, D), BF),
            pltpu.VMEM((2, SLOT, D), BF),
            pltpu.VMEM((4, 3, ROWS, D), BF),
            pltpu.VMEM((2, ROWS, D), BF),
            pltpu.VMEM((2, ROWS, D), BF),
            pltpu.VMEM((8, 128), F32),
            pltpu.VMEM((8, 128), F32),
            pltpu.VMEM((8, 128), jnp.int32),
            pltpu.VMEM((8, 128), jnp.int32),
            pltpu.VMEM((8, 128), jnp.int32),
            pltpu.VMEM((8, A_COLS), F32),
            pltpu.VMEM((2, 256, A_COLS), BF),
            pltpu.VMEM((2, 2, 256, A_HALF), BF),
            pltpu.VMEM((2, B_HALF, 256), BF),
            pltpu.VMEM((2, 2, 256, A_COLS), BF),
            pltpu.VMEM((2, B_COLS, 256), BF),
            pltpu.VMEM((256, A_COLS), BF),
            pltpu.VMEM((8, A_COLS), F32),
            pltpu.VMEM((7, 8, D), F32),
            pltpu.VMEM((6, 8, D), F32),
            dma((7,)),
            dma((2, 10)),
            dma((2, 10)),
            dma((2, 2, 9)),
            dma((2, 2, 9)),
            dma((7,)),
            dma((7,)),
            dma((2, 2, 3 * PARTS)),
            dma((2, 2, 3 * PARTS)),
            dma((2, 2, 4 * PARTS)),
            dma((2, 2, 4 * PARTS)),
            dma((2, 2, 2)),
            dma((2, 2, 2)),
            dma((2, 2, 3 * PARTS)),
            dma((2, 2, 3 * PARTS)),
            dma((2, 2, PARTS)),
            dma((2, 2, PARTS)),
            dma((5, 2)),
            dma((5, 2)),
            dma((2, 3)),
            dma((2, 3)),
            dma((2, 4)),
            dma((2, 4)),
            dma((6,)),
            dma((6,)),
            dma((7,)),
            dma((7,)),
            dma((7,)),
            dma((2, 2)),
            pltpu.SemaphoreType.REGULAR,
            pltpu.SemaphoreType.REGULAR((2,)),
        ],
        compiler_params=pltpu.CompilerParams(
            collective_id=1, has_side_effects=True, vmem_limit_bytes=VMEM_LIMIT
        ),
        name="both_layers",
    )(
        rows_in, cotangent, qkv_w, up_w, out_w, down_w,
        bias_qkv, bias_up, bias_out, bias_down, gain, shift, mine, cosine, sine,
    )


def widen_kernel(lo, ig, gq, gu, go, gd, sums, gqb, gub, *outs):
    lo_out, ig_out, gq_out, gu_out, go_out, gd_out, gain, shift, out_b, down_b, qkv_b, up_b = outs
    lo_out[...] = lo[...]
    ig_out[...] = ig[...]
    gq_out[...] = gq[...].astype(F32)
    gu_out[...] = gu[...].astype(F32)
    go_out[...] = go[...].astype(F32)
    gd_out[...] = gd[...].astype(F32)
    gain[...] = sums[0:1]
    shift[...] = sums[1:2]
    out_b[...] = sums[2:3]
    down_b[...] = sums[2:3]
    for k in range(3):
        qkv_b[k] = gqb[k : k + 1]
    up_b[...] = gub[...]


def widened(lo, ig, gq, gu, go, gd, sums, gqb, gub):
    steps = 2
    shape = jax.ShapeDtypeStruct

    def cut(whole, dim):
        block = tuple(size // steps if at == dim else size for at, size in enumerate(whole))
        return pl.BlockSpec(block, lambda i: tuple(i if at == dim else 0 for at in range(len(whole))))

    def same(whole):
        return pl.BlockSpec(whole, lambda i: (0,) * len(whole))

    large = [cut(lo.shape, 1), cut(ig.shape, 1), cut(gq.shape, 1), cut(gu.shape, 0), cut(go.shape, 0), cut(gd.shape, 0)]
    small = [(1, D)] * 4 + [(3, 1, 2 * MIX), (1, 2 * UP)]
    return pl.pallas_call(
        widen_kernel,
        grid=(steps,),
        out_shape=(
            [shape(lo.shape, BF), shape(ig.shape, BF)]
            + [shape(each.shape, F32) for each in (gq, gu, go, gd)]
            + [shape(each, F32) for each in small]
        ),
        in_specs=large + [same(sums.shape), same(gqb.shape), same(gub.shape)],
        out_specs=large + [same(each) for each in small],
        compiler_params=pltpu.CompilerParams(vmem_limit_bytes=VMEM_LIMIT),
        name="widened",
    )(lo, ig, gq, gu, go, gd, sums, gqb, gub)


def shards(
    inputs,
    cotangent,
    doc_split,
    qkv_weight,
    qkv_bias,
    out_weight,
    out_bias,
    fc1_weight,
    fc1_bias,
    fc2_weight,
    fc2_bias,
    ln_gain,
    ln_bias,
):
    results = both_layers(
        inputs[:, 0],
        cotangent[:, 0],
        qkv_weight[0].transpose(1, 0, 2),
        fc1_weight[0],
        out_weight[0],
        fc2_weight[0],
        qkv_bias[0][:, None, :],
        fc1_bias,
        out_bias,
        fc2_bias,
        ln_gain,
        ln_bias,
        doc_split.reshape(1, 2),
    )
    layer_out, input_grad, grad_qkv, grad_up, grad_out, grad_down, gain, shift, out_b, down_b, qkv_b, up_b = widened(
        *results
    )
    return (
        layer_out[None, :, None],
        input_grad[None, :, None],
        grad_qkv.transpose(1, 0, 2)[None],
        qkv_b.transpose(1, 0, 2),
        grad_out[None],
        out_b,
        grad_up[None],
        up_b,
        grad_down[None],
        down_b,
        gain,
        shift,
    )


def solution(mesh):
    rows = P(None, "dp", "tensor", None)
    placed_weights = (
        P("section", "dp", None, "tensor"),
        P("section", None, "tensor"),
        P("section", "tensor", "dp"),
        P("section", None),
        P("section", "dp", "tensor"),
        P("section", "tensor"),
        P("section", "tensor", "dp"),
        P("section", None),
        P("section", None),
        P("section", None),
    )
    out_rows = P("section", None, "dp", "tensor", None)
    return jax.shard_map(
        shards,
        mesh=mesh,
        in_specs=(rows, rows, P(None, "dp")) + placed_weights,
        out_specs=(out_rows, out_rows) + placed_weights,
        check_vma=False,
    )
```
